32 devices in a mesh: dp: 4 (over z), wide: 2 (over x), narrow: 4 (over y, core).
Axes of the slice: x: 2, y: 2, z: 4, core: 2. Of those that a mesh axis runs over, the one named last changes fastest.
Arguments:
- tokens: bfloat16 [25216, 512], P(('dp', 'wide', 'narrow')), may hold values from -6 to 6
- grad_out: bfloat16 [25216, 512], P(('dp', 'wide', 'narrow')), may hold values from -6 to 6
- gates: float32 [25216, 2], P(('dp', 'wide', 'narrow')), may hold values from 0.25 to 0.75
- routes: int32 [25216, 2], P(('dp', 'wide', 'narrow')), may hold values from 0 to 31, all different within a row; in each aligned block of 788 rows (0 to 787, 788 to 1575, ...) at most 66 rows name the same one
- ln1_gain: float32 [512], replicated, may hold values from 0.5 to 1.5
- ln1_bias: float32 [512], replicated, may hold values from -1 to 1
- ln2_gain: float32 [512], replicated, may hold values from 0.5 to 1.5
- ln2_bias: float32 [512], replicated, may hold values from -1 to 1
- w_qkv: bfloat16 [3, 512, 512], P(None, 'wide', 'narrow'), may hold values from -0.25 to 0.25
- w_attn_out: bfloat16 [512, 512], P('narrow', 'wide'), may hold values from -1 to 1
- w_expert_in: bfloat16 [32, 512, 2048], P(None, 'wide', 'narrow'), may hold values from -0.25 to 0.25
- w_expert_out: bfloat16 [32, 2048, 512], P(None, 'narrow', 'wide'), may hold values from -0.125 to 0.125
Outputs:
- mixed: bfloat16 [25216, 512], P(('dp', 'wide', 'narrow'))
- grad_input: float32 [25216, 512], P(('dp', 'wide', 'narrow'))
- grad_ln1_gain: float32 [512], replicated
- grad_ln1_bias: float32 [512], replicated
- grad_ln2_gain: float32 [512], replicated
- grad_ln2_bias: float32 [512], replicated
- grad_qkv: float32 [3, 512, 512], P(None, 'wide', 'narrow')
- grad_attn_out: float32 [512, 512], P('narrow', 'wide')
- grad_expert_in: float32 [32, 512, 2048], P(None, 'wide', 'narrow')
- grad_expert_out: float32 [32, 2048, 512], P(None, 'narrow', 'wide')
The draws below stay inside these ranges and needn't reach their ends.
Inputs may be any that keep to these rules, and one draw needn't show every extreme that they name: `routes`: the two ids of a row differ. Within the rows of one device no expert is named more than 66 times, a bound that some block reaches.
All inputs are finite; a program needn't handle non-finite values.
Results may differ from the reference program's by a relative error of at most 0.019.
Values may be sent and summed in bfloat16 or wider, within the bound.
No kernel may reach another device: no remote copies, remote signals or barrier semaphores. Data moves between devices by JAX's collectives and lax.ppermute only.
A program may use at most 256 MiB of HBM per device.

```python
import math
import jax
import jax.numpy as jnp
import numpy as np
from jax import lax

HEADS = 8
HEAD_DIM = 64
FF = 2048
EXPERTS = 32
TOP = 2
SEQ = 197
IMG_DEV = 4
D = 512
TOK_DEV = 788
CAP = 66
TOKENS = 25216


def with_spikes(drawn, key, source, target, shards_of, factor):
    def block_of(position):
        return (jnp.arange(drawn.shape[position]) // (drawn.shape[position] // shards_of)).reshape((-1,) + (1,) * (drawn.ndim - 1 - position))

    one_side = jax.random.permutation(key, shards_of)[block_of(target)]
    other_side = (block_of(target) + shards_of // 2) % shards_of
    return jnp.where((block_of(source) == one_side) | (block_of(source) == other_side), factor * drawn, drawn)


def block_scale(rng, extent, shards, smallest, high):
    def one(dim, blocks):
        draws = jax.random.uniform(jax.random.fold_in(jax.random.fold_in(rng, 6), dim), (blocks,), jnp.float32, smallest / len(shards), high / len(shards))
        return jnp.repeat(jnp.exp(draws), extent[dim] // blocks).reshape((-1,) + (1,) * (len(extent) - dim - 1))

    gain = one(*shards[0])
    for cut in shards[1:]:
        gain = gain * one(*cut)
    return gain


def shared_out(key, own, number, rows, count, top, most, skew):
    order = jax.random.permutation(key, count)
    packed, ordinary = load_shares(count, rows * top, most, skew, True), load_shares(count, rows * top, most, skew, False)
    places = jnp.arange(count)

    def named(tallies, rotation):
        used = int((tallies > 0).sum())
        fixed = max(1, used // 4)
        shifted = fixed + (places - fixed + rotation * (used - fixed)) % max(1, count - fixed)
        return jnp.zeros((count,), jnp.int32).at[order[jnp.where(places < fixed, places, shifted)]].set(jnp.asarray(tallies, jnp.int32))

    tallies = jnp.where(number % 4 == 0, named(packed, number // 4), named(ordinary, number - number // 4 - 1))
    mixed = jax.random.permutation(jax.random.fold_in(own, 3), count)
    donor, sink = mixed[0:count // 2 * 2:2], mixed[1:count // 2 * 2:2]
    room = jnp.minimum(tallies[donor] - 1, most - tallies[sink]) // 2
    room = jnp.where((donor == order[0]) | (sink == order[0]) | (tallies[sink] == 0), 0, jnp.maximum(room, 0))
    shifted = jax.random.randint(jax.random.fold_in(own, 4), (count // 2,), 0, 1 << 20) % (room + 1)
    tallies = tallies.at[donor].add(-shifted).at[sink].add(shifted)
    items = jnp.searchsorted(jnp.cumsum(tallies), jnp.arange(rows * top), side="right").astype(jnp.int32)
    listing = items.reshape(top, rows).T
    listing = listing[jax.random.permutation(jax.random.fold_in(own, 1), rows)]
    rotation = jax.random.randint(jax.random.fold_in(own, 2), (rows, 1), 0, top)
    return jnp.take_along_axis(listing, (jnp.arange(top)[None, :] + rotation) % top, axis=1)


def load_shares(count, total, limit, skew, full):
    loads = [(1 << 20) // math.isqrt(rank ** skew) + 1 for rank in range(1, count + 1)]
    largest = limit if full else min(limit, max(-(-total // count), total * loads[0] // sum(loads)))
    least = 1 if total - largest >= count - 1 else 0
    given, surplus = [largest] + [least] * (count - 1), total - largest - least * (count - 1)
    while surplus > 0:
        movable = [i for i in range(1, count) if given[i] < largest] or [i for i in range(1, count) if given[i] < limit]
        whole, budget = sum([loads[i] for i in movable]), surplus
        for i in movable:
            addition = min(limit - given[i], max(1, budget * loads[i] // whole), surplus)
            given[i] = given[i] + addition
            surplus = surplus - addition
    return np.array(given)


def bell_draw(own_key, dims, deviation, limit, shards=(), kind=jnp.bfloat16):
    array = jax.random.normal(own_key, dims, jnp.float32) * deviation
    if len(shards) > 0:
        array = block_scale(own_key, dims, shards, -0.22, 0.18) * array
    return jnp.clip(array, min=-limit, max=limit).astype(kind)


def gaussian_with(key, dims, scale, limit, split, heavy, kind=jnp.bfloat16):
    values = scale * jax.random.normal(key, dims, jnp.float32)
    if split:
        values = values * block_scale(key, dims, split, -0.22, 0.18)
    return jnp.clip(with_spikes(values, jax.random.fold_in(key, 3), *heavy), -limit, limit).astype(kind)


def setup_inputs(seed: int = 0) -> dict:
    arg_keys = jax.random.split(jax.random.key(seed), 13)
    tokens = bell_draw(arg_keys[0], (TOKENS, D), 1.0, 6.0, ((0, 32),))
    grad_out = gaussian_with(arg_keys[1], (TOKENS, D), 1.0, 6.0, ((0, 32),), (0, 1, 32, 2.75))
    gates = jnp.clip(0.25 + 0.5 * jax.random.uniform(arg_keys[2], (TOKENS, TOP), jnp.float32) ** block_scale(arg_keys[2], (TOKENS, TOP), ((0, 32),), -0.2, 0.2), 0.25, 0.75)
    routes_keys = jax.random.split(jax.random.fold_in(arg_keys[3], 1), TOKENS // TOK_DEV)
    routes_turns = jax.random.permutation(jax.random.fold_in(arg_keys[3], 3), TOKENS // TOK_DEV)
    routes = jax.vmap(lambda own, number: shared_out(jax.random.fold_in(arg_keys[3], 2), own, number, TOK_DEV, EXPERTS, TOP, CAP, 0))(routes_keys, routes_turns).reshape((TOKENS, TOP))
    ln1_gain = jnp.clip(1.0 + 0.1 * jax.random.normal(arg_keys[4], (D,), jnp.float32), 0.5, 1.5)
    ln1_bias = bell_draw(arg_keys[5], (D,), 0.2, 1.0, (), jnp.float32)
    ln2_gain = jnp.clip(1.0 + 0.1 * jax.random.normal(arg_keys[6], (D,), jnp.float32), 0.5, 1.5)
    ln2_bias = bell_draw(arg_keys[7], (D,), 0.2, 1.0, (), jnp.float32)
    w_qkv = bell_draw(arg_keys[8], (3, D, D), D ** -0.5, 0.25, ((1, 2), (2, 4)))
    w_attn_out = bell_draw(arg_keys[9], (D, D), (D // 16) ** -0.5, 1.0, ((0, 4), (1, 2)))
    w_expert_in = bell_draw(arg_keys[10], (EXPERTS, D, FF), D ** -0.5, 0.25, ((1, 2), (2, 4)))
    w_expert_out = bell_draw(arg_keys[11], (EXPERTS, FF, D), FF ** -0.5, 0.125, ((1, 4), (2, 2)))
    return {"tokens": tokens, "grad_out": grad_out, "gates": gates, "routes": routes, "ln1_gain": ln1_gain, "ln1_bias": ln1_bias, "ln2_gain": ln2_gain, "ln2_bias": ln2_bias, "w_qkv": w_qkv, "w_attn_out": w_attn_out, "w_expert_in": w_expert_in, "w_expert_out": w_expert_out}


norm_eps = 1e-06
exact_precision = lax.Precision.HIGHEST

@jax.custom_vjp
def low(v):
    return lax.optimization_barrier(v.astype(jnp.bfloat16)).astype(jnp.float32)

@jax.custom_vjp
def low_back(v):
    return v

def low_keep(v):
    return (low(v), None)

def low_pass(kept, grad):
    return (grad,)

def back_keep(v):
    return (v, None)

def back_low(kept, grad):
    return (low(grad),)
low.defvjp(low_keep, low_pass)
low_back.defvjp(back_keep, back_low)

def normalize(values, norm_gain, norm_shift):
    average = lax.optimization_barrier(jnp.mean(values, axis=-1, keepdims=True))
    centered = values - average
    scaled = centered * lax.rsqrt(lax.optimization_barrier(jnp.mean(centered * centered, axis=-1, keepdims=True)) + norm_eps)
    return scaled * norm_gain + norm_shift

def route_slots(routes):
    flat_ids = routes.reshape(-1).astype(jnp.int32)
    onehot = (flat_ids[:, None] == jnp.arange(EXPERTS, dtype=jnp.int32)[None, :]).astype(jnp.int32)
    order_rank = lax.optimization_barrier(jnp.sum((jnp.cumsum(onehot, axis=0, dtype=jnp.int32) - 1) * onehot, axis=1, dtype=jnp.int32))
    slot_ids = (order_rank * EXPERTS + flat_ids).astype(jnp.int32)
    entry_count = flat_ids.shape[0]
    sources = jnp.full((CAP * EXPERTS,), entry_count, jnp.int32).at[slot_ids].set(jnp.arange(entry_count, dtype=jnp.int32))
    return (slot_ids.reshape(routes.shape), sources)

def block_layer(params, item):
    gain_one, bias_one, gain_two, bias_two, qkv_weight, out_weight, in_weight, down_weight = params
    stream, gate_rows, slot_ids, sources = item
    normed = low(normalize(stream, gain_one, bias_one))
    projected = jnp.einsum('rd,jdc->jrc', normed, qkv_weight, precision=exact_precision)
    projected = low(low_back(projected))
    head_shape = (IMG_DEV, SEQ, HEADS, HEAD_DIM)
    query = projected[0].reshape(head_shape)
    keys = projected[1].reshape(head_shape)
    values = projected[2].reshape(head_shape)
    score_scale = HEAD_DIM ** (-0.5)
    scores = low_back(jnp.einsum('ishd,ithd->ihst', query, keys, precision=exact_precision) * score_scale)
    probs = jax.nn.softmax(scores, axis=-1)
    attended = jnp.einsum('ihst,ithd->ishd', low(probs), values, precision=exact_precision).reshape(TOK_DEV, D)
    attended = low(low_back(attended))
    resid = stream + low_back(jnp.dot(attended, out_weight, precision=exact_precision))
    normed_two = low(normalize(resid, gain_two, bias_two))
    owner_rows = sources // TOP
    padded = jnp.concatenate([normed_two, jnp.zeros((1, D), normed_two.dtype)], axis=0)
    dispatched = padded[owner_rows].reshape(CAP, EXPERTS, D)
    preact = low_back(jnp.einsum('ced,edf->cef', dispatched, in_weight, precision=exact_precision))
    activated = low(jax.nn.gelu(preact))
    expert_out = low_back(jnp.einsum('cef,efd->ced', activated, down_weight, precision=exact_precision))
    expert_flat = expert_out.reshape(CAP * EXPERTS, D)
    return resid + lax.optimization_barrier(jnp.sum(gate_rows[:, :, None] * expert_flat[slot_ids], axis=1))

def reference(tokens, grad_out, gates, routes, ln1_gain, ln1_bias, ln2_gain, ln2_bias, w_qkv, w_attn_out, w_expert_in, w_expert_out):
    block_count = tokens.shape[0] // TOK_DEV
    slot_blocks, source_blocks = lax.map(route_slots, routes.reshape(block_count, TOK_DEV, TOP))
    gate_blocks = gates.astype(jnp.float32).reshape(block_count, TOK_DEV, TOP)
    layer_step = jax.checkpoint(block_layer)

    def forward(stream, gain_one, bias_one, gain_two, bias_two, qkv_weight, out_weight, in_weight, down_weight):
        params = (gain_one, bias_one, gain_two, bias_two, qkv_weight, out_weight, in_weight, down_weight)

        def per_block(item):
            return layer_step(params, item)
        result = lax.map(per_block, (stream.reshape(block_count, TOK_DEV, D), gate_blocks, slot_blocks, source_blocks))
        return result.reshape(block_count * TOK_DEV, D)
    mixed, pull_back = jax.vjp(forward, tokens.astype(jnp.float32), ln1_gain.astype(jnp.float32), ln1_bias.astype(jnp.float32), ln2_gain.astype(jnp.float32), ln2_bias.astype(jnp.float32), w_qkv.astype(jnp.float32), w_attn_out.astype(jnp.float32), w_expert_in.astype(jnp.float32), w_expert_out.astype(jnp.float32))
    grads = pull_back(grad_out.astype(jnp.float32))
    return (mixed.astype(jnp.bfloat16), grads[0], grads[1], grads[2], grads[3], grads[4], grads[5], grads[6], grads[7], grads[8])
```

```python
import functools
import math

import jax
import jax.numpy as jnp
from jax import lax
from jax.experimental import pallas as pl
from jax.experimental.pallas import tpu as pltpu
from jax.sharding import Mesh, PartitionSpec as P

HEAD_DIM = 64
EXPERTS = 32
TOP = 2
SEQ = 197
IMG_STEP = 4
CAP = 66

norm_eps = 1e-06

f32 = jnp.float32
bf16 = jnp.bfloat16


SLOTS = -(-CAP // 8) * 8
IMG_ROWS = -(-SEQ // 16) * 16
LANES = 128
VMEM_LIMIT = 56 * 1024 * 1024


def dot(a, b):
    return lax.dot_general(a, b, (((1,), (0,)), ((), ())), preferred_element_type=f32)


def dot_bt(a, b):
    return lax.dot_general(a, b, (((1,), (1,)), ((), ())), preferred_element_type=f32)


def dot_at(a, b):
    return lax.dot_general(a, b, (((0,), (0,)), ((), ())), preferred_element_type=f32)


def norm_parts(values):
    average = jnp.mean(values, axis=-1, keepdims=True)
    centered = values - average
    scale = lax.rsqrt(jnp.mean(centered * centered, axis=-1, keepdims=True) + norm_eps)
    return centered * scale, scale


def norm_back(hat, scale, gain, grad):
    t = grad * gain
    return scale * (
        t
        - jnp.mean(t, axis=-1, keepdims=True)
        - hat * jnp.mean(t * hat, axis=-1, keepdims=True)
    )


def full_spec(shape):
    zeros = (0,) * len(shape)
    return pl.BlockSpec(shape, lambda *_: zeros)


def image_spec(shape):
    rest = (0,) * (len(shape) - 1)
    return pl.BlockSpec((1,) + shape[1:], lambda i: (i,) + rest)


def route_kernel(rep, tile, routes_ref, routes_t_ref, gates_ref, cot_ref, slot_ref, slot_t_ref, *gd_refs):
    rows = routes_ref.shape[0]
    before = lax.broadcasted_iota(jnp.int32, (rows, rows), 0)
    after = lax.broadcasted_iota(jnp.int32, (rows, rows), 1)
    ids_t = lax.broadcasted_iota(jnp.int32, (EXPERTS, rows), 0)
    ids = lax.broadcasted_iota(jnp.int32, (rows, EXPERTS), 1)
    hot_t = [(ids_t == routes_t_ref[k : k + 1, :]).astype(f32) for k in range(TOP)]
    hot = [(ids == routes_ref[:, k : k + 1]).astype(f32) for k in range(TOP)]
    count_t = dot(sum(hot_t).astype(bf16), (before < after).astype(f32).astype(bf16))
    count = dot((after < before).astype(f32).astype(bf16), sum(hot).astype(bf16))
    slot_t = []
    for k in range(TOP):
        rank_t = jnp.sum(hot_t[k] * count_t, axis=0, keepdims=True).astype(jnp.int32)
        slot_t.append(routes_t_ref[k : k + 1, :] * SLOTS + rank_t)
        slot_t_ref[k : k + 1, :] = slot_t[k]
        rank = jnp.sum(hot[k] * count, axis=1, keepdims=True).astype(jnp.int32)
        slot_ref[:, k : k + 1] = routes_ref[:, k : k + 1] * SLOTS + rank
    cot = cot_ref[...].astype(f32)
    weighed = [(gates_ref[:, k : k + 1] * cot).astype(bf16) for k in range(TOP)]
    part = gd_refs[0].shape[0] // rep
    for g, gd_ref in enumerate(gd_refs):
        for start in range(0, part, tile):
            place = lax.broadcasted_iota(jnp.int32, (tile, rows), 0) + (g * part + start)
            total = sum(
                dot((place == slot_t[k]).astype(f32).astype(bf16), weighed[k]) for k in range(TOP)
            ).astype(bf16)
            for copy in range(rep):
                gd_ref[copy * part + start : copy * part + start + tile, :] = total


def route_and_grad_slots(routes, gates, cot, rep, groups, owners):
    rows, features = cot.shape
    part = owners * SLOTS
    tile = 384 if part % 384 == 0 else part
    shapes = [
        jax.ShapeDtypeStruct((rows, TOP), jnp.int32),
        jax.ShapeDtypeStruct((TOP, rows), jnp.int32),
    ] + [jax.ShapeDtypeStruct((rep * part, features), bf16)] * groups
    return pl.pallas_call(
        functools.partial(route_kernel, rep, tile),
        out_shape=shapes,
        compiler_params=pltpu.CompilerParams(vmem_limit_bytes=VMEM_LIMIT),
        name="route_grad_slots",
    )(routes, routes.T, gates, cot)


def unpack_weights(wide, narrow, weights_ref, qkv_scratch, out_scratch):
    deep, across = qkv_scratch.shape[1] // wide, LANES
    for x in range(wide):
        for n in range(narrow):
            block = x * narrow + n
            for j in range(3):
                qkv_scratch[j, x * deep : (x + 1) * deep, n * across : (n + 1) * across] = weights_ref[
                    block, j * deep : (j + 1) * deep, :
                ]
            for c in range(deep // LANES):
                first = 3 * deep + c * across
                out_scratch[
                    n * across : (n + 1) * across,
                    x * deep + c * LANES : x * deep + (c + 1) * LANES,
                ] = weights_ref[block, first : first + across, :]


def head_masks():
    lane = lax.broadcasted_iota(jnp.int32, (1, LANES), 1)
    per = LANES // HEAD_DIM
    return [(lane // HEAD_DIM) == h for h in range(per)]


def masked(value, mask):
    return jnp.where(mask, value, jnp.zeros_like(value))


def forward_kernel(
    wide,
    narrow,
    rep,
    tile,
    tokens_ref,
    norms_ref,
    weights_ref,
    slot_t_ref,
    proj_ref,
    att_ref,
    resid_ref,
    *rest,
):
    x_refs, (qkv_w, out_w, norm_scratch) = rest[:-3], rest[-3:]
    step = pl.program_id(0)
    features = tokens_ref.shape[2]

    @pl.when(step == 0)
    def _():
        unpack_weights(wide, narrow, weights_ref, qkv_w, out_w)
        norm_scratch[...] = jnp.zeros_like(norm_scratch)

    stream = tokens_ref[0].astype(f32)
    hat, _ = norm_parts(stream)
    normed = (hat * norms_ref[0:1, :] + norms_ref[1:2, :]).astype(bf16)
    proj = [dot(normed, qkv_w[j]).astype(bf16) for j in range(3)]
    for j in range(3):
        proj_ref[0, :, j * features : (j + 1) * features] = proj[j]
    masks = head_masks()
    scale = HEAD_DIM ** (-0.5)
    pieces = []
    for pair in range(features // LANES):
        cols = slice(pair * LANES, (pair + 1) * LANES)
        q, k, v = proj[0][:, cols], proj[1][:, cols], proj[2][:, cols]
        total = None
        for mask in masks:
            scores = dot_bt(masked(q, mask), k) * scale
            weights = jnp.exp(scores - jnp.max(scores, axis=-1, keepdims=True))
            probs = weights / jnp.sum(weights, axis=-1, keepdims=True)
            one = dot(probs.astype(bf16), masked(v, mask))
            total = one if total is None else total + one
        pieces.append(total.astype(bf16))
    attended = jnp.concatenate(pieces, axis=1)
    att_ref[0] = attended
    resid = stream + dot(attended, out_w[...])
    resid_ref[0] = resid
    hat_two, _ = norm_parts(resid)
    norm_scratch[step, : stream.shape[0], :] = (
        hat_two * norms_ref[2:3, :] + norms_ref[3:4, :]
    ).astype(bf16)

    @pl.when(step == pl.num_programs(0) - 1)
    def _():
        count = slot_t_ref.shape[1]
        rows = norm_scratch[...].reshape(count, features)
        part = x_refs[0].shape[0] // rep
        for g, x_ref in enumerate(x_refs):
            for start in range(0, part, tile):
                place = lax.broadcasted_iota(jnp.int32, (tile, count), 0) + (g * part + start)
                here = (place == slot_t_ref[0:1, :]) | (place == slot_t_ref[1:2, :])
                total = dot(here.astype(f32).astype(bf16), rows).astype(bf16)
                for copy in range(rep):
                    x_ref[copy * part + start : copy * part + start + tile, :] = total


def attention_and_slots(tokens, norms, weights, slot_t, wide, narrow, rep, groups, owners):
    images, rows, features = tokens.shape
    part = owners * SLOTS
    tile = 384 if part % 384 == 0 else part
    slot_shape = (rep * part, features)
    per_image = [(images, rows, 3 * features), (images, rows, features), (images, rows, features)]
    return pl.pallas_call(
        functools.partial(forward_kernel, wide, narrow, rep, tile),
        grid=(images,),
        in_specs=[
            image_spec(tokens.shape),
            full_spec(norms.shape),
            full_spec(weights.shape),
            full_spec(slot_t.shape),
        ],
        out_specs=[image_spec(s) for s in per_image] + [full_spec(slot_shape)] * groups,
        out_shape=[
            jax.ShapeDtypeStruct(per_image[0], bf16),
            jax.ShapeDtypeStruct(per_image[1], bf16),
            jax.ShapeDtypeStruct(per_image[2], f32),
        ]
        + [jax.ShapeDtypeStruct(slot_shape, bf16)] * groups,
        scratch_shapes=[
            pltpu.VMEM((3, features, features), bf16),
            pltpu.VMEM((features, features), bf16),
            pltpu.VMEM((images, IMG_ROWS, features), bf16),
        ],
        compiler_params=pltpu.CompilerParams(vmem_limit_bytes=VMEM_LIMIT),
        name="attention_forward",
    )(tokens, norms, weights, slot_t)


GELU_A = math.sqrt(2.0 / math.pi)
GELU_B = 0.044715 * GELU_A


def gelu_pair(u):
    u2 = u * u
    p = GELU_B * u2 + GELU_A
    half = 0.5 * jnp.tanh(u * p) + 0.5
    slope = half + (u * (6.0 * p - 4.0 * GELU_A)) * (half - half * half)
    return u * half, slope


def identity(size):
    a = lax.broadcasted_iota(jnp.int32, (size, size), 0)
    b = lax.broadcasted_iota(jnp.int32, (size, size), 1)
    return (a == b).astype(f32).astype(bf16)


def expert_kernel(
    tile,
    own_rows,
    rep_ref,
    x_ref,
    gd_ref,
    wi_ref,
    wo_ref,
    gin_ref,
    gout_ref,
    y_ref,
    gx_ref,
    x_t,
    gd_t,
    act,
    gp,
    wo_s,
    y_acc,
    gx_acc,
):
    step = pl.program_id(0)
    rows, features = x_ref.shape
    wide, deep, hidden = wi_ref.shape[0], wi_ref.shape[2], wi_ref.shape[3]

    @pl.when(step == 0)
    def _():
        eye = identity(features)

        def turn(t, carry):
            at = pl.ds(pl.multiple_of(t * tile, tile), tile)
            x_t[:, at] = dot_bt(eye, x_ref[at, :]).astype(bf16)
            gd_t[:, at] = dot_bt(eye, gd_ref[at, :]).astype(bf16)
            return carry

        lax.fori_loop(0, rows // tile, turn, 0)
        y_acc[...] = jnp.zeros_like(y_acc)
        gx_acc[...] = jnp.zeros_like(gx_acc)

    for x in range(wide):
        wo_s[:, x * deep : (x + 1) * deep] = wo_ref[x, 0]
    wi = wi_ref[:, 0].reshape(wide * deep, hidden)

    def hidden_rows(t, carry):
        at = pl.ds(pl.multiple_of(t * tile, tile), tile)
        value, slope = gelu_pair(dot(x_ref[at, :], wi))
        act[at, :] = value.astype(bf16)
        gp[at, :] = (dot_bt(gd_ref[at, :], wo_s[...]) * slope).astype(bf16)
        return carry

    lax.fori_loop(0, rows // tile, hidden_rows, 0)

    gin = dot(x_t[...], gp[...]).astype(bf16)
    for x in range(wide):
        gin_ref[x, 0] = gin[x * deep : (x + 1) * deep, :]
    gout = dot_bt(identity(hidden), dot(gd_t[...], act[...]).astype(bf16)).astype(bf16)
    for x in range(wide):
        gout_ref[x, 0] = gout[:, x * deep : (x + 1) * deep]

    first = rep_ref[0] * own_rows

    def own(t, carry):
        at = pl.ds(pl.multiple_of(t * tile, tile), tile)
        here = pl.ds(pl.multiple_of(first + t * tile, tile), tile)
        y_acc[at, :] += dot(act[here, :], wo_s[...])
        gx_acc[at, :] += dot_bt(gp[here, :], wi)
        return carry

    lax.fori_loop(0, own_rows // tile, own, 0)

    @pl.when(step == pl.num_programs(0) - 1)
    def _():
        y_ref[...] = y_acc[...].astype(bf16)
        gx_ref[...] = gx_acc[...].astype(bf16)


def expert(rep_index, x, gd, w_in, w_out, own_rows, wide, narrow):
    rows, features = x.shape
    deep, hidden = w_in.shape[1], w_in.shape[2]
    w_in = w_in.reshape(wide, narrow, deep, hidden)
    w_out = w_out.reshape(wide, narrow, hidden, deep)
    tile = 384 if own_rows % 384 == 0 else math.gcd(own_rows, 128)
    in_spec = pl.BlockSpec((wide, 1, deep, hidden), lambda n, r: (0, n, 0, 0))
    out_spec = pl.BlockSpec((wide, 1, hidden, deep), lambda n, r: (0, n, 0, 0))
    whole = lambda shape: pl.BlockSpec(shape, lambda n, r: (0, 0))
    gin, gout, y, gx = pl.pallas_call(
        functools.partial(expert_kernel, tile, own_rows),
        grid_spec=pltpu.PrefetchScalarGridSpec(
            num_scalar_prefetch=1,
            grid=(narrow,),
            in_specs=[whole(x.shape), whole(gd.shape), in_spec, out_spec],
            out_specs=[in_spec, out_spec, whole((own_rows, features)), whole((own_rows, features))],
            scratch_shapes=[
                pltpu.VMEM((features, rows), bf16),
                pltpu.VMEM((features, rows), bf16),
                pltpu.VMEM((rows, hidden), bf16),
                pltpu.VMEM((rows, hidden), bf16),
                pltpu.VMEM((hidden, features), bf16),
                pltpu.VMEM((own_rows, features), f32),
                pltpu.VMEM((own_rows, features), f32),
            ],
        ),
        out_shape=[
            jax.ShapeDtypeStruct(w_in.shape, bf16),
            jax.ShapeDtypeStruct(w_out.shape, bf16),
            jax.ShapeDtypeStruct((own_rows, features), bf16),
            jax.ShapeDtypeStruct((own_rows, features), bf16),
        ],
        compiler_params=pltpu.CompilerParams(vmem_limit_bytes=VMEM_LIMIT),
        cost_estimate=pl.CostEstimate(
            flops=2 * narrow * features * hidden * (4 * rows + 2 * own_rows),
            bytes_accessed=20_000_000,
            transcendentals=rows * hidden * narrow,
        ),
        name="expert",
    )(rep_index, x, gd, w_in, w_out)
    return gin.reshape(-1, deep, hidden), gout.reshape(-1, hidden, deep), y, gx


def mixed_kernel(resid_ref, slot_ref, gates_ref, *rest):
    y_refs, mixed_ref = rest[:-1], rest[-1]
    total = resid_ref[0]
    rows = total.shape[0]
    part = y_refs[0].shape[0]
    for k in range(TOP):
        picked = None
        for g, y_ref in enumerate(y_refs):
            place = lax.broadcasted_iota(jnp.int32, (rows, part), 1) + g * part
            one = dot((place == slot_ref[0, :, k : k + 1]).astype(f32).astype(bf16), y_ref[...])
            picked = one if picked is None else picked + one
        total = total + gates_ref[0, :, k : k + 1] * picked
    mixed_ref[0] = total.astype(bf16)


def mix(resid, slots, gates, ys):
    return pl.pallas_call(
        mixed_kernel,
        grid=(resid.shape[0],),
        in_specs=[image_spec(resid.shape), image_spec(slots.shape), image_spec(gates.shape)]
        + [full_spec(y.shape) for y in ys],
        out_specs=image_spec(resid.shape),
        out_shape=jax.ShapeDtypeStruct(resid.shape, bf16),
        compiler_params=pltpu.CompilerParams(vmem_limit_bytes=VMEM_LIMIT),
        name="mix",
    )(resid, slots, gates, *ys)


def backward_kernel(wide, narrow, groups, *refs):
    (tokens_ref, cot_ref, norms_ref, weights_ref, slot_ref, proj_ref, att_ref, resid_ref) = refs[:8]
    gx_refs = refs[8 : 8 + groups]
    (grad_ref, grads_w_ref, grads_n_ref) = refs[8 + groups : 11 + groups]
    (qkv_w, out_w, normed_s, att_s, branch_s, proj_s) = refs[11 + groups :]
    step = pl.program_id(0)
    rows, features = tokens_ref.shape[1], tokens_ref.shape[2]

    @pl.when(step == 0)
    def _():
        unpack_weights(wide, narrow, weights_ref, qkv_w, out_w)
        normed_s[...] = jnp.zeros_like(normed_s)
        att_s[...] = jnp.zeros_like(att_s)
        branch_s[...] = jnp.zeros_like(branch_s)
        proj_s[...] = jnp.zeros_like(proj_s)
        grads_n_ref[...] = jnp.zeros_like(grads_n_ref)

    part = gx_refs[0].shape[0]
    grad_normed = None
    for g, gx_ref in enumerate(gx_refs):
        place = lax.broadcasted_iota(jnp.int32, (rows, part), 1) + g * part
        here = (place == slot_ref[0, :, 0:1]) | (place == slot_ref[0, :, 1:2])
        one = dot(here.astype(f32).astype(bf16), gx_ref[...])
        grad_normed = one if grad_normed is None else grad_normed + one
    hat_two, scale_two = norm_parts(resid_ref[0])
    grads_n_ref[2:3, :] += jnp.sum(grad_normed * hat_two, axis=0, keepdims=True)
    grads_n_ref[3:4, :] += jnp.sum(grad_normed, axis=0, keepdims=True)
    grad_resid = cot_ref[0].astype(f32) + norm_back(
        hat_two, scale_two, norms_ref[2:3, :], grad_normed
    )
    branch = grad_resid.astype(bf16)
    branch_s[step, :rows, :] = branch
    att_s[step, :rows, :] = att_ref[0]
    grad_att = dot_bt(branch, out_w[...]).astype(bf16)

    masks = head_masks()
    scale = HEAD_DIM ** (-0.5)
    pairs = features // LANES
    pieces = [[None] * pairs for _ in range(3)]
    for pair in range(pairs):
        at = [j * features + pair * LANES for j in range(3)]
        q, k, v = [proj_ref[0, :, a : a + LANES] for a in at]
        ga = grad_att[:, pair * LANES : (pair + 1) * LANES]
        sums = [None] * 3
        for mask in masks:
            scores = dot_bt(masked(k, mask), q) * scale
            weights = jnp.exp(scores - jnp.max(scores, axis=0, keepdims=True))
            probs = weights / jnp.sum(weights, axis=0, keepdims=True)
            ga_h = masked(ga, mask)
            dprobs = dot_bt(v, ga_h)
            inner = jnp.sum(probs * dprobs, axis=0, keepdims=True)
            grad_scores = (probs * (dprobs - inner)).astype(bf16)
            parts = (
                dot_at(grad_scores, masked(k, mask)),
                dot(grad_scores, masked(q, mask)),
                dot(probs.astype(bf16), ga_h),
            )
            for j in range(3):
                sums[j] = parts[j] if sums[j] is None else sums[j] + parts[j]
        pieces[0][pair] = (sums[0] * scale).astype(bf16)
        pieces[1][pair] = (sums[1] * scale).astype(bf16)
        pieces[2][pair] = sums[2].astype(bf16)

    stream = tokens_ref[0].astype(f32)
    hat, scale_one = norm_parts(stream)
    normed_s[step, :rows, :] = (hat * norms_ref[0:1, :] + norms_ref[1:2, :]).astype(bf16)
    grad_first = None
    for j in range(3):
        grad_proj = jnp.concatenate(pieces[j], axis=1)
        proj_s[j, step, :rows, :] = grad_proj
        one = dot_bt(grad_proj, qkv_w[j])
        grad_first = one if grad_first is None else grad_first + one
    grads_n_ref[0:1, :] += jnp.sum(grad_first * hat, axis=0, keepdims=True)
    grads_n_ref[1:2, :] += jnp.sum(grad_first, axis=0, keepdims=True)
    grad_ref[0] = grad_resid + norm_back(hat, scale_one, norms_ref[0:1, :], grad_first)

    @pl.when(step == pl.num_programs(0) - 1)
    def _():
        count = normed_s.shape[0] * normed_s.shape[1]
        deep = features // wide
        flat = lambda value: value.reshape(count, features)
        normed_t = flat(normed_s[...])
        for j in range(3):
            grad = dot_at(normed_t, flat(proj_s[j])).astype(bf16)
            for x in range(wide):
                for n in range(narrow):
                    grads_w_ref[x * narrow + n, j * deep : (j + 1) * deep, :] = grad[
                        x * deep : (x + 1) * deep, n * LANES : (n + 1) * LANES
                    ]
        grad = dot_at(flat(att_s[...]), flat(branch_s[...])).astype(bf16)
        for x in range(wide):
            for n in range(narrow):
                for c in range(deep // LANES):
                    first = 3 * deep + c * LANES
                    grads_w_ref[x * narrow + n, first : first + LANES, :] = grad[
                        n * LANES : (n + 1) * LANES,
                        x * deep + c * LANES : x * deep + (c + 1) * LANES,
                    ]


def attention_back(tokens, cot, norms, weights, slots, proj, att, resid, gxs, wide, narrow):
    images, rows, features = tokens.shape
    stash = (images, IMG_ROWS, features)
    return pl.pallas_call(
        functools.partial(backward_kernel, wide, narrow, len(gxs)),
        grid=(images,),
        in_specs=[
            image_spec(tokens.shape),
            image_spec(cot.shape),
            full_spec(norms.shape),
            full_spec(weights.shape),
            image_spec(slots.shape),
            image_spec(proj.shape),
            image_spec(att.shape),
            image_spec(resid.shape),
        ]
        + [full_spec(gx.shape) for gx in gxs],
        out_specs=[image_spec(tokens.shape), full_spec(weights.shape), full_spec((4, features))],
        out_shape=[
            jax.ShapeDtypeStruct(tokens.shape, f32),
            jax.ShapeDtypeStruct(weights.shape, bf16),
            jax.ShapeDtypeStruct((4, features), f32),
        ],
        scratch_shapes=[
            pltpu.VMEM((3, features, features), bf16),
            pltpu.VMEM((features, features), bf16),
            pltpu.VMEM(stash, bf16),
            pltpu.VMEM(stash, bf16),
            pltpu.VMEM(stash, bf16),
            pltpu.VMEM((3,) + stash, bf16),
        ],
        compiler_params=pltpu.CompilerParams(vmem_limit_bytes=VMEM_LIMIT),
        name="attention_backward",
    )(tokens, cot, norms, weights, slots, proj, att, resid, *gxs)


def owned_on_device(
    sizes,
    tokens,
    grad_out,
    gates,
    routes,
    ln1_gain,
    ln1_bias,
    ln2_gain,
    ln2_bias,
    w_qkv,
    w_attn_out,
    w_expert_in,
    w_expert_out,
):
    rep, own_planes, wide, narrow = sizes
    plane = wide * narrow
    owners = own_planes * plane
    groups = EXPERTS // owners
    everyone = ("rep", "own", "wide", "narrow")
    rows, features = tokens.shape
    images = rows // SEQ
    deep = w_qkv.shape[1]
    rep_index = lax.axis_index("rep").astype(jnp.int32).reshape(1)
    own_index = lax.axis_index("own")

    def in_plane(values):
        return lax.all_to_all(values, ("wide", "narrow"), 0, 0, tiled=True)

    small = jnp.concatenate(
        [w_qkv.reshape(3 * deep, LANES)]
        + [w_attn_out[:, c * LANES : (c + 1) * LANES] for c in range(deep // LANES)],
        axis=0,
    )
    weights = in_plane(jnp.broadcast_to(small[None], (plane,) + small.shape))

    slots, slot_t, *gds = route_and_grad_slots(routes, gates, grad_out, rep, groups, owners)

    def to_owners(values):
        return lax.all_to_all(
            values.reshape(-1, SLOTS, features), everyone, 0, 0, tiled=True
        ).reshape(-1, features)

    def to_tokens(values):
        return lax.all_to_all(
            values.reshape(-1, SLOTS, features), ("own", "wide", "narrow"), 0, 0, tiled=True
        ).reshape(-1, features)

    def owned(values, g):
        return in_plane(
            lax.dynamic_slice_in_dim(values, g * owners + own_index * plane, plane, axis=0)
        )

    w_in = [owned(w_expert_in, g) for g in range(groups)]
    w_out = [owned(w_expert_out, g) for g in range(groups)]

    norms = jnp.stack([ln1_gain, ln1_bias, ln2_gain, ln2_bias])
    per_image = lambda values: values.reshape((images, SEQ) + values.shape[1:])
    slot_wide = jnp.pad(
        slot_t.reshape(TOP, images, SEQ), ((0, 0), (0, 0), (0, IMG_ROWS - SEQ)), constant_values=-1
    ).reshape(TOP, images * IMG_ROWS)
    tokens3, cot3, slots3, gates3 = map(per_image, (tokens, grad_out, slots, gates))
    proj, att, resid, *xs = attention_and_slots(
        tokens3, norms, weights, slot_wide, wide, narrow, rep, groups, owners
    )

    gd_all = [to_owners(v) for v in gds]
    x_all = [to_owners(v) for v in xs]
    grads_in, grads_out, ys, gxs = zip(
        *[
            expert(rep_index, x_all[g], gd_all[g], w_in[g], w_out[g], owners * SLOTS, wide, narrow)
            for g in range(groups)
        ]
    )
    gx_back = [to_tokens(v) for v in gxs]
    y_back = [to_tokens(v) for v in ys]

    def to_blocks(parts):
        pieces = [lax.all_gather(in_plane(v), "own", axis=0, tiled=True) for v in parts]
        return jnp.concatenate(pieces, axis=0).astype(f32)

    out_in, out_out = to_blocks(grads_in), to_blocks(grads_out)

    mixed = mix(resid, slots3, gates3, y_back).reshape(rows, features)
    grad_input, grads_w, grads_n = attention_back(
        tokens3, cot3, norms, weights, slots3, proj, att, resid, gx_back, wide, narrow
    )
    grads_n = lax.psum(grads_n, everyone)
    block = jnp.sum(in_plane(grads_w).astype(f32), axis=0).astype(bf16)
    block = lax.psum(block, ("rep", "own")).astype(f32)
    grad_qkv = block[: 3 * deep].reshape(3, deep, LANES)
    grad_attn_out = jnp.concatenate(
        [
            block[3 * deep + c * LANES : 3 * deep + (c + 1) * LANES]
            for c in range(deep // LANES)
        ],
        axis=1,
    )
    return (
        mixed,
        grad_input.reshape(rows, features),
        grads_n[0],
        grads_n[1],
        grads_n[2],
        grads_n[3],
        grad_qkv,
        grad_attn_out,
        out_in,
        out_out,
    )


def normalize(values, norm_gain, norm_shift):
    average = jnp.mean(values, axis=-1, keepdims=True)
    centered = values - average
    scaled = centered * lax.rsqrt(jnp.mean(centered * centered, axis=-1, keepdims=True) + norm_eps)
    return scaled * norm_gain + norm_shift


def route_slots(routes):
    flat_ids = routes.reshape(-1)
    onehot = (flat_ids[:, None] == jnp.arange(EXPERTS, dtype=jnp.int32)[None, :]).astype(jnp.int32)
    order_rank = jnp.sum(
        (jnp.cumsum(onehot, axis=0, dtype=jnp.int32) - 1) * onehot, axis=1, dtype=jnp.int32
    )
    slot_ids = order_rank * EXPERTS + flat_ids
    entry_count = flat_ids.shape[0]
    sources = (
        jnp.full((CAP * EXPERTS,), entry_count, jnp.int32)
        .at[slot_ids]
        .set(jnp.arange(entry_count, dtype=jnp.int32))
    )
    return (slot_ids.reshape(routes.shape), sources)


def narrow_rows(values):
    return lax.all_gather(values, "narrow", axis=0, tiled=True)


def narrow_sums(values):
    return lax.psum_scatter(
        values.astype(jnp.bfloat16), "narrow", scatter_dimension=0, tiled=True
    ).astype(jnp.float32)


def attention_forward(query, keys, values, head_count):
    row_count = query.shape[0]
    group_count = row_count // (IMG_STEP * SEQ)
    block_shape = (group_count, IMG_STEP, SEQ, head_count, HEAD_DIM)
    score_scale = HEAD_DIM ** (-0.5)

    def one_group(block):
        query_blk, key_blk, value_blk = block
        scores = (
            jnp.einsum("ishd,ithd->ihst", query_blk, key_blk, preferred_element_type=jnp.float32)
            * score_scale
        )
        row_top = jnp.max(scores, axis=-1, keepdims=True)
        weights = jnp.exp(scores - row_top)
        row_total = jnp.sum(weights, axis=-1, keepdims=True)
        probs = weights / row_total
        output = jnp.einsum(
            "ihst,ithd->ishd",
            probs.astype(jnp.bfloat16),
            value_blk,
            preferred_element_type=jnp.float32,
        )
        return (output.astype(jnp.bfloat16), (row_top + jnp.log(row_total))[..., 0])

    output, log_total = lax.map(
        one_group,
        (query.reshape(block_shape), keys.reshape(block_shape), values.reshape(block_shape)),
    )
    return (output.reshape(row_count, head_count * HEAD_DIM), log_total)


def attention_backward(query, keys, values, grad_att, log_total, head_count):
    row_count = query.shape[0]
    group_count = row_count // (IMG_STEP * SEQ)
    block_shape = (group_count, IMG_STEP, SEQ, head_count, HEAD_DIM)
    score_scale = HEAD_DIM ** (-0.5)

    def one_group(block):
        query_blk, key_blk, value_blk, grad_blk, total_blk = block
        scores = (
            jnp.einsum("ishd,ithd->ihst", query_blk, key_blk, preferred_element_type=jnp.float32)
            * score_scale
        )
        probs = jnp.exp(scores - total_blk[..., None])
        dprobs = jnp.einsum(
            "ishd,ithd->ihst", grad_blk, value_blk, preferred_element_type=jnp.float32
        )
        inner = jnp.sum(probs * dprobs, axis=-1, keepdims=True)
        grad_scores = (probs * (dprobs - inner)).astype(jnp.bfloat16)
        grad_query = (
            jnp.einsum("ihst,ithd->ishd", grad_scores, key_blk, preferred_element_type=jnp.float32)
            * score_scale
        )
        grad_key = (
            jnp.einsum(
                "ihst,ishd->ithd", grad_scores, query_blk, preferred_element_type=jnp.float32
            )
            * score_scale
        )
        grad_value = jnp.einsum(
            "ihst,ishd->ithd",
            probs.astype(jnp.bfloat16),
            grad_blk,
            preferred_element_type=jnp.float32,
        )
        return (
            grad_query.astype(jnp.bfloat16),
            grad_key.astype(jnp.bfloat16),
            grad_value.astype(jnp.bfloat16),
        )

    pieces = lax.map(
        one_group,
        (
            query.reshape(block_shape),
            keys.reshape(block_shape),
            values.reshape(block_shape),
            grad_att.reshape(block_shape),
            log_total,
        ),
    )
    return jnp.stack([piece.reshape(row_count, head_count * HEAD_DIM) for piece in pieces])


def on_device(
    tokens,
    grad_out,
    gates,
    routes,
    ln1_gain,
    ln1_bias,
    ln2_gain,
    ln2_bias,
    w_qkv,
    w_attn_out,
    w_expert_in,
    w_expert_out,
):
    stream = tokens.astype(jnp.float32)
    feature_count = stream.shape[1]
    normed = normalize(stream, ln1_gain, ln1_bias).astype(jnp.bfloat16)
    qkv_part, out_part = (
        lax.all_gather(w_qkv, "wide", axis=1, tiled=True),
        lax.all_gather(w_attn_out, "wide", axis=1, tiled=True),
    )
    qkv_full, out_full = (qkv_part, out_part)
    att_rows = narrow_rows(normed)
    projected = jnp.einsum(
        "rd,jdc->jrc", att_rows, qkv_full, preferred_element_type=jnp.float32
    ).astype(jnp.bfloat16)
    head_count = projected.shape[2] // HEAD_DIM
    attended, log_total = attention_forward(projected[0], projected[1], projected[2], head_count)
    branch = jnp.dot(attended, out_full, preferred_element_type=jnp.float32)
    att_sum = narrow_sums(branch)
    resid = stream + att_sum
    normed_two = normalize(resid, ln2_gain, ln2_bias).astype(jnp.bfloat16)
    slot_ids, sources = route_slots(routes)
    owner_rows = sources // TOP
    padded = jnp.concatenate([normed_two, jnp.zeros((1, feature_count), jnp.bfloat16)], axis=0)
    dispatched = padded[owner_rows].reshape(CAP, EXPERTS, feature_count)
    gathered_slots = narrow_rows(dispatched)
    in_full, down_full = (
        lax.all_gather(w_expert_in, "wide", axis=1, tiled=True),
        lax.all_gather(w_expert_out, "wide", axis=2, tiled=True),
    )
    down_form = "cef,efd->ced"
    back_form = "ced,efd->cef"
    grad_down_form = "cef,ced->efd"
    preact = jnp.einsum("ced,edf->cef", gathered_slots, in_full, preferred_element_type=jnp.float32)
    activated = jax.nn.gelu(preact).astype(jnp.bfloat16)
    partial_out = jnp.einsum(down_form, activated, down_full, preferred_element_type=jnp.float32)
    expert_flat = narrow_sums(partial_out).reshape(CAP * EXPERTS, feature_count)
    mixed = (resid + jnp.sum(gates[:, :, None] * expert_flat[slot_ids], axis=1)).astype(
        jnp.bfloat16
    )
    cotangent = grad_out.astype(jnp.float32)
    gate_pad = jnp.concatenate([gates.reshape(-1), jnp.zeros((1,), jnp.float32)], axis=0)
    cot_pad = jnp.concatenate([cotangent, jnp.zeros((1, feature_count), jnp.float32)], axis=0)
    grad_disp = (
        (gate_pad[sources][:, None] * cot_pad[owner_rows])
        .astype(jnp.bfloat16)
        .reshape(CAP, EXPERTS, feature_count)
    )
    grad_slots = narrow_rows(grad_disp)
    grad_activated = jnp.einsum(
        back_form, grad_slots, down_full, preferred_element_type=jnp.float32
    )
    gelu_back = jax.vjp(jax.nn.gelu, preact)[1]
    grad_preact = gelu_back(grad_activated)[0].astype(jnp.bfloat16)
    grad_down = jnp.einsum(
        grad_down_form, activated, grad_slots, preferred_element_type=jnp.float32
    )
    grad_in = jnp.einsum(
        "ced,cef->edf", gathered_slots, grad_preact, preferred_element_type=jnp.float32
    )
    grad_partial = jnp.einsum(
        "cef,edf->ced", grad_preact, in_full, preferred_element_type=jnp.float32
    )
    grad_slot_rows = narrow_sums(grad_partial).reshape(CAP * EXPERTS, feature_count)
    grad_normed_two = jnp.sum(grad_slot_rows[slot_ids], axis=1)
    norm_two_back = jax.vjp(normalize, resid, ln2_gain, ln2_bias)[1]
    grad_resid_norm, grad_gain_two, grad_bias_two = norm_two_back(grad_normed_two)
    grad_resid = cotangent + grad_resid_norm
    grad_branch = grad_resid.astype(jnp.bfloat16)
    grad_branch_rows = narrow_rows(grad_branch)
    grad_out_weight = jnp.dot(attended.T, grad_branch_rows, preferred_element_type=jnp.float32)
    grad_att = jnp.dot(grad_branch_rows, out_full.T, preferred_element_type=jnp.float32).astype(
        jnp.bfloat16
    )
    grad_proj = attention_backward(
        projected[0], projected[1], projected[2], grad_att, log_total, head_count
    )
    grad_qkv_weight = jnp.einsum(
        "rd,jrc->jdc", att_rows, grad_proj, preferred_element_type=jnp.float32
    )
    grad_normed_part = jnp.einsum(
        "jrc,jdc->rd", grad_proj, qkv_full, preferred_element_type=jnp.float32
    )
    grad_normed = narrow_sums(grad_normed_part)
    norm_one_back = jax.vjp(normalize, stream, ln1_gain, ln1_bias)[1]
    grad_stream_norm, grad_gain_one, grad_bias_one = norm_one_back(grad_normed)
    grad_input = grad_resid + grad_stream_norm
    grad_in_block, grad_down_block = (
        lax.psum_scatter(
            grad_in.astype(jnp.bfloat16), "wide", scatter_dimension=1, tiled=True
        ).astype(jnp.float32),
        lax.psum_scatter(
            grad_down.astype(jnp.bfloat16), "wide", scatter_dimension=2, tiled=True
        ).astype(jnp.float32),
    )
    grad_qkv_block, grad_out_block = (
        lax.psum_scatter(
            grad_qkv_weight.astype(jnp.bfloat16), "wide", scatter_dimension=1, tiled=True
        ).astype(jnp.float32),
        lax.psum_scatter(
            grad_out_weight.astype(jnp.bfloat16), "wide", scatter_dimension=1, tiled=True
        ).astype(jnp.float32),
    )
    block_grads = (
        lax.psum(grad_qkv_block.astype(jnp.bfloat16), "dp").astype(jnp.float32),
        lax.psum(grad_out_block.astype(jnp.bfloat16), "dp").astype(jnp.float32),
        lax.psum(grad_in_block.astype(jnp.bfloat16), "dp").astype(jnp.float32),
        lax.psum(grad_down_block.astype(jnp.bfloat16), "dp").astype(jnp.float32),
    )
    norm_totals = lax.psum(
        (grad_gain_one, grad_bias_one, grad_gain_two, grad_bias_two), ("dp", "wide", "narrow")
    )
    return (
        mixed,
        grad_input,
        norm_totals[0],
        norm_totals[1],
        norm_totals[2],
        norm_totals[3],
        block_grads[0],
        block_grads[1],
        block_grads[2],
        block_grads[3],
    )


def solution(mesh):
    dp, wide, narrow = (mesh.shape[name] for name in ("dp", "wide", "narrow"))
    for rep in (2, 1):
        if dp % rep == 0 and EXPERTS % ((dp // rep) * wide * narrow) == 0:
            sizes = (rep, dp // rep, wide, narrow)
            split = Mesh(mesh.devices.reshape(sizes), ("rep", "own", "wide", "narrow"))
            return placed(functools.partial(owned_on_device, sizes), split, ("rep", "own"))
    return placed(on_device, mesh, ("dp",))


def placed(function, mesh, dp_axes):
    rows = P(dp_axes + ("wide", "narrow"), None)
    specs_in = (
        rows,
        rows,
        rows,
        rows,
        P(),
        P(),
        P(),
        P(),
        P(None, "wide", "narrow"),
        P("narrow", "wide"),
        P(None, "wide", "narrow"),
        P(None, "narrow", "wide"),
    )
    specs_out = (
        rows,
        rows,
        P(),
        P(),
        P(),
        P(),
        P(None, "wide", "narrow"),
        P("narrow", "wide"),
        P(None, "wide", "narrow"),
        P(None, "narrow", "wide"),
    )
    return jax.shard_map(
        function, mesh=mesh, in_specs=specs_in, out_specs=specs_out, check_vma=False
    )
```

```python
import functools
import math

import jax
import jax.numpy as jnp
from jax import lax
from jax.experimental import pallas as pl
from jax.experimental.pallas import tpu as pltpu
from jax.sharding import Mesh, PartitionSpec as P

HEAD_DIM = 64
EXPERTS = 32
TOP = 2
SEQ = 197
IMG_STEP = 4
CAP = 66

norm_eps = 1e-06

f32 = jnp.float32
bf16 = jnp.bfloat16


SLOTS = -(-CAP // 8) * 8
IMG_ROWS = -(-SEQ // 16) * 16
LANES = 128
TAIL = 16
VMEM_LIMIT = 56 * 1024 * 1024


def dot(a, b):
    return lax.dot_general(a, b, (((1,), (0,)), ((), ())), preferred_element_type=f32)


def dot_bt(a, b):
    return lax.dot_general(a, b, (((1,), (1,)), ((), ())), preferred_element_type=f32)


def dot_at(a, b):
    return lax.dot_general(a, b, (((0,), (0,)), ((), ())), preferred_element_type=f32)


def norm_parts(values):
    average = jnp.mean(values, axis=-1, keepdims=True)
    centered = values - average
    scale = lax.rsqrt(jnp.mean(centered * centered, axis=-1, keepdims=True) + norm_eps)
    return centered * scale, scale


def norm_back(hat, scale, gain, grad):
    t = grad * gain
    return scale * (
        t
        - jnp.mean(t, axis=-1, keepdims=True)
        - hat * jnp.mean(t * hat, axis=-1, keepdims=True)
    )


def full_spec(shape):
    zeros = (0,) * len(shape)
    return pl.BlockSpec(shape, lambda *_: zeros)


def image_spec(shape):
    rest = (0,) * (len(shape) - 1)
    return pl.BlockSpec((1,) + shape[1:], lambda i: (i,) + rest)


def back_rows(slot_ref, k, group, wide, offset):
    first = TOP + k if wide else k
    here = slot_ref[0, :, 2 * TOP + k : 2 * TOP + k + 1] == group
    return jnp.where(here, slot_ref[0, :, first : first + 1] + offset, -1)


def one_hot(mask):
    return mask.astype(f32).astype(bf16)


def route_kernel(plane, own_ref, routes_ref, routes_t_ref, back_ref, slot_t_ref):
    rows = routes_ref.shape[0]
    quarters = EXPERTS // plane
    groups = quarters // 2
    before = lax.broadcasted_iota(jnp.int32, (rows, rows), 0)
    after = lax.broadcasted_iota(jnp.int32, (rows, rows), 1)
    ids_t = lax.broadcasted_iota(jnp.int32, (EXPERTS, rows), 0)
    ids = lax.broadcasted_iota(jnp.int32, (rows, EXPERTS), 1)
    hot_t = [(ids_t == routes_t_ref[k : k + 1, :]).astype(f32) for k in range(TOP)]
    hot = [(ids == routes_ref[:, k : k + 1]).astype(f32) for k in range(TOP)]
    count_t = dot(sum(hot_t).astype(bf16), one_hot(before < after))
    count = dot(one_hot(after < before), sum(hot).astype(bf16))

    def place_of(ids):
        group, parity = ids // (2 * plane), ids // plane % 2
        return ids % plane, jnp.where(parity == own_ref[0], group, groups + group)

    for k in range(TOP):
        rank_t = jnp.sum(hot_t[k] * count_t, axis=0, keepdims=True).astype(jnp.int32)
        place, q = place_of(routes_t_ref[k : k + 1, :])
        slot_t_ref[k : k + 1, :] = (place * quarters + q) * SLOTS + rank_t
        rank = jnp.sum(hot[k] * count, axis=1, keepdims=True).astype(jnp.int32)
        chosen = routes_ref[:, k : k + 1]
        item = chosen % (2 * plane)
        back_ref[:, k : k + 1] = item * SLOTS + rank
        back_ref[:, TOP + k : TOP + k + 1] = item * 2 * SLOTS + rank
        back_ref[:, 2 * TOP + k : 2 * TOP + k + 1] = chosen // (2 * plane)


def route(own, routes, plane):
    rows = routes.shape[0]
    return pl.pallas_call(
        functools.partial(route_kernel, plane),
        in_specs=[pl.BlockSpec(memory_space=pltpu.SMEM)] + [pl.BlockSpec(memory_space=pltpu.VMEM)] * 2,
        out_shape=[
            jax.ShapeDtypeStruct((rows, 3 * TOP), jnp.int32),
            jax.ShapeDtypeStruct((TOP, rows), jnp.int32),
        ],
        compiler_params=pltpu.CompilerParams(vmem_limit_bytes=VMEM_LIMIT),
        cost_estimate=pl.CostEstimate(flops=60_000_000, bytes_accessed=100_000, transcendentals=0),
        name="route",
    )(own, routes, routes.T)


def grad_slots_kernel(plane, own_ref, sent_ref, *gd_refs):
    rows = sent_ref.shape[1] - 2 * HEADER
    features = sent_ref.shape[2]
    header = jnp.concatenate(
        [sent_ref[0, i * HEADER : (i + 1) * HEADER, :].astype(f32) for i in range(2)], axis=1
    )[:, :rows]
    before = lax.broadcasted_iota(jnp.int32, (rows, rows), 0)
    after = lax.broadcasted_iota(jnp.int32, (rows, rows), 1)
    ids_t = lax.broadcasted_iota(jnp.int32, (EXPERTS, rows), 0)
    routes = [header[k : k + 1, :].astype(jnp.int32) for k in range(TOP)]
    gates = [
        (header[2 + k : 3 + k, :] + header[4 + k : 5 + k, :]) + header[6 + k : 7 + k, :]
        for k in range(TOP)
    ]
    hot = [(ids_t == routes[k]).astype(f32) for k in range(TOP)]
    count = dot(sum(hot).astype(bf16), one_hot(before < after))
    slots = []
    for k in range(TOP):
        rank = jnp.sum(hot[k] * count, axis=0, keepdims=True).astype(jnp.int32)
        q = routes[k] // plane
        slot = ((q // 2) * plane + routes[k] % plane) * SLOTS + rank
        slots.append(jnp.where(q % 2 == own_ref[0], slot, -1))
    cot = sent_ref[0, 2 * HEADER :, :]
    per = plane * SLOTS
    for g, gd_ref in enumerate(gd_refs):
        place = lax.broadcasted_iota(jnp.int32, (per, rows), 0) + g * per
        here = [place == slot for slot in slots]
        gate = sum(jnp.where(here[k], gates[k], 0.0) for k in range(TOP))
        picked = dot(one_hot(here[0] | here[1]), cot)
        weighed = jnp.sum(gate, axis=1, keepdims=True) * picked
        for p in range(plane):
            gd_ref[p, 0] = weighed[p * SLOTS : (p + 1) * SLOTS, :].astype(bf16)


HEADER = 8


def with_header(routes, gates, cot):
    rows, features = cot.shape
    high = lax.reduce_precision(gates, 8, 7)
    middle = lax.reduce_precision(gates - high, 8, 7)
    low = (gates - high) - middle
    lines = jnp.concatenate([v.T for v in (routes.astype(f32), high, middle, low)], axis=0)
    lines = jnp.pad(lines, ((0, 0), (0, 2 * features - rows))).astype(bf16)
    return jnp.concatenate([lines[:, :features], lines[:, features:], cot], axis=0)


def grad_slots(own, sent, plane, groups):
    chunks, rows, features = sent.shape
    shape = (plane, chunks, SLOTS, features)
    return pl.pallas_call(
        functools.partial(grad_slots_kernel, plane),
        grid_spec=pltpu.PrefetchScalarGridSpec(
            num_scalar_prefetch=1,
            grid=(chunks,),
            in_specs=[pl.BlockSpec((1, rows, features), lambda i, own: (own[1] ^ i, 0, 0))],
            out_specs=[
                pl.BlockSpec((plane, 1, SLOTS, features), lambda i, own: (0, i, 0, 0))
            ]
            * groups,
        ),
        out_shape=[jax.ShapeDtypeStruct(shape, bf16)] * groups,
        compiler_params=pltpu.CompilerParams(vmem_limit_bytes=VMEM_LIMIT),
        cost_estimate=pl.CostEstimate(flops=8_000_000_000, bytes_accessed=10_000_000, transcendentals=0),
        name="grad_slots",
    )(own, sent)


def unpack_weights(wide, narrow, spot_ref, weights_refs, qkv_scratch, out_scratch):
    deep, across = qkv_scratch.shape[1] // wide, LANES
    for k in range(wide * narrow):
        block_ref = weights_refs[k % 2].at[k // 2]
        x = spot_ref[0] ^ (k // narrow)
        n = spot_ref[1] ^ (k % narrow)
        x_at = pl.multiple_of(x * deep, deep)
        n_at = pl.multiple_of(n * across, across)
        for j in range(3):
            qkv_scratch[j, pl.ds(x_at, deep), pl.ds(n_at, across)] = block_ref[
                j * deep : (j + 1) * deep, :
            ]
        for c in range(deep // LANES):
            first = 3 * deep + c * across
            out_scratch[
                pl.ds(n_at, across), pl.ds(pl.multiple_of(x_at + c * LANES, LANES), LANES)
            ] = block_ref[first : first + across, :]


def head_masks():
    lane = lax.broadcasted_iota(jnp.int32, (1, LANES), 1)
    per = LANES // HEAD_DIM
    return [(lane // HEAD_DIM) == h for h in range(per)]


def masked(value, mask):
    return jnp.where(mask, value, jnp.zeros_like(value))


def forward_kernel(
    wide,
    narrow,
    tile,
    spot_ref,
    tokens_ref,
    norms_ref,
    weights_a_ref,
    weights_b_ref,
    slot_t_ref,
    proj_ref,
    att_ref,
    resid_ref,
    x_ref,
    qkv_w,
    out_w,
    norm_scratch,
):
    step = pl.program_id(0)
    features = tokens_ref.shape[2]

    @pl.when(step == 0)
    def _():
        unpack_weights(wide, narrow, spot_ref, (weights_a_ref, weights_b_ref), qkv_w, out_w)
        norm_scratch[...] = jnp.zeros_like(norm_scratch)

    stream = tokens_ref[0].astype(f32)
    hat, _ = norm_parts(stream)
    normed = (hat * norms_ref[0:1, :] + norms_ref[1:2, :]).astype(bf16)
    proj = [dot(normed, qkv_w[j]).astype(bf16) for j in range(3)]
    for j in range(3):
        proj_ref[0, :, j * features : (j + 1) * features] = proj[j]
    masks = head_masks()
    scale = HEAD_DIM ** (-0.5)
    pieces = []
    for pair in range(features // LANES):
        cols = slice(pair * LANES, (pair + 1) * LANES)
        q, k, v = proj[0][:, cols], proj[1][:, cols], proj[2][:, cols]
        total = None
        for mask in masks:
            scores = dot_bt(masked(q, mask), k) * scale
            weights = jnp.exp(scores - jnp.max(scores, axis=-1, keepdims=True))
            probs = weights / jnp.sum(weights, axis=-1, keepdims=True)
            one = dot(probs.astype(bf16), masked(v, mask))
            total = one if total is None else total + one
        pieces.append(total.astype(bf16))
    attended = jnp.concatenate(pieces, axis=1)
    att_ref[0] = attended
    resid = stream + dot(attended, out_w[...])
    resid_ref[0] = resid
    hat_two, _ = norm_parts(resid)
    norm_scratch[step, : stream.shape[0], :] = (
        hat_two * norms_ref[2:3, :] + norms_ref[3:4, :]
    ).astype(bf16)

    @pl.when(step == pl.num_programs(0) - 1)
    def _():
        count = slot_t_ref.shape[1]
        rows = norm_scratch[...].reshape(count, features)
        for start in range(0, x_ref.shape[0], tile):
            place = lax.broadcasted_iota(jnp.int32, (tile, count), 0) + start
            here = (place == slot_t_ref[0:1, :]) | (place == slot_t_ref[1:2, :])
            x_ref[start : start + tile, :] = dot(one_hot(here), rows).astype(bf16)


def attention_and_slots(spot, tokens, norms, weights, slot_t, wide, narrow):
    images, rows, features = tokens.shape
    total = EXPERTS * SLOTS
    tile = 384 if total % 384 == 0 else SLOTS * wide * narrow
    per_image = [(images, rows, 3 * features), (images, rows, features), (images, rows, features)]
    return pl.pallas_call(
        functools.partial(forward_kernel, wide, narrow, tile),
        grid=(images,),
        in_specs=[
            pl.BlockSpec(memory_space=pltpu.SMEM),
            image_spec(tokens.shape),
            full_spec(norms.shape),
            full_spec(weights[0].shape),
            full_spec(weights[1].shape),
            full_spec(slot_t.shape),
        ],
        out_specs=[image_spec(s) for s in per_image] + [full_spec((total, features))],
        out_shape=[
            jax.ShapeDtypeStruct(per_image[0], bf16),
            jax.ShapeDtypeStruct(per_image[1], bf16),
            jax.ShapeDtypeStruct(per_image[2], f32),
            jax.ShapeDtypeStruct((total, features), bf16),
        ],
        scratch_shapes=[
            pltpu.VMEM((3, features, features), bf16),
            pltpu.VMEM((features, features), bf16),
            pltpu.VMEM((images, IMG_ROWS, features), bf16),
        ],
        compiler_params=pltpu.CompilerParams(vmem_limit_bytes=VMEM_LIMIT),
        cost_estimate=pl.CostEstimate(flops=6_000_000_000, bytes_accessed=9_000_000, transcendentals=2_000_000),
        name="attention_forward",
    )(spot, tokens, norms, *weights, slot_t)


def pack_kernel(first_ref, w_in_ref, w_out_ref, *out_refs):
    deep, hidden = w_in_ref.shape[1], w_in_ref.shape[2]
    base = deep * (hidden // LANES) if len(out_refs) == 1 else 0
    for c in range(hidden // LANES):
        out_refs[0][0, c * deep : (c + 1) * deep, :] = w_in_ref[0, :, c * LANES : (c + 1) * LANES]
    for c in range(deep // LANES):
        out_refs[-1][0, base + c * hidden : base + (c + 1) * hidden, :] = w_out_ref[
            0, :, c * LANES : (c + 1) * LANES
        ]


def pack(first, w_in, w_out, plane, arrays):
    deep, hidden = w_in.shape[1], w_in.shape[2]
    rows = 2 * deep * hidden // LANES // arrays
    at = lambda i, first: (first[0] + i, 0, 0)
    return pl.pallas_call(
        pack_kernel,
        grid_spec=pltpu.PrefetchScalarGridSpec(
            num_scalar_prefetch=1,
            grid=(plane,),
            in_specs=[pl.BlockSpec((1, deep, hidden), at), pl.BlockSpec((1, hidden, deep), at)],
            out_specs=[pl.BlockSpec((1, rows, LANES), lambda i, first: (i, 0, 0))] * arrays,
        ),
        out_shape=[jax.ShapeDtypeStruct((plane, rows, LANES), bf16)] * arrays,
        cost_estimate=pl.CostEstimate(flops=0, bytes_accessed=9_000_000, transcendentals=0),
        name="pack_weights",
    )(first, w_in, w_out)


GELU_A = math.sqrt(2.0 / math.pi)
GELU_B = 0.044715 * GELU_A


def gelu_pair(u):
    u2 = u * u
    p = GELU_B * u2 + GELU_A
    half = 0.5 * jnp.tanh(u * p) + 0.5
    slope = half + (u * (6.0 * p - 4.0 * GELU_A)) * (half - half * half)
    return u * half, slope


def identity(size):
    a = lax.broadcasted_iota(jnp.int32, (size, size), 0)
    b = lax.broadcasted_iota(jnp.int32, (size, size), 1)
    return (a == b).astype(f32).astype(bf16)


def expert_kernel(deep, hidden, parts, tile, where_ref, *refs):
    x_refs, (gd_ref, wi_ref, wo_ref, gi_ref, go_ref) = refs[:parts], refs[parts : parts + 5]
    gx_ref, y_ref = refs[parts + 5 : parts + 7]
    (x_s, gd_s, act, gp, wi_s, wo_s, y_acc, gx_acc, sem) = refs[parts + 7 :]
    step = pl.program_id(0)
    wide = wi_ref.shape[0]
    rows, features = x_s.shape
    own_rows = rows // 2
    chunk = own_rows // 2

    @pl.when(step == 0)
    def _():
        copies = [pltpu.make_async_copy(gd_ref, gd_s, sem.at[parts])]
        first = 0
        for i, x_ref in enumerate(x_refs):
            part = x_ref if len(x_ref.shape) == 2 else x_ref.at[where_ref[0]]
            count = part.shape[0]
            copies.append(pltpu.make_async_copy(part, x_s.at[pl.ds(first, count), :], sem.at[i]))
            first += count
        for copy in copies:
            copy.start()
        y_acc[...] = jnp.zeros_like(y_acc)
        gx_acc[...] = jnp.zeros_like(gx_acc)
        for copy in copies:
            copy.wait()


    for x in range(wide):
        for c in range(hidden // LANES):
            wi_s[x * deep : (x + 1) * deep, c * LANES : (c + 1) * LANES] = wi_ref[
                x, 0, c * deep : (c + 1) * deep, :
            ]
        for c in range(deep // LANES):
            first = x * deep + c * LANES
            wo_s[:, first : first + LANES] = wo_ref[x, 0, c * hidden : (c + 1) * hidden, :]

    for t in range(rows // tile):
        at = slice(t * tile, (t + 1) * tile)
        value, slope = gelu_pair(dot(x_s[at, :], wi_s[...]))
        value = value.astype(bf16)
        act[at, :] = value
        back = (dot_bt(gd_s[at, :], wo_s[...]) * slope).astype(bf16)
        gp[at, :] = back
        if t < own_rows // tile:
            y_acc[at, :] += dot(value, wo_s[...])
            gx_acc[at, :] += dot_bt(back, wi_s[...])
    gin = dot_at(x_s[...], gp[...]).astype(bf16)
    for x in range(wide):
        for c in range(hidden // LANES):
            gi_ref[x, 0, c * deep : (c + 1) * deep, :] = gin[
                x * deep : (x + 1) * deep, c * LANES : (c + 1) * LANES
            ]
    gout = dot_at(act[...], gd_s[...]).astype(bf16)
    for x in range(wide):
        for c in range(deep // LANES):
            first = x * deep + c * LANES
            go_ref[x, 0, c * hidden : (c + 1) * hidden, :] = gout[:, first : first + LANES]

    @pl.when(step == pl.num_programs(0) - 1)
    def _():
        for i in range(2):
            at = slice(i * chunk, (i + 1) * chunk)
            to = pl.ds(pl.multiple_of((where_ref[1] ^ i) * chunk, chunk), chunk)
            gx_ref[to, :] = gx_acc[at, :].astype(bf16)
            y_ref[to, :] = y_acc[at, :].astype(bf16)


def expert(where, xs, gd, weights, wide, narrow, deep, hidden):
    rows, features = gd.shape
    own_rows = rows // 2
    chunk = own_rows // 2
    packed = deep * hidden // LANES
    last = len(weights) - 1
    tile = 384 if own_rows % 384 == 0 else SLOTS * 2
    anywhere = pl.BlockSpec(memory_space=pl.ANY)
    whole = lambda shape: pl.BlockSpec(shape, lambda s: (0,) * len(shape))
    per_step = pl.BlockSpec((wide, 1, packed, LANES), lambda s: (0, s, 0, 0))
    blocks = (wide, narrow, packed, LANES)
    g_in, g_out, gx, y = pl.pallas_call(
        functools.partial(expert_kernel, deep, hidden, len(xs), tile),
        grid=(narrow,),
        in_specs=[pl.BlockSpec(memory_space=pltpu.SMEM)] + [anywhere] * (len(xs) + 1)
        + [per_step, pl.BlockSpec((wide, 1, packed, LANES), lambda s: (0, s, 1 - last, 0))],
        out_specs=[per_step] * 2 + [whole((own_rows, features))] * 2,
        scratch_shapes=[
            pltpu.VMEM((rows, features), bf16),
            pltpu.VMEM((rows, features), bf16),
            pltpu.VMEM((rows, hidden), bf16),
            pltpu.VMEM((rows, hidden), bf16),
            pltpu.VMEM((features, hidden), bf16),
            pltpu.VMEM((hidden, features), bf16),
            pltpu.VMEM((own_rows, features), f32),
            pltpu.VMEM((own_rows, features), f32),
            pltpu.SemaphoreType.DMA((len(xs) + 1,)),
        ],
        out_shape=[
            jax.ShapeDtypeStruct(blocks, bf16),
            jax.ShapeDtypeStruct(blocks, bf16),
        ]
        + [jax.ShapeDtypeStruct((own_rows, features), bf16)] * 2,
        compiler_params=pltpu.CompilerParams(vmem_limit_bytes=VMEM_LIMIT),
        cost_estimate=pl.CostEstimate(
            flops=2 * narrow * features * hidden * (4 * rows + 2 * own_rows),
            bytes_accessed=20_000_000,
            transcendentals=rows * hidden * narrow,
        ),
        name="expert",
    )(where, *xs, gd, *[w.reshape((wide, narrow) + w.shape[1:]) for w in (weights[0], weights[last])])
    return [g.reshape(wide * narrow, packed, LANES) for g in (g_in, g_out)], gx, y


def place_kernel(where_ref, g_ref, *refs):
    out_ref = refs[-1]
    rows = out_ref.shape[1]
    for i in range(out_ref.shape[0]):
        for c in range(out_ref.shape[2] // LANES):
            out_ref[i, :, c * LANES : (c + 1) * LANES] = g_ref[
                0, i, c * rows : (c + 1) * rows, :
            ].astype(f32)


def place(where, g, so_far, rows, columns):
    g = g.reshape((-1,) + g.shape[-3:])
    parts, plane, packed, _ = g.shape
    each = math.gcd(plane, 4)
    anywhere = pl.BlockSpec(memory_space=pl.ANY)
    part = (lambda where: where[0]) if parts > 1 else (lambda where: 0)
    return pl.pallas_call(
        place_kernel,
        grid_spec=pltpu.PrefetchScalarGridSpec(
            num_scalar_prefetch=1,
            grid=(plane // each,),
            in_specs=[pl.BlockSpec((1, each, packed, LANES), lambda i, where: (part(where), i, 0, 0))]
            + [anywhere] * len(so_far),
            out_specs=pl.BlockSpec(
                (each, rows, columns), lambda i, where: (where[1] // each + i, 0, 0)
            ),
        ),
        out_shape=jax.ShapeDtypeStruct((EXPERTS, rows, columns), f32),
        input_output_aliases={2 + i: i for i in range(len(so_far))},
        compiler_params=pltpu.CompilerParams(vmem_limit_bytes=VMEM_LIMIT),
        cost_estimate=pl.CostEstimate(flops=0, bytes_accessed=6_000_000, transcendentals=0),
        name="place_grads",
    )(where, g, *so_far)


def mixed_kernel(resid_ref, slot_ref, gates_ref, *rest):
    back_refs, mixed_ref = rest[:-1], rest[-1]
    total = resid_ref[0]
    rows = total.shape[0]
    for k in range(TOP):
        picked = None
        for g, back_ref in enumerate(back_refs):
            wide = g < len(back_refs) - 1
            place = lax.broadcasted_iota(jnp.int32, (rows, back_ref.shape[0]), 1)
            here = place == back_rows(slot_ref, k, g, wide, SLOTS if wide else 0)
            one = dot(one_hot(here), back_ref[...])
            picked = one if picked is None else picked + one
        total = total + gates_ref[0, :, k : k + 1] * picked
    mixed_ref[0] = total.astype(bf16)


def mix(resid, slots, gates, backs):
    return pl.pallas_call(
        mixed_kernel,
        grid=(resid.shape[0],),
        in_specs=[image_spec(resid.shape), image_spec(slots.shape), image_spec(gates.shape)]
        + [full_spec(y.shape) for y in backs],
        out_specs=image_spec(resid.shape),
        out_shape=jax.ShapeDtypeStruct(resid.shape, bf16),
        compiler_params=pltpu.CompilerParams(vmem_limit_bytes=VMEM_LIMIT),
        cost_estimate=pl.CostEstimate(flops=6_000_000_000, bytes_accessed=6_000_000, transcendentals=0),
        name="mix",
    )(resid, slots, gates, *backs)


def backward_kernel(wide, narrow, parts, *refs):
    (spot_ref, tokens_ref, cot_ref, norms_ref, weights_a_ref, weights_b_ref) = refs[:6]
    (slot_ref, proj_ref, att_ref, resid_ref) = refs[6:10]
    back_refs = refs[10 : 10 + parts]
    (grad_ref, grads_w_ref) = refs[10 + parts : 12 + parts]
    (qkv_w, out_w, normed_s, att_s, branch_s, proj_s, grads_n_ref) = refs[12 + parts :]
    step = pl.program_id(0)
    rows, features = tokens_ref.shape[1], tokens_ref.shape[2]

    @pl.when(step == 0)
    def _():
        unpack_weights(wide, narrow, spot_ref, (weights_a_ref, weights_b_ref), qkv_w, out_w)
        normed_s[...] = jnp.zeros_like(normed_s)
        att_s[...] = jnp.zeros_like(att_s)
        branch_s[...] = jnp.zeros_like(branch_s)
        proj_s[...] = jnp.zeros_like(proj_s)
        grads_n_ref[...] = jnp.zeros_like(grads_n_ref)

    grad_normed = None
    for g, back_ref in enumerate(back_refs):
        place = lax.broadcasted_iota(jnp.int32, (rows, back_ref.shape[0]), 1)
        own = [back_rows(slot_ref, k, g, g < parts - 1, 0) for k in range(TOP)]
        here = (place == own[0]) | (place == own[1])
        one = dot(one_hot(here), back_ref[...])
        grad_normed = one if grad_normed is None else grad_normed + one
    hat_two, scale_two = norm_parts(resid_ref[0])
    grads_n_ref[2:3, :] += jnp.sum(grad_normed * hat_two, axis=0, keepdims=True)
    grads_n_ref[3:4, :] += jnp.sum(grad_normed, axis=0, keepdims=True)
    grad_resid = cot_ref[0].astype(f32) + norm_back(
        hat_two, scale_two, norms_ref[2:3, :], grad_normed
    )
    branch = grad_resid.astype(bf16)
    branch_s[step, :rows, :] = branch
    att_s[step, :rows, :] = att_ref[0]
    grad_att = dot_bt(branch, out_w[...]).astype(bf16)

    masks = head_masks()
    scale = HEAD_DIM ** (-0.5)
    pairs = features // LANES
    pieces = [[None] * pairs for _ in range(3)]
    for pair in range(pairs):
        at = [j * features + pair * LANES for j in range(3)]
        q, k, v = [proj_ref[0, :, a : a + LANES] for a in at]
        ga = grad_att[:, pair * LANES : (pair + 1) * LANES]
        sums = [None] * 3
        for mask in masks:
            scores = dot_bt(masked(k, mask), q) * scale
            weights = jnp.exp(scores - jnp.max(scores, axis=0, keepdims=True))
            probs = weights / jnp.sum(weights, axis=0, keepdims=True)
            ga_h = masked(ga, mask)
            dprobs = dot_bt(v, ga_h)
            inner = jnp.sum(probs * dprobs, axis=0, keepdims=True)
            grad_scores = (probs * (dprobs - inner)).astype(bf16)
            parts_h = (
                dot_at(grad_scores, masked(k, mask)),
                dot(grad_scores, masked(q, mask)),
                dot(probs.astype(bf16), ga_h),
            )
            for j in range(3):
                sums[j] = parts_h[j] if sums[j] is None else sums[j] + parts_h[j]
        pieces[0][pair] = (sums[0] * scale).astype(bf16)
        pieces[1][pair] = (sums[1] * scale).astype(bf16)
        pieces[2][pair] = sums[2].astype(bf16)

    stream = tokens_ref[0].astype(f32)
    hat, scale_one = norm_parts(stream)
    normed_s[step, :rows, :] = (hat * norms_ref[0:1, :] + norms_ref[1:2, :]).astype(bf16)
    grad_first = None
    for j in range(3):
        grad_proj = jnp.concatenate(pieces[j], axis=1)
        proj_s[j, step, :rows, :] = grad_proj
        one = dot_bt(grad_proj, qkv_w[j])
        grad_first = one if grad_first is None else grad_first + one
    grads_n_ref[0:1, :] += jnp.sum(grad_first * hat, axis=0, keepdims=True)
    grads_n_ref[1:2, :] += jnp.sum(grad_first, axis=0, keepdims=True)
    grad_ref[0] = grad_resid + norm_back(hat, scale_one, norms_ref[0:1, :], grad_first)

    @pl.when(step == pl.num_programs(0) - 1)
    def _():
        count = normed_s.shape[0] * normed_s.shape[1]
        deep = features // wide
        flat = lambda value: value.reshape(count, features)
        normed_t = flat(normed_s[...])
        for j in range(3):
            grad = dot_at(normed_t, flat(proj_s[j])).astype(bf16)
            for x in range(wide):
                for n in range(narrow):
                    grads_w_ref[x * narrow + n, j * deep : (j + 1) * deep, :] = grad[
                        x * deep : (x + 1) * deep, n * LANES : (n + 1) * LANES
                    ]
        per = features // LANES
        tail = jnp.concatenate(
            [
                grads_n_ref[i : i + 1, c * LANES : (c + 1) * LANES]
                for i in range(4)
                for c in range(per)
            ],
            axis=0,
        )
        high = tail.astype(bf16)
        both = jnp.concatenate([high, (tail - high.astype(f32)).astype(bf16)], axis=0)
        for d in range(wide * narrow):
            grads_w_ref[d, grads_w_ref.shape[1] - 2 * TAIL :, :] = both
        grad = dot_at(flat(att_s[...]), flat(branch_s[...])).astype(bf16)
        for x in range(wide):
            for n in range(narrow):
                for c in range(deep // LANES):
                    first = 3 * deep + c * LANES
                    grads_w_ref[x * narrow + n, first : first + LANES, :] = grad[
                        n * LANES : (n + 1) * LANES,
                        x * deep + c * LANES : x * deep + (c + 1) * LANES,
                    ]


def attention_back(spot, tokens, cot, norms, weights, slots, proj, att, resid, backs, wide, narrow):
    images, rows, features = tokens.shape
    stash = (images, IMG_ROWS, features)
    small = (wide * narrow, weights[0].shape[1] + 2 * TAIL, LANES)
    return pl.pallas_call(
        functools.partial(backward_kernel, wide, narrow, len(backs)),
        grid=(images,),
        in_specs=[
            pl.BlockSpec(memory_space=pltpu.SMEM),
            image_spec(tokens.shape),
            image_spec(cot.shape),
            full_spec(norms.shape),
            full_spec(weights[0].shape),
            full_spec(weights[1].shape),
            image_spec(slots.shape),
            image_spec(proj.shape),
            image_spec(att.shape),
            image_spec(resid.shape),
        ]
        + [full_spec(back.shape) for back in backs],
        out_specs=[image_spec(tokens.shape), full_spec(small)],
        out_shape=[
            jax.ShapeDtypeStruct(tokens.shape, f32),
            jax.ShapeDtypeStruct(small, bf16),
        ],
        scratch_shapes=[
            pltpu.VMEM((3, features, features), bf16),
            pltpu.VMEM((features, features), bf16),
            pltpu.VMEM(stash, bf16),
            pltpu.VMEM(stash, bf16),
            pltpu.VMEM(stash, bf16),
            pltpu.VMEM((3,) + stash, bf16),
            pltpu.VMEM((4, features), f32),
        ],
        compiler_params=pltpu.CompilerParams(vmem_limit_bytes=VMEM_LIMIT),
        cost_estimate=pl.CostEstimate(flops=9_000_000_000, bytes_accessed=12_000_000, transcendentals=2_000_000),
        name="attention_backward",
    )(spot, tokens, cot, norms, *weights, slots, proj, att, resid, *backs)


def owned_on_device(
    sizes,
    tokens,
    grad_out,
    gates,
    routes,
    ln1_gain,
    ln1_bias,
    ln2_gain,
    ln2_bias,
    w_qkv,
    w_attn_out,
    w_expert_in,
    w_expert_out,
):
    pairs, wide, narrow = sizes
    planes, plane = 2 * pairs, wide * narrow
    groups = EXPERTS // (2 * plane)
    rows, features = tokens.shape
    images = rows // SEQ
    qkv_deep = w_qkv.shape[1]
    deep, hidden = w_expert_in.shape[1], w_expert_in.shape[2]
    pair_index, parity = lax.axis_index("pair"), lax.axis_index("parity")
    x_index, n_index = lax.axis_index("wide"), lax.axis_index("narrow")
    own = parity.astype(jnp.int32).reshape(1)
    own_and_plane = jnp.stack([parity, 2 * pair_index + parity]).astype(jnp.int32)
    far_and_own = jnp.stack([1 - pair_index, parity]).astype(jnp.int32)
    spot = jnp.stack([x_index, n_index, x_index * narrow + n_index]).astype(jnp.int32)

    def in_plane(values):
        return lax.all_to_all(values, ("wide", "narrow"), 0, 0, tiled=True)

    def in_pair(values):
        return lax.all_to_all(values, ("parity", "wide", "narrow"), 0, 0, tiled=True)

    def across(values, k):
        return lax.ppermute(values, ("wide", "narrow"), [(i, i ^ k) for i in range(plane)])

    def along(values, k):
        return lax.ppermute(values, ("pair", "parity"), [(i, i ^ k) for i in range(planes)])

    def with_near(values):
        return lax.all_gather(values, "parity", axis=0)

    def after(values, first):
        return lax.optimization_barrier((values, first))[0]

    small = jnp.concatenate(
        [w_qkv.reshape(3 * qkv_deep, LANES)]
        + [w_attn_out[:, c * LANES : (c + 1) * LANES] for c in range(qkv_deep // LANES)],
        axis=0,
    )
    same_core = jnp.stack([small] + [across(small, k) for k in range(2, plane, 2)])
    weights = (same_core, across(same_core, 1))

    sent_all = lax.all_gather(with_header(routes, gates, grad_out), ("pair", "parity"), axis=0)

    back_slots, slot_t = route(own, routes, plane)
    packed = [
        pack(
            (g * 2 * plane + parity * plane).astype(jnp.int32).reshape(1),
            w_expert_in,
            w_expert_out,
            plane,
            1 if g else 2,
        )
        for g in range(groups)
    ]

    norms = jnp.stack([ln1_gain, ln1_bias, ln2_gain, ln2_bias])
    per_image = lambda values: values.reshape((images, SEQ) + values.shape[1:])
    slot_wide = jnp.pad(
        slot_t.reshape(TOP, images, SEQ), ((0, 0), (0, 0), (0, IMG_ROWS - SEQ)), constant_values=-1
    ).reshape(TOP, images * IMG_ROWS)
    tokens3, cot3, slots3, gates3 = map(per_image, (tokens, grad_out, back_slots, gates))
    proj, att, resid, x = attention_and_slots(
        spot, tokens3, norms, weights, slot_wide, wide, narrow
    )

    def quarter(moved, q):
        return moved[:, q * SLOTS : (q + 1) * SLOTS].reshape(plane * SLOTS, features)

    def by_plane(values):
        return jnp.moveaxis(values.reshape(plane, planes, SLOTS, features), 1, 0).reshape(
            planes * plane * SLOTS, features
        )

    gd_sent = grad_slots(own_and_plane, sent_all, plane, groups)
    first_in = in_plane(after(packed[0][0], same_core))
    moved = in_plane(after(x, first_in).reshape(plane, -1, features))
    first_out = in_plane(after(packed[0][1], (moved, gd_sent)))
    mine, other = quarter(moved, 0), quarter(moved, groups)
    nearest, far_mine = along(other, 1), along(mine, 2)
    xs = [[mine, nearest, far_mine, along(other, 3)]]
    gd_parts = [v.reshape(plane, planes * SLOTS, features) for v in gd_sent]
    gds = [by_plane(in_plane(after(gd_parts[0], (first_out, nearest, far_mine, packed[1:]))))]
    nears = [
        jnp.concatenate([quarter(moved, g), along(quarter(moved, groups + g), 1)], axis=0)
        for g in range(1, groups)
    ]
    xs += [
        [near, lax.all_gather(after(near, xs[0]), "pair", axis=0)] for near in nears
    ]

    def to_tokens(parts, before):
        sent = jnp.concatenate([v.reshape(2 * plane, SLOTS, features) for v in parts], axis=1)
        return in_pair(after(sent, before)).reshape(-1, features)

    shapes = ((deep, hidden), (hidden, deep))
    out_blocks = [(), ()]

    def put(i, g, own_part, before):
        which = parity if own_part else 1 - parity
        where = jnp.stack([which, g * 2 * plane + which * plane]).astype(jnp.int32)
        part = after((grads if own_part else swaps)[g][i], before)
        out_blocks[i] = (place(where, part, out_blocks[i], *shapes[i]),)

    def after_blocks(values):
        values, out_blocks[:] = lax.optimization_barrier((values, out_blocks))
        return values

    held = (first_in, first_out)
    before = (gds[0], xs[0], nears)
    grads, swaps, gx_back, y_back = [], [], [], []
    for g in range(groups):
        grad, gx, y = expert(far_and_own, xs[g], gds[g], held, wide, narrow, deep, hidden)
        grads.append([])
        swaps.append([])
        if g < groups - 1:
            held = tuple(in_plane(after(v, before)) for v in packed[g + 1])
            grads[g].append(in_plane(after(grad[0], held)))
            swaps[g].append(with_near(grads[g][0]))
            gds.append(by_plane(in_plane(after(gd_parts[g + 1], (grads[g][0], xs[g + 1])))))
            put(0, g, True, ())
            grads[g].append(in_plane(after_blocks(after(grad[1], gds[g + 1]))))
            swaps[g].append(with_near(grads[g][1]))
            gds[g + 1] = after(gds[g + 1], grads[g][1])
            before = to_tokens([gx, y], grads[g][1])
            y_back.append(before)
            gx_back.append(before)
        else:
            grads[g].append(in_plane(after(grad[0], before)))
            swaps[g].append(with_near(grads[g][0]))
            if g:
                put(1, g - 1, True, ())
                put(0, g - 1, False, ())
            before = to_tokens([after_blocks(gx)], grads[g][0])
            gx_back.append(before)
            grads[g].append(in_plane(after(grad[1], before)))
            before = grads[g][1]
            last_y = y

    last = groups - 1
    grad_input, grads_w = attention_back(
        spot, tokens3, cot3, norms, weights, slots3, proj, att, resid, gx_back, wide, narrow
    )
    count = grads_w.shape[1] - 2 * TAIL
    swaps[last].append(with_near(after(grads[last][1], grads_w)))
    grads_w = in_plane(after(grads_w, before))
    y_back.append(to_tokens([last_y], grads_w))
    for g in range(last):
        put(1, g, False, ())
    put(0, last, True, ())
    put(1, last, True, ())
    put(0, last, False, ())
    mixed = mix(after_blocks(resid), slots3, gates3, y_back).reshape(rows, features)
    put(1, last, False, mixed)
    (out_in,), (out_out,) = out_blocks
    summed = jnp.sum(grads_w.astype(f32), axis=0)
    tail = summed[count : count + TAIL] + summed[count + TAIL :]
    high = lax.reduce_precision(tail, 8, 7)
    block = jnp.concatenate(
        [summed[:count].astype(bf16), high.astype(bf16), (tail - high).astype(bf16)], axis=0
    )
    terms = after([block] + [along(block, k) for k in range(1, planes)], mixed)
    terms = [v.astype(f32) for v in terms]
    block = (terms[0] + terms[1]) + (terms[2] + terms[3])
    grads_n = (block[count : count + TAIL] + block[count + TAIL :]).reshape(4, features)
    grad_qkv = block[: 3 * qkv_deep].reshape(3, qkv_deep, LANES)
    grad_attn_out = jnp.concatenate(
        [
            block[3 * qkv_deep + c * LANES : 3 * qkv_deep + (c + 1) * LANES]
            for c in range(qkv_deep // LANES)
        ],
        axis=1,
    )
    return (
        mixed,
        grad_input.reshape(rows, features),
        grads_n[0],
        grads_n[1],
        grads_n[2],
        grads_n[3],
        grad_qkv,
        grad_attn_out,
        out_in,
        out_out,
    )


def normalize(values, norm_gain, norm_shift):
    average = jnp.mean(values, axis=-1, keepdims=True)
    centered = values - average
    scaled = centered * lax.rsqrt(jnp.mean(centered * centered, axis=-1, keepdims=True) + norm_eps)
    return scaled * norm_gain + norm_shift


def route_slots(routes):
    flat_ids = routes.reshape(-1)
    onehot = (flat_ids[:, None] == jnp.arange(EXPERTS, dtype=jnp.int32)[None, :]).astype(jnp.int32)
    order_rank = jnp.sum(
        (jnp.cumsum(onehot, axis=0, dtype=jnp.int32) - 1) * onehot, axis=1, dtype=jnp.int32
    )
    slot_ids = order_rank * EXPERTS + flat_ids
    entry_count = flat_ids.shape[0]
    sources = (
        jnp.full((CAP * EXPERTS,), entry_count, jnp.int32)
        .at[slot_ids]
        .set(jnp.arange(entry_count, dtype=jnp.int32))
    )
    return (slot_ids.reshape(routes.shape), sources)


def narrow_rows(values):
    return lax.all_gather(values, "narrow", axis=0, tiled=True)


def narrow_sums(values):
    return lax.psum_scatter(
        values.astype(jnp.bfloat16), "narrow", scatter_dimension=0, tiled=True
    ).astype(jnp.float32)


def attention_forward(query, keys, values, head_count):
    row_count = query.shape[0]
    group_count = row_count // (IMG_STEP * SEQ)
    block_shape = (group_count, IMG_STEP, SEQ, head_count, HEAD_DIM)
    score_scale = HEAD_DIM ** (-0.5)

    def one_group(block):
        query_blk, key_blk, value_blk = block
        scores = (
            jnp.einsum("ishd,ithd->ihst", query_blk, key_blk, preferred_element_type=jnp.float32)
            * score_scale
        )
        row_top = jnp.max(scores, axis=-1, keepdims=True)
        weights = jnp.exp(scores - row_top)
        row_total = jnp.sum(weights, axis=-1, keepdims=True)
        probs = weights / row_total
        output = jnp.einsum(
            "ihst,ithd->ishd",
            probs.astype(jnp.bfloat16),
            value_blk,
            preferred_element_type=jnp.float32,
        )
        return (output.astype(jnp.bfloat16), (row_top + jnp.log(row_total))[..., 0])

    output, log_total = lax.map(
        one_group,
        (query.reshape(block_shape), keys.reshape(block_shape), values.reshape(block_shape)),
    )
    return (output.reshape(row_count, head_count * HEAD_DIM), log_total)


def attention_backward(query, keys, values, grad_att, log_total, head_count):
    row_count = query.shape[0]
    group_count = row_count // (IMG_STEP * SEQ)
    block_shape = (group_count, IMG_STEP, SEQ, head_count, HEAD_DIM)
    score_scale = HEAD_DIM ** (-0.5)

    def one_group(block):
        query_blk, key_blk, value_blk, grad_blk, total_blk = block
        scores = (
            jnp.einsum("ishd,ithd->ihst", query_blk, key_blk, preferred_element_type=jnp.float32)
            * score_scale
        )
        probs = jnp.exp(scores - total_blk[..., None])
        dprobs = jnp.einsum(
            "ishd,ithd->ihst", grad_blk, value_blk, preferred_element_type=jnp.float32
        )
        inner = jnp.sum(probs * dprobs, axis=-1, keepdims=True)
        grad_scores = (probs * (dprobs - inner)).astype(jnp.bfloat16)
        grad_query = (
            jnp.einsum("ihst,ithd->ishd", grad_scores, key_blk, preferred_element_type=jnp.float32)
            * score_scale
        )
        grad_key = (
            jnp.einsum(
                "ihst,ishd->ithd", grad_scores, query_blk, preferred_element_type=jnp.float32
            )
            * score_scale
        )
        grad_value = jnp.einsum(
            "ihst,ishd->ithd",
            probs.astype(jnp.bfloat16),
            grad_blk,
            preferred_element_type=jnp.float32,
        )
        return (
            grad_query.astype(jnp.bfloat16),
            grad_key.astype(jnp.bfloat16),
            grad_value.astype(jnp.bfloat16),
        )

    pieces = lax.map(
        one_group,
        (
            query.reshape(block_shape),
            keys.reshape(block_shape),
            values.reshape(block_shape),
            grad_att.reshape(block_shape),
            log_total,
        ),
    )
    return jnp.stack([piece.reshape(row_count, head_count * HEAD_DIM) for piece in pieces])


def on_device(
    tokens,
    grad_out,
    gates,
    routes,
    ln1_gain,
    ln1_bias,
    ln2_gain,
    ln2_bias,
    w_qkv,
    w_attn_out,
    w_expert_in,
    w_expert_out,
):
    stream = tokens.astype(jnp.float32)
    feature_count = stream.shape[1]
    normed = normalize(stream, ln1_gain, ln1_bias).astype(jnp.bfloat16)
    qkv_part, out_part = (
        lax.all_gather(w_qkv, "wide", axis=1, tiled=True),
        lax.all_gather(w_attn_out, "wide", axis=1, tiled=True),
    )
    qkv_full, out_full = (qkv_part, out_part)
    att_rows = narrow_rows(normed)
    projected = jnp.einsum(
        "rd,jdc->jrc", att_rows, qkv_full, preferred_element_type=jnp.float32
    ).astype(jnp.bfloat16)
    head_count = projected.shape[2] // HEAD_DIM
    attended, log_total = attention_forward(projected[0], projected[1], projected[2], head_count)
    branch = jnp.dot(attended, out_full, preferred_element_type=jnp.float32)
    att_sum = narrow_sums(branch)
    resid = stream + att_sum
    normed_two = normalize(resid, ln2_gain, ln2_bias).astype(jnp.bfloat16)
    slot_ids, sources = route_slots(routes)
    owner_rows = sources // TOP
    padded = jnp.concatenate([normed_two, jnp.zeros((1, feature_count), jnp.bfloat16)], axis=0)
    dispatched = padded[owner_rows].reshape(CAP, EXPERTS, feature_count)
    gathered_slots = narrow_rows(dispatched)
    in_full, down_full = (
        lax.all_gather(w_expert_in, "wide", axis=1, tiled=True),
        lax.all_gather(w_expert_out, "wide", axis=2, tiled=True),
    )
    down_form = "cef,efd->ced"
    back_form = "ced,efd->cef"
    grad_down_form = "cef,ced->efd"
    preact = jnp.einsum("ced,edf->cef", gathered_slots, in_full, preferred_element_type=jnp.float32)
    activated = jax.nn.gelu(preact).astype(jnp.bfloat16)
    partial_out = jnp.einsum(down_form, activated, down_full, preferred_element_type=jnp.float32)
    expert_flat = narrow_sums(partial_out).reshape(CAP * EXPERTS, feature_count)
    mixed = (resid + jnp.sum(gates[:, :, None] * expert_flat[slot_ids], axis=1)).astype(
        jnp.bfloat16
    )
    cotangent = grad_out.astype(jnp.float32)
    gate_pad = jnp.concatenate([gates.reshape(-1), jnp.zeros((1,), jnp.float32)], axis=0)
    cot_pad = jnp.concatenate([cotangent, jnp.zeros((1, feature_count), jnp.float32)], axis=0)
    grad_disp = (
        (gate_pad[sources][:, None] * cot_pad[owner_rows])
        .astype(jnp.bfloat16)
        .reshape(CAP, EXPERTS, feature_count)
    )
    grad_slots = narrow_rows(grad_disp)
    grad_activated = jnp.einsum(
        back_form, grad_slots, down_full, preferred_element_type=jnp.float32
    )
    gelu_back = jax.vjp(jax.nn.gelu, preact)[1]
    grad_preact = gelu_back(grad_activated)[0].astype(jnp.bfloat16)
    grad_down = jnp.einsum(
        grad_down_form, activated, grad_slots, preferred_element_type=jnp.float32
    )
    grad_in = jnp.einsum(
        "ced,cef->edf", gathered_slots, grad_preact, preferred_element_type=jnp.float32
    )
    grad_partial = jnp.einsum(
        "cef,edf->ced", grad_preact, in_full, preferred_element_type=jnp.float32
    )
    grad_slot_rows = narrow_sums(grad_partial).reshape(CAP * EXPERTS, feature_count)
    grad_normed_two = jnp.sum(grad_slot_rows[slot_ids], axis=1)
    norm_two_back = jax.vjp(normalize, resid, ln2_gain, ln2_bias)[1]
    grad_resid_norm, grad_gain_two, grad_bias_two = norm_two_back(grad_normed_two)
    grad_resid = cotangent + grad_resid_norm
    grad_branch = grad_resid.astype(jnp.bfloat16)
    grad_branch_rows = narrow_rows(grad_branch)
    grad_out_weight = jnp.dot(attended.T, grad_branch_rows, preferred_element_type=jnp.float32)
    grad_att = jnp.dot(grad_branch_rows, out_full.T, preferred_element_type=jnp.float32).astype(
        jnp.bfloat16
    )
    grad_proj = attention_backward(
        projected[0], projected[1], projected[2], grad_att, log_total, head_count
    )
    grad_qkv_weight = jnp.einsum(
        "rd,jrc->jdc", att_rows, grad_proj, preferred_element_type=jnp.float32
    )
    grad_normed_part = jnp.einsum(
        "jrc,jdc->rd", grad_proj, qkv_full, preferred_element_type=jnp.float32
    )
    grad_normed = narrow_sums(grad_normed_part)
    norm_one_back = jax.vjp(normalize, stream, ln1_gain, ln1_bias)[1]
    grad_stream_norm, grad_gain_one, grad_bias_one = norm_one_back(grad_normed)
    grad_input = grad_resid + grad_stream_norm
    grad_in_block, grad_down_block = (
        lax.psum_scatter(
            grad_in.astype(jnp.bfloat16), "wide", scatter_dimension=1, tiled=True
        ).astype(jnp.float32),
        lax.psum_scatter(
            grad_down.astype(jnp.bfloat16), "wide", scatter_dimension=2, tiled=True
        ).astype(jnp.float32),
    )
    grad_qkv_block, grad_out_block = (
        lax.psum_scatter(
            grad_qkv_weight.astype(jnp.bfloat16), "wide", scatter_dimension=1, tiled=True
        ).astype(jnp.float32),
        lax.psum_scatter(
            grad_out_weight.astype(jnp.bfloat16), "wide", scatter_dimension=1, tiled=True
        ).astype(jnp.float32),
    )
    block_grads = (
        lax.psum(grad_qkv_block.astype(jnp.bfloat16), "dp").astype(jnp.float32),
        lax.psum(grad_out_block.astype(jnp.bfloat16), "dp").astype(jnp.float32),
        lax.psum(grad_in_block.astype(jnp.bfloat16), "dp").astype(jnp.float32),
        lax.psum(grad_down_block.astype(jnp.bfloat16), "dp").astype(jnp.float32),
    )
    norm_totals = lax.psum(
        (grad_gain_one, grad_bias_one, grad_gain_two, grad_bias_two), ("dp", "wide", "narrow")
    )
    return (
        mixed,
        grad_input,
        norm_totals[0],
        norm_totals[1],
        norm_totals[2],
        norm_totals[3],
        block_grads[0],
        block_grads[1],
        block_grads[2],
        block_grads[3],
    )


def solution(mesh):
    planes, wide, narrow = (mesh.shape[name] for name in ("dp", "wide", "narrow"))
    plane = wide * narrow
    if planes == 4 and EXPERTS % (2 * plane) == 0 and plane & (plane - 1) == 0 and narrow % 2 == 0:
        sizes = (planes // 2, 2, wide, narrow)
        split = Mesh(mesh.devices.reshape(sizes), ("pair", "parity", "wide", "narrow"))
        return placed(
            functools.partial(owned_on_device, (planes // 2, wide, narrow)),
            split,
            ("pair", "parity", "wide", "narrow"),
        )
    return placed(on_device, mesh, ("dp", "wide", "narrow"))


def placed(function, mesh, row_axes):
    rows = P(row_axes, None)
    specs_in = (
        rows,
        rows,
        rows,
        rows,
        P(),
        P(),
        P(),
        P(),
        P(None, "wide", "narrow"),
        P("narrow", "wide"),
        P(None, "wide", "narrow"),
        P(None, "narrow", "wide"),
    )
    specs_out = (
        rows,
        rows,
        P(),
        P(),
        P(),
        P(),
        P(None, "wide", "narrow"),
        P("narrow", "wide"),
        P(None, "wide", "narrow"),
        P(None, "narrow", "wide"),
    )
    return jax.shard_map(
        function, mesh=mesh, in_specs=specs_in, out_specs=specs_out, check_vma=False
    )
```

```python
import functools
import math

import jax
import jax.numpy as jnp
from jax import lax
from jax.experimental import pallas as pl
from jax.experimental.pallas import tpu as pltpu
from jax.sharding import Mesh, PartitionSpec as P

HEAD_DIM = 64
EXPERTS = 32
TOP = 2
SEQ = 197
IMG_STEP = 4
CAP = 66

norm_eps = 1e-06

f32 = jnp.float32
bf16 = jnp.bfloat16


SLOTS = -(-CAP // 8) * 8
IMG_ROWS = -(-SEQ // 16) * 16
LANES = 128
TAIL = 16
VMEM_LIMIT = 56 * 1024 * 1024


def dot(a, b):
    return lax.dot_general(a, b, (((1,), (0,)), ((), ())), preferred_element_type=f32)


def dot_bt(a, b):
    return lax.dot_general(a, b, (((1,), (1,)), ((), ())), preferred_element_type=f32)


def dot_at(a, b):
    return lax.dot_general(a, b, (((0,), (0,)), ((), ())), preferred_element_type=f32)


def norm_parts(values):
    average = jnp.mean(values, axis=-1, keepdims=True)
    centered = values - average
    scale = lax.rsqrt(jnp.mean(centered * centered, axis=-1, keepdims=True) + norm_eps)
    return centered * scale, scale


def norm_back(hat, scale, gain, grad):
    t = grad * gain
    return scale * (
        t
        - jnp.mean(t, axis=-1, keepdims=True)
        - hat * jnp.mean(t * hat, axis=-1, keepdims=True)
    )


def full_spec(shape):
    zeros = (0,) * len(shape)
    return pl.BlockSpec(shape, lambda *_: zeros)


def image_spec(shape):
    rest = (0,) * (len(shape) - 1)
    return pl.BlockSpec((1,) + shape[1:], lambda i: (i,) + rest)


def back_rows(slot_ref, k, group, wide, offset):
    first = TOP + k if wide else k
    here = slot_ref[0, :, 2 * TOP + k : 2 * TOP + k + 1] == group
    return jnp.where(here, slot_ref[0, :, first : first + 1] + offset, -1)


def one_hot(mask):
    return mask.astype(f32).astype(bf16)


def route_kernel(plane, own_ref, routes_ref, routes_t_ref, back_ref, slot_t_ref):
    rows = routes_ref.shape[0]
    quarters = EXPERTS // plane
    groups = quarters // 2
    before = lax.broadcasted_iota(jnp.int32, (rows, rows), 0)
    after = lax.broadcasted_iota(jnp.int32, (rows, rows), 1)
    ids_t = lax.broadcasted_iota(jnp.int32, (EXPERTS, rows), 0)
    ids = lax.broadcasted_iota(jnp.int32, (rows, EXPERTS), 1)
    hot_t = [(ids_t == routes_t_ref[k : k + 1, :]).astype(f32) for k in range(TOP)]
    hot = [(ids == routes_ref[:, k : k + 1]).astype(f32) for k in range(TOP)]
    count_t = dot(sum(hot_t).astype(bf16), one_hot(before < after))
    count = dot(one_hot(after < before), sum(hot).astype(bf16))

    def place_of(ids):
        group, parity = ids // (2 * plane), ids // plane % 2
        return ids % plane, jnp.where(parity == own_ref[0], group, groups + group)

    for k in range(TOP):
        rank_t = jnp.sum(hot_t[k] * count_t, axis=0, keepdims=True).astype(jnp.int32)
        place, q = place_of(routes_t_ref[k : k + 1, :])
        slot_t_ref[k : k + 1, :] = (place * quarters + q) * SLOTS + rank_t
        rank = jnp.sum(hot[k] * count, axis=1, keepdims=True).astype(jnp.int32)
        chosen = routes_ref[:, k : k + 1]
        item = chosen % (2 * plane)
        back_ref[:, k : k + 1] = item * SLOTS + rank
        back_ref[:, TOP + k : TOP + k + 1] = item * 2 * SLOTS + rank
        back_ref[:, 2 * TOP + k : 2 * TOP + k + 1] = chosen // (2 * plane)


def route(own, routes, plane):
    rows = routes.shape[0]
    return pl.pallas_call(
        functools.partial(route_kernel, plane),
        in_specs=[pl.BlockSpec(memory_space=pltpu.SMEM)] + [pl.BlockSpec(memory_space=pltpu.VMEM)] * 2,
        out_shape=[
            jax.ShapeDtypeStruct((rows, 3 * TOP), jnp.int32),
            jax.ShapeDtypeStruct((TOP, rows), jnp.int32),
        ],
        compiler_params=pltpu.CompilerParams(vmem_limit_bytes=VMEM_LIMIT),
        cost_estimate=pl.CostEstimate(flops=60_000_000, bytes_accessed=100_000, transcendentals=0),
        name="route",
    )(own, routes, routes.T)


def grad_slots_kernel(plane, group, own_ref, sent_ref, gd_ref):
    rows = sent_ref.shape[1] - 2 * HEADER
    features = sent_ref.shape[2]
    header = jnp.concatenate(
        [sent_ref[0, i * HEADER : (i + 1) * HEADER, :].astype(f32) for i in range(2)], axis=1
    )[:, :rows]
    before = lax.broadcasted_iota(jnp.int32, (rows, rows), 0)
    after = lax.broadcasted_iota(jnp.int32, (rows, rows), 1)
    ids_t = lax.broadcasted_iota(jnp.int32, (EXPERTS, rows), 0)
    routes = [header[k : k + 1, :].astype(jnp.int32) for k in range(TOP)]
    gates = [
        (header[2 + k : 3 + k, :] + header[4 + k : 5 + k, :]) + header[6 + k : 7 + k, :]
        for k in range(TOP)
    ]
    hot = [(ids_t == routes[k]).astype(f32) for k in range(TOP)]
    count = dot(sum(hot).astype(bf16), one_hot(before < after))
    per = plane * SLOTS
    place = lax.broadcasted_iota(jnp.int32, (per, rows), 0)
    here = []
    for k in range(TOP):
        rank = jnp.sum(hot[k] * count, axis=0, keepdims=True).astype(jnp.int32)
        mine = routes[k] // plane == 2 * group + own_ref[0]
        here.append(place == jnp.where(mine, routes[k] % plane * SLOTS + rank, -1))
    gate = sum(jnp.where(here[k], gates[k], 0.0) for k in range(TOP))
    picked = dot(one_hot(here[0] | here[1]), sent_ref[0, 2 * HEADER :, :])
    weighed = jnp.sum(gate, axis=1, keepdims=True) * picked
    for p in range(plane):
        gd_ref[p, 0] = weighed[p * SLOTS : (p + 1) * SLOTS, :].astype(bf16)


HEADER = 8


def with_header(routes, gates, cot):
    rows, features = cot.shape
    high = lax.reduce_precision(gates, 8, 7)
    middle = lax.reduce_precision(gates - high, 8, 7)
    low = (gates - high) - middle
    lines = jnp.concatenate([v.T for v in (routes.astype(f32), high, middle, low)], axis=0)
    lines = jnp.pad(lines, ((0, 0), (0, 2 * features - rows))).astype(bf16)
    return jnp.concatenate([lines[:, :features], lines[:, features:], cot], axis=0)


def grad_slots(own, sent, plane, group):
    chunks, rows, features = sent.shape
    shape = (plane, chunks, SLOTS, features)
    return pl.pallas_call(
        functools.partial(grad_slots_kernel, plane, group),
        grid_spec=pltpu.PrefetchScalarGridSpec(
            num_scalar_prefetch=1,
            grid=(chunks,),
            in_specs=[pl.BlockSpec((1, rows, features), lambda i, own: (own[1] ^ i, 0, 0))],
            out_specs=pl.BlockSpec((plane, 1, SLOTS, features), lambda i, own: (0, i, 0, 0)),
        ),
        out_shape=jax.ShapeDtypeStruct(shape, bf16),
        compiler_params=pltpu.CompilerParams(vmem_limit_bytes=VMEM_LIMIT),
        cost_estimate=pl.CostEstimate(flops=8_000_000_000, bytes_accessed=10_000_000, transcendentals=0),
        name="grad_slots",
    )(own, sent)


def unpack_weights(wide, narrow, spot_ref, weights_refs, qkv_scratch, out_scratch):
    deep, across = qkv_scratch.shape[1] // wide, LANES
    for k in range(wide * narrow):
        block_ref = weights_refs[k % 2].at[k // 2]
        x = spot_ref[0] ^ (k // narrow)
        n = spot_ref[1] ^ (k % narrow)
        x_at = pl.multiple_of(x * deep, deep)
        n_at = pl.multiple_of(n * across, across)
        for j in range(3):
            qkv_scratch[j, pl.ds(x_at, deep), pl.ds(n_at, across)] = block_ref[
                j * deep : (j + 1) * deep, :
            ]
        for c in range(deep // LANES):
            first = 3 * deep + c * across
            out_scratch[
                pl.ds(n_at, across), pl.ds(pl.multiple_of(x_at + c * LANES, LANES), LANES)
            ] = block_ref[first : first + across, :]


def head_masks():
    lane = lax.broadcasted_iota(jnp.int32, (1, LANES), 1)
    per = LANES // HEAD_DIM
    return [(lane // HEAD_DIM) == h for h in range(per)]


def masked(value, mask):
    return jnp.where(mask, value, jnp.zeros_like(value))


def forward_kernel(
    wide,
    narrow,
    tile,
    spot_ref,
    tokens_ref,
    norms_ref,
    weights_a_ref,
    weights_b_ref,
    slot_t_ref,
    proj_ref,
    att_ref,
    resid_ref,
    x_ref,
    qkv_w,
    out_w,
    norm_scratch,
):
    step = pl.program_id(0)
    features = tokens_ref.shape[2]

    @pl.when(step == 0)
    def _():
        unpack_weights(wide, narrow, spot_ref, (weights_a_ref, weights_b_ref), qkv_w, out_w)
        norm_scratch[...] = jnp.zeros_like(norm_scratch)

    stream = tokens_ref[0].astype(f32)
    hat, _ = norm_parts(stream)
    normed = (hat * norms_ref[0:1, :] + norms_ref[1:2, :]).astype(bf16)
    proj = [dot(normed, qkv_w[j]).astype(bf16) for j in range(3)]
    for j in range(3):
        proj_ref[0, :, j * features : (j + 1) * features] = proj[j]
    masks = head_masks()
    scale = HEAD_DIM ** (-0.5)
    pieces = []
    for pair in range(features // LANES):
        cols = slice(pair * LANES, (pair + 1) * LANES)
        q, k, v = proj[0][:, cols], proj[1][:, cols], proj[2][:, cols]
        total = None
        for mask in masks:
            scores = dot_bt(masked(q, mask), k) * scale
            weights = jnp.exp(scores - jnp.max(scores, axis=-1, keepdims=True))
            probs = weights / jnp.sum(weights, axis=-1, keepdims=True)
            one = dot(probs.astype(bf16), masked(v, mask))
            total = one if total is None else total + one
        pieces.append(total.astype(bf16))
    attended = jnp.concatenate(pieces, axis=1)
    att_ref[0] = attended
    resid = stream + dot(attended, out_w[...])
    resid_ref[0] = resid
    hat_two, _ = norm_parts(resid)
    norm_scratch[step, : stream.shape[0], :] = (
        hat_two * norms_ref[2:3, :] + norms_ref[3:4, :]
    ).astype(bf16)

    @pl.when(step == pl.num_programs(0) - 1)
    def _():
        count = slot_t_ref.shape[1]
        rows = norm_scratch[...].reshape(count, features)
        for start in range(0, x_ref.shape[0], tile):
            place = lax.broadcasted_iota(jnp.int32, (tile, count), 0) + start
            here = (place == slot_t_ref[0:1, :]) | (place == slot_t_ref[1:2, :])
            x_ref[start : start + tile, :] = dot(one_hot(here), rows).astype(bf16)


def attention_and_slots(spot, tokens, norms, weights, slot_t, wide, narrow):
    images, rows, features = tokens.shape
    total = EXPERTS * SLOTS
    tile = 384 if total % 384 == 0 else SLOTS * wide * narrow
    per_image = [(images, rows, 3 * features), (images, rows, features), (images, rows, features)]
    return pl.pallas_call(
        functools.partial(forward_kernel, wide, narrow, tile),
        grid=(images,),
        in_specs=[
            pl.BlockSpec(memory_space=pltpu.SMEM),
            image_spec(tokens.shape),
            full_spec(norms.shape),
            full_spec(weights[0].shape),
            full_spec(weights[1].shape),
            full_spec(slot_t.shape),
        ],
        out_specs=[image_spec(s) for s in per_image] + [full_spec((total, features))],
        out_shape=[
            jax.ShapeDtypeStruct(per_image[0], bf16),
            jax.ShapeDtypeStruct(per_image[1], bf16),
            jax.ShapeDtypeStruct(per_image[2], f32),
            jax.ShapeDtypeStruct((total, features), bf16),
        ],
        scratch_shapes=[
            pltpu.VMEM((3, features, features), bf16),
            pltpu.VMEM((features, features), bf16),
            pltpu.VMEM((images, IMG_ROWS, features), bf16),
        ],
        compiler_params=pltpu.CompilerParams(vmem_limit_bytes=VMEM_LIMIT),
        cost_estimate=pl.CostEstimate(flops=6_000_000_000, bytes_accessed=9_000_000, transcendentals=2_000_000),
        name="attention_forward",
    )(spot, tokens, norms, *weights, slot_t)


def pack_kernel(first_ref, w_in_ref, w_out_ref, *out_refs):
    deep, hidden = w_in_ref.shape[1], w_in_ref.shape[2]
    base = deep * (hidden // LANES) if len(out_refs) == 1 else 0
    for c in range(hidden // LANES):
        out_refs[0][0, c * deep : (c + 1) * deep, :] = w_in_ref[0, :, c * LANES : (c + 1) * LANES]
    for c in range(deep // LANES):
        out_refs[-1][0, base + c * hidden : base + (c + 1) * hidden, :] = w_out_ref[
            0, :, c * LANES : (c + 1) * LANES
        ]


def pack(first, w_in, w_out, plane, arrays):
    deep, hidden = w_in.shape[1], w_in.shape[2]
    rows = 2 * deep * hidden // LANES // arrays
    at = lambda i, first: (first[0] + i, 0, 0)
    return pl.pallas_call(
        pack_kernel,
        grid_spec=pltpu.PrefetchScalarGridSpec(
            num_scalar_prefetch=1,
            grid=(plane,),
            in_specs=[pl.BlockSpec((1, deep, hidden), at), pl.BlockSpec((1, hidden, deep), at)],
            out_specs=[pl.BlockSpec((1, rows, LANES), lambda i, first: (i, 0, 0))] * arrays,
        ),
        out_shape=[jax.ShapeDtypeStruct((plane, rows, LANES), bf16)] * arrays,
        cost_estimate=pl.CostEstimate(flops=0, bytes_accessed=9_000_000, transcendentals=0),
        name="pack_weights",
    )(first, w_in, w_out)


GELU_A = math.sqrt(2.0 / math.pi)
GELU_B = 0.044715 * GELU_A


def gelu_pair(u):
    u2 = u * u
    p = GELU_B * u2 + GELU_A
    half = 0.5 * jnp.tanh(u * p) + 0.5
    slope = half + (u * (6.0 * p - 4.0 * GELU_A)) * (half - half * half)
    return u * half, slope


def identity(size):
    a = lax.broadcasted_iota(jnp.int32, (size, size), 0)
    b = lax.broadcasted_iota(jnp.int32, (size, size), 1)
    return (a == b).astype(f32).astype(bf16)


def expert_kernel(deep, hidden, parts, tile, where_ref, *refs):
    x_refs, (gd_ref, wi_ref, wo_ref, gi_ref, go_ref) = refs[:parts], refs[parts : parts + 5]
    gx_ref, y_ref = refs[parts + 5 : parts + 7]
    (x_s, gd_s, act, gp, wi_s, wo_s, y_acc, gx_acc, sem) = refs[parts + 7 :]
    step = pl.program_id(0)
    wide = wi_ref.shape[0]
    rows, features = x_s.shape
    own_rows = rows // 2
    chunk = own_rows // 2

    @pl.when(step == 0)
    def _():
        copies = [pltpu.make_async_copy(gd_ref, gd_s, sem.at[parts])]
        first = 0
        for i, x_ref in enumerate(x_refs):
            part = x_ref if len(x_ref.shape) == 2 else x_ref.at[where_ref[0]]
            count = part.shape[0]
            copies.append(pltpu.make_async_copy(part, x_s.at[pl.ds(first, count), :], sem.at[i]))
            first += count
        for copy in copies:
            copy.start()
        y_acc[...] = jnp.zeros_like(y_acc)
        gx_acc[...] = jnp.zeros_like(gx_acc)
        for copy in copies:
            copy.wait()


    for x in range(wide):
        for c in range(hidden // LANES):
            wi_s[x * deep : (x + 1) * deep, c * LANES : (c + 1) * LANES] = wi_ref[
                x, 0, c * deep : (c + 1) * deep, :
            ]
        for c in range(deep // LANES):
            first = x * deep + c * LANES
            wo_s[:, first : first + LANES] = wo_ref[x, 0, c * hidden : (c + 1) * hidden, :]

    for t in range(rows // tile):
        at = slice(t * tile, (t + 1) * tile)
        value, slope = gelu_pair(dot(x_s[at, :], wi_s[...]))
        value = value.astype(bf16)
        act[at, :] = value
        back = (dot_bt(gd_s[at, :], wo_s[...]) * slope).astype(bf16)
        gp[at, :] = back
        if t < own_rows // tile:
            y_acc[at, :] += dot(value, wo_s[...])
            gx_acc[at, :] += dot_bt(back, wi_s[...])
    gin = dot_at(x_s[...], gp[...]).astype(bf16)
    for x in range(wide):
        for c in range(hidden // LANES):
            gi_ref[x, 0, c * deep : (c + 1) * deep, :] = gin[
                x * deep : (x + 1) * deep, c * LANES : (c + 1) * LANES
            ]
    gout = dot_at(act[...], gd_s[...]).astype(bf16)
    for x in range(wide):
        for c in range(deep // LANES):
            first = x * deep + c * LANES
            go_ref[x, 0, c * hidden : (c + 1) * hidden, :] = gout[:, first : first + LANES]

    @pl.when(step == pl.num_programs(0) - 1)
    def _():
        for i in range(2):
            at = slice(i * chunk, (i + 1) * chunk)
            to = pl.ds(pl.multiple_of((where_ref[1] ^ i) * chunk, chunk), chunk)
            gx_ref[to, :] = gx_acc[at, :].astype(bf16)
            y_ref[to, :] = y_acc[at, :].astype(bf16)


def expert(where, xs, gd, weights, wide, narrow, deep, hidden):
    rows, features = gd.shape
    own_rows = rows // 2
    chunk = own_rows // 2
    packed = deep * hidden // LANES
    last = len(weights) - 1
    tile = 384 if own_rows % 384 == 0 else SLOTS * 2
    anywhere = pl.BlockSpec(memory_space=pl.ANY)
    whole = lambda shape: pl.BlockSpec(shape, lambda s: (0,) * len(shape))
    per_step = pl.BlockSpec((wide, 1, packed, LANES), lambda s: (0, s, 0, 0))
    blocks = (wide, narrow, packed, LANES)
    g_in, g_out, gx, y = pl.pallas_call(
        functools.partial(expert_kernel, deep, hidden, len(xs), tile),
        grid=(narrow,),
        in_specs=[pl.BlockSpec(memory_space=pltpu.SMEM)] + [anywhere] * (len(xs) + 1)
        + [per_step, pl.BlockSpec((wide, 1, packed, LANES), lambda s: (0, s, 1 - last, 0))],
        out_specs=[per_step] * 2 + [whole((own_rows, features))] * 2,
        scratch_shapes=[
            pltpu.VMEM((rows, features), bf16),
            pltpu.VMEM((rows, features), bf16),
            pltpu.VMEM((rows, hidden), bf16),
            pltpu.VMEM((rows, hidden), bf16),
            pltpu.VMEM((features, hidden), bf16),
            pltpu.VMEM((hidden, features), bf16),
            pltpu.VMEM((own_rows, features), f32),
            pltpu.VMEM((own_rows, features), f32),
            pltpu.SemaphoreType.DMA((len(xs) + 1,)),
        ],
        out_shape=[
            jax.ShapeDtypeStruct(blocks, bf16),
            jax.ShapeDtypeStruct(blocks, bf16),
        ]
        + [jax.ShapeDtypeStruct((own_rows, features), bf16)] * 2,
        compiler_params=pltpu.CompilerParams(vmem_limit_bytes=VMEM_LIMIT),
        cost_estimate=pl.CostEstimate(
            flops=2 * narrow * features * hidden * (4 * rows + 2 * own_rows),
            bytes_accessed=20_000_000,
            transcendentals=rows * hidden * narrow,
        ),
        name="expert",
    )(where, *xs, gd, *[w.reshape((wide, narrow) + w.shape[1:]) for w in (weights[0], weights[last])])
    return [g.reshape(wide * narrow, packed, LANES) for g in (g_in, g_out)], gx, y


def place_kernel(where_ref, g_ref, *refs):
    out_ref = refs[-1]
    rows = out_ref.shape[1]
    for i in range(out_ref.shape[0]):
        for c in range(out_ref.shape[2] // LANES):
            out_ref[i, :, c * LANES : (c + 1) * LANES] = g_ref[
                0, i, c * rows : (c + 1) * rows, :
            ].astype(f32)


def place(where, g, so_far, rows, columns):
    g = g.reshape((-1,) + g.shape[-3:])
    parts, plane, packed, _ = g.shape
    each = math.gcd(plane, 4)
    anywhere = pl.BlockSpec(memory_space=pl.ANY)
    part = (lambda where: where[0]) if parts > 1 else (lambda where: 0)
    return pl.pallas_call(
        place_kernel,
        grid_spec=pltpu.PrefetchScalarGridSpec(
            num_scalar_prefetch=1,
            grid=(plane // each,),
            in_specs=[pl.BlockSpec((1, each, packed, LANES), lambda i, where: (part(where), i, 0, 0))]
            + [anywhere] * len(so_far),
            out_specs=pl.BlockSpec(
                (each, rows, columns), lambda i, where: (where[1] // each + i, 0, 0)
            ),
        ),
        out_shape=jax.ShapeDtypeStruct((EXPERTS, rows, columns), f32),
        input_output_aliases={2 + i: i for i in range(len(so_far))},
        compiler_params=pltpu.CompilerParams(vmem_limit_bytes=VMEM_LIMIT),
        cost_estimate=pl.CostEstimate(flops=0, bytes_accessed=6_000_000, transcendentals=0),
        name="place_grads",
    )(where, g, *so_far)


def mixed_kernel(resid_ref, slot_ref, gates_ref, *rest):
    back_refs, mixed_ref = rest[:-1], rest[-1]
    total = resid_ref[0]
    rows = total.shape[0]
    for k in range(TOP):
        picked = None
        for g, back_ref in enumerate(back_refs):
            wide = g < len(back_refs) - 1
            place = lax.broadcasted_iota(jnp.int32, (rows, back_ref.shape[0]), 1)
            here = place == back_rows(slot_ref, k, g, wide, SLOTS if wide else 0)
            one = dot(one_hot(here), back_ref[...])
            picked = one if picked is None else picked + one
        total = total + gates_ref[0, :, k : k + 1] * picked
    mixed_ref[0] = total.astype(bf16)


def mix(resid, slots, gates, backs):
    return pl.pallas_call(
        mixed_kernel,
        grid=(resid.shape[0],),
        in_specs=[image_spec(resid.shape), image_spec(slots.shape), image_spec(gates.shape)]
        + [full_spec(y.shape) for y in backs],
        out_specs=image_spec(resid.shape),
        out_shape=jax.ShapeDtypeStruct(resid.shape, bf16),
        compiler_params=pltpu.CompilerParams(vmem_limit_bytes=VMEM_LIMIT),
        cost_estimate=pl.CostEstimate(flops=6_000_000_000, bytes_accessed=6_000_000, transcendentals=0),
        name="mix",
    )(resid, slots, gates, *backs)


def backward_kernel(wide, narrow, parts, *refs):
    (spot_ref, tokens_ref, cot_ref, norms_ref, weights_a_ref, weights_b_ref) = refs[:6]
    (slot_ref, proj_ref, att_ref, resid_ref) = refs[6:10]
    back_refs = refs[10 : 10 + parts]
    (grad_ref, grads_w_ref) = refs[10 + parts : 12 + parts]
    (qkv_w, out_w, normed_s, att_s, branch_s, proj_s, grads_n_ref) = refs[12 + parts :]
    step = pl.program_id(0)
    rows, features = tokens_ref.shape[1], tokens_ref.shape[2]

    @pl.when(step == 0)
    def _():
        unpack_weights(wide, narrow, spot_ref, (weights_a_ref, weights_b_ref), qkv_w, out_w)
        normed_s[...] = jnp.zeros_like(normed_s)
        att_s[...] = jnp.zeros_like(att_s)
        branch_s[...] = jnp.zeros_like(branch_s)
        proj_s[...] = jnp.zeros_like(proj_s)
        grads_n_ref[...] = jnp.zeros_like(grads_n_ref)

    grad_normed = None
    for g, back_ref in enumerate(back_refs):
        place = lax.broadcasted_iota(jnp.int32, (rows, back_ref.shape[0]), 1)
        own = [back_rows(slot_ref, k, g, g < parts - 1, 0) for k in range(TOP)]
        here = (place == own[0]) | (place == own[1])
        one = dot(one_hot(here), back_ref[...])
        grad_normed = one if grad_normed is None else grad_normed + one
    hat_two, scale_two = norm_parts(resid_ref[0])
    grads_n_ref[2:3, :] += jnp.sum(grad_normed * hat_two, axis=0, keepdims=True)
    grads_n_ref[3:4, :] += jnp.sum(grad_normed, axis=0, keepdims=True)
    grad_resid = cot_ref[0].astype(f32) + norm_back(
        hat_two, scale_two, norms_ref[2:3, :], grad_normed
    )
    branch = grad_resid.astype(bf16)
    branch_s[step, :rows, :] = branch
    att_s[step, :rows, :] = att_ref[0]
    grad_att = dot_bt(branch, out_w[...]).astype(bf16)

    masks = head_masks()
    scale = HEAD_DIM ** (-0.5)
    pairs = features // LANES
    pieces = [[None] * pairs for _ in range(3)]
    for pair in range(pairs):
        at = [j * features + pair * LANES for j in range(3)]
        q, k, v = [proj_ref[0, :, a : a + LANES] for a in at]
        ga = grad_att[:, pair * LANES : (pair + 1) * LANES]
        sums = [None] * 3
        for mask in masks:
            scores = dot_bt(masked(k, mask), q) * scale
            weights = jnp.exp(scores - jnp.max(scores, axis=0, keepdims=True))
            probs = weights / jnp.sum(weights, axis=0, keepdims=True)
            ga_h = masked(ga, mask)
            dprobs = dot_bt(v, ga_h)
            inner = jnp.sum(probs * dprobs, axis=0, keepdims=True)
            grad_scores = (probs * (dprobs - inner)).astype(bf16)
            parts_h = (
                dot_at(grad_scores, masked(k, mask)),
                dot(grad_scores, masked(q, mask)),
                dot(probs.astype(bf16), ga_h),
            )
            for j in range(3):
                sums[j] = parts_h[j] if sums[j] is None else sums[j] + parts_h[j]
        pieces[0][pair] = (sums[0] * scale).astype(bf16)
        pieces[1][pair] = (sums[1] * scale).astype(bf16)
        pieces[2][pair] = sums[2].astype(bf16)

    stream = tokens_ref[0].astype(f32)
    hat, scale_one = norm_parts(stream)
    normed_s[step, :rows, :] = (hat * norms_ref[0:1, :] + norms_ref[1:2, :]).astype(bf16)
    grad_first = None
    for j in range(3):
        grad_proj = jnp.concatenate(pieces[j], axis=1)
        proj_s[j, step, :rows, :] = grad_proj
        one = dot_bt(grad_proj, qkv_w[j])
        grad_first = one if grad_first is None else grad_first + one
    grads_n_ref[0:1, :] += jnp.sum(grad_first * hat, axis=0, keepdims=True)
    grads_n_ref[1:2, :] += jnp.sum(grad_first, axis=0, keepdims=True)
    grad_ref[0] = grad_resid + norm_back(hat, scale_one, norms_ref[0:1, :], grad_first)

    @pl.when(step == pl.num_programs(0) - 1)
    def _():
        count = normed_s.shape[0] * normed_s.shape[1]
        deep = features // wide
        flat = lambda value: value.reshape(count, features)
        normed_t = flat(normed_s[...])
        for j in range(3):
            grad = dot_at(normed_t, flat(proj_s[j])).astype(bf16)
            for x in range(wide):
                for n in range(narrow):
                    grads_w_ref[x * narrow + n, j * deep : (j + 1) * deep, :] = grad[
                        x * deep : (x + 1) * deep, n * LANES : (n + 1) * LANES
                    ]
        per = features // LANES
        tail = jnp.concatenate(
            [
                grads_n_ref[i : i + 1, c * LANES : (c + 1) * LANES]
                for i in range(4)
                for c in range(per)
            ],
            axis=0,
        )
        high = tail.astype(bf16)
        both = jnp.concatenate([high, (tail - high.astype(f32)).astype(bf16)], axis=0)
        for d in range(wide * narrow):
            grads_w_ref[d, grads_w_ref.shape[1] - 2 * TAIL :, :] = both
        grad = dot_at(flat(att_s[...]), flat(branch_s[...])).astype(bf16)
        for x in range(wide):
            for n in range(narrow):
                for c in range(deep // LANES):
                    first = 3 * deep + c * LANES
                    grads_w_ref[x * narrow + n, first : first + LANES, :] = grad[
                        n * LANES : (n + 1) * LANES,
                        x * deep + c * LANES : x * deep + (c + 1) * LANES,
                    ]


def attention_back(spot, tokens, cot, norms, weights, slots, proj, att, resid, backs, wide, narrow):
    images, rows, features = tokens.shape
    stash = (images, IMG_ROWS, features)
    small = (wide * narrow, weights[0].shape[1] + 2 * TAIL, LANES)
    return pl.pallas_call(
        functools.partial(backward_kernel, wide, narrow, len(backs)),
        grid=(images,),
        in_specs=[
            pl.BlockSpec(memory_space=pltpu.SMEM),
            image_spec(tokens.shape),
            image_spec(cot.shape),
            full_spec(norms.shape),
            full_spec(weights[0].shape),
            full_spec(weights[1].shape),
            image_spec(slots.shape),
            image_spec(proj.shape),
            image_spec(att.shape),
            image_spec(resid.shape),
        ]
        + [full_spec(back.shape) for back in backs],
        out_specs=[image_spec(tokens.shape), full_spec(small)],
        out_shape=[
            jax.ShapeDtypeStruct(tokens.shape, f32),
            jax.ShapeDtypeStruct(small, bf16),
        ],
        scratch_shapes=[
            pltpu.VMEM((3, features, features), bf16),
            pltpu.VMEM((features, features), bf16),
            pltpu.VMEM(stash, bf16),
            pltpu.VMEM(stash, bf16),
            pltpu.VMEM(stash, bf16),
            pltpu.VMEM((3,) + stash, bf16),
            pltpu.VMEM((4, features), f32),
        ],
        compiler_params=pltpu.CompilerParams(vmem_limit_bytes=VMEM_LIMIT),
        cost_estimate=pl.CostEstimate(flops=9_000_000_000, bytes_accessed=12_000_000, transcendentals=2_000_000),
        name="attention_backward",
    )(spot, tokens, cot, norms, *weights, slots, proj, att, resid, *backs)


def owned_on_device(
    sizes,
    tokens,
    grad_out,
    gates,
    routes,
    ln1_gain,
    ln1_bias,
    ln2_gain,
    ln2_bias,
    w_qkv,
    w_attn_out,
    w_expert_in,
    w_expert_out,
):
    pairs, wide, narrow = sizes
    planes, plane = 2 * pairs, wide * narrow
    groups = EXPERTS // (2 * plane)
    rows, features = tokens.shape
    images = rows // SEQ
    qkv_deep = w_qkv.shape[1]
    deep, hidden = w_expert_in.shape[1], w_expert_in.shape[2]
    pair_index, parity = lax.axis_index("pair"), lax.axis_index("parity")
    x_index, n_index = lax.axis_index("wide"), lax.axis_index("narrow")
    own = parity.astype(jnp.int32).reshape(1)
    own_and_plane = jnp.stack([parity, 2 * pair_index + parity]).astype(jnp.int32)
    far_and_own = jnp.stack([1 - pair_index, parity]).astype(jnp.int32)
    spot = jnp.stack([x_index, n_index, x_index * narrow + n_index]).astype(jnp.int32)

    def in_plane(values):
        return lax.all_to_all(values, ("wide", "narrow"), 0, 0, tiled=True)

    def in_pair(values):
        return lax.all_to_all(values, ("parity", "wide", "narrow"), 0, 0, tiled=True)

    def across(values, k):
        return lax.ppermute(values, ("wide", "narrow"), [(i, i ^ k) for i in range(plane)])

    def along(values, k):
        return lax.ppermute(values, ("pair", "parity"), [(i, i ^ k) for i in range(planes)])

    def with_near(values):
        return lax.all_gather(values, "parity", axis=0)

    def after(values, first):
        return lax.optimization_barrier((values, first))[0]

    small = jnp.concatenate(
        [w_qkv.reshape(3 * qkv_deep, LANES)]
        + [w_attn_out[:, c * LANES : (c + 1) * LANES] for c in range(qkv_deep // LANES)],
        axis=0,
    )
    same_core = jnp.stack([small] + [across(small, k) for k in range(2, plane, 2)])
    weights = (same_core, across(same_core, 1))

    sent_all = lax.all_gather(with_header(routes, gates, grad_out), ("pair", "parity"), axis=0)

    back_slots, slot_t = route(own, routes, plane)
    packed = [
        pack(
            (g * 2 * plane + parity * plane).astype(jnp.int32).reshape(1),
            w_expert_in,
            w_expert_out,
            plane,
            1 if g else 2,
        )
        for g in range(groups)
    ]

    norms = jnp.stack([ln1_gain, ln1_bias, ln2_gain, ln2_bias])
    per_image = lambda values: values.reshape((images, SEQ) + values.shape[1:])
    slot_wide = jnp.pad(
        slot_t.reshape(TOP, images, SEQ), ((0, 0), (0, 0), (0, IMG_ROWS - SEQ)), constant_values=-1
    ).reshape(TOP, images * IMG_ROWS)
    tokens3, cot3, slots3, gates3 = map(per_image, (tokens, grad_out, back_slots, gates))
    proj, att, resid, x = attention_and_slots(
        spot, tokens3, norms, weights, slot_wide, wide, narrow
    )

    def quarter(moved, q):
        return moved[:, q * SLOTS : (q + 1) * SLOTS].reshape(plane * SLOTS, features)

    def by_plane(values):
        return jnp.moveaxis(values.reshape(plane, planes, SLOTS, features), 1, 0).reshape(
            planes * plane * SLOTS, features
        )

    gd_sent = [grad_slots(own_and_plane, sent_all, plane, g) for g in range(groups)]
    first_in = in_plane(packed[0][0])
    moved = in_plane(after(x, first_in).reshape(plane, -1, features))
    mine, other = quarter(moved, 0), quarter(moved, groups)
    nearest, far_mine = along(other, 1), along(mine, 2)
    first_out = in_plane(after(packed[0][1], (moved, gd_sent[0])))
    xs = [[mine, nearest, far_mine, along(other, 3)]]
    gd_parts = [v.reshape(plane, planes * SLOTS, features) for v in gd_sent]
    gds = [by_plane(in_plane(after(gd_parts[0], (first_out, nearest, far_mine, packed[1:]))))]
    nears = [
        jnp.concatenate([quarter(moved, g), along(quarter(moved, groups + g), 1)], axis=0)
        for g in range(1, groups)
    ]
    xs += [
        [near, lax.all_gather(after(near, xs[0]), "pair", axis=0)] for near in nears
    ]

    def to_tokens(parts, before):
        sent = jnp.concatenate([v.reshape(2 * plane, SLOTS, features) for v in parts], axis=1)
        return in_pair(after(sent, before)).reshape(-1, features)

    shapes = ((deep, hidden), (hidden, deep))
    out_blocks = [(), ()]

    def put(i, g, own_part, before):
        which = parity if own_part else 1 - parity
        where = jnp.stack([which, g * 2 * plane + which * plane]).astype(jnp.int32)
        part = after((grads if own_part else swaps)[g][i], before)
        out_blocks[i] = (place(where, part, out_blocks[i], *shapes[i]),)

    def after_blocks(values):
        values, out_blocks[:] = lax.optimization_barrier((values, out_blocks))
        return values

    held = (first_in, first_out)
    before = (gds[0], first_out, xs[0], nears)
    grads, swaps, gx_back, y_back = [], [], [], []
    last = groups - 1
    for g in range(groups):
        grad, gx, y = expert(far_and_own, xs[g], gds[g], held, wide, narrow, deep, hidden)
        grads.append([])
        swaps.append([])
        if g < last:
            held = tuple(in_plane(after(v, before)) for v in packed[g + 1])
            grads[g].append(in_plane(after(grad[0], held)))
            swaps[g].append(with_near(grads[g][0]))
            gds.append(by_plane(in_plane(after(gd_parts[g + 1], (grads[g][0], xs[g + 1])))))
            put(0, g, True, ())
            grads[g].append(in_plane(after_blocks(after(grad[1], gds[g + 1]))))
            swaps[g].append(with_near(grads[g][1]))
            gds[g + 1] = after(gds[g + 1], grads[g][1])
            before = to_tokens([gx, y], grads[g][1])
            y_back.append(before)
            gx_back.append(before)
        else:
            grads[g].append(in_plane(after(grad[0], before)))
            swaps[g].append(with_near(grads[g][0]))
            if g:
                put(1, g - 1, True, ())
                put(0, g - 1, False, ())
            before = to_tokens([after_blocks(gx)], grads[g][-1])
            gx_back.append(before)
            grads[g].append(in_plane(after(grad[1], before)))
            before = grads[g][1]
            last_y = y

    grad_input, grads_w = attention_back(
        spot, tokens3, cot3, norms, weights, slots3, proj, att, resid, gx_back, wide, narrow
    )
    count = grads_w.shape[1] - 2 * TAIL
    swaps[last].append(with_near(grads[last][1]))
    grads_w = in_plane(after(grads_w, before))
    y_back.append(to_tokens([last_y], grads_w))
    for g in range(last):
        put(1, g, False, ())
    put(0, last, True, ())
    put(1, last, True, ())
    put(0, last, False, ())
    mixed = mix(after_blocks(resid), slots3, gates3, y_back).reshape(rows, features)
    put(1, last, False, mixed)
    (out_in,), (out_out,) = out_blocks

    def low_rows(values):
        tail = values[count : count + TAIL]
        high = lax.reduce_precision(tail, 8, 7)
        rest = lax.reduce_precision(tail - high, 8, 7)
        kept = lax.reduce_precision(values[:count], 8, 7)
        return jnp.concatenate([kept, high, rest], axis=0).astype(bf16)

    def both_parts(values):
        values = values.astype(f32)
        return jnp.concatenate(
            [values[:count], values[count : count + TAIL] + values[count + TAIL :]], axis=0
        )

    block = low_rows(both_parts(jnp.sum(grads_w.astype(f32), axis=0)))
    for k in (1, 2):
        block = both_parts(block) + both_parts(along(block, k))
        block = low_rows(block) if k == 1 else block
    block = after(block, mixed)
    grads_n = block[count:].reshape(4, features)
    grad_qkv = block[: 3 * qkv_deep].reshape(3, qkv_deep, LANES)
    grad_attn_out = jnp.concatenate(
        [
            block[3 * qkv_deep + c * LANES : 3 * qkv_deep + (c + 1) * LANES]
            for c in range(qkv_deep // LANES)
        ],
        axis=1,
    )
    return (
        mixed,
        grad_input.reshape(rows, features),
        grads_n[0],
        grads_n[1],
        grads_n[2],
        grads_n[3],
        grad_qkv,
        grad_attn_out,
        out_in,
        out_out,
    )


def normalize(values, norm_gain, norm_shift):
    average = jnp.mean(values, axis=-1, keepdims=True)
    centered = values - average
    scaled = centered * lax.rsqrt(jnp.mean(centered * centered, axis=-1, keepdims=True) + norm_eps)
    return scaled * norm_gain + norm_shift


def route_slots(routes):
    flat_ids = routes.reshape(-1)
    onehot = (flat_ids[:, None] == jnp.arange(EXPERTS, dtype=jnp.int32)[None, :]).astype(jnp.int32)
    order_rank = jnp.sum(
        (jnp.cumsum(onehot, axis=0, dtype=jnp.int32) - 1) * onehot, axis=1, dtype=jnp.int32
    )
    slot_ids = order_rank * EXPERTS + flat_ids
    entry_count = flat_ids.shape[0]
    sources = (
        jnp.full((CAP * EXPERTS,), entry_count, jnp.int32)
        .at[slot_ids]
        .set(jnp.arange(entry_count, dtype=jnp.int32))
    )
    return (slot_ids.reshape(routes.shape), sources)


def narrow_rows(values):
    return lax.all_gather(values, "narrow", axis=0, tiled=True)


def narrow_sums(values):
    return lax.psum_scatter(
        values.astype(jnp.bfloat16), "narrow", scatter_dimension=0, tiled=True
    ).astype(jnp.float32)


def attention_forward(query, keys, values, head_count):
    row_count = query.shape[0]
    group_count = row_count // (IMG_STEP * SEQ)
    block_shape = (group_count, IMG_STEP, SEQ, head_count, HEAD_DIM)
    score_scale = HEAD_DIM ** (-0.5)

    def one_group(block):
        query_blk, key_blk, value_blk = block
        scores = (
            jnp.einsum("ishd,ithd->ihst", query_blk, key_blk, preferred_element_type=jnp.float32)
            * score_scale
        )
        row_top = jnp.max(scores, axis=-1, keepdims=True)
        weights = jnp.exp(scores - row_top)
        row_total = jnp.sum(weights, axis=-1, keepdims=True)
        probs = weights / row_total
        output = jnp.einsum(
            "ihst,ithd->ishd",
            probs.astype(jnp.bfloat16),
            value_blk,
            preferred_element_type=jnp.float32,
        )
        return (output.astype(jnp.bfloat16), (row_top + jnp.log(row_total))[..., 0])

    output, log_total = lax.map(
        one_group,
        (query.reshape(block_shape), keys.reshape(block_shape), values.reshape(block_shape)),
    )
    return (output.reshape(row_count, head_count * HEAD_DIM), log_total)


def attention_backward(query, keys, values, grad_att, log_total, head_count):
    row_count = query.shape[0]
    group_count = row_count // (IMG_STEP * SEQ)
    block_shape = (group_count, IMG_STEP, SEQ, head_count, HEAD_DIM)
    score_scale = HEAD_DIM ** (-0.5)

    def one_group(block):
        query_blk, key_blk, value_blk, grad_blk, total_blk = block
        scores = (
            jnp.einsum("ishd,ithd->ihst", query_blk, key_blk, preferred_element_type=jnp.float32)
            * score_scale
        )
        probs = jnp.exp(scores - total_blk[..., None])
        dprobs = jnp.einsum(
            "ishd,ithd->ihst", grad_blk, value_blk, preferred_element_type=jnp.float32
        )
        inner = jnp.sum(probs * dprobs, axis=-1, keepdims=True)
        grad_scores = (probs * (dprobs - inner)).astype(jnp.bfloat16)
        grad_query = (
            jnp.einsum("ihst,ithd->ishd", grad_scores, key_blk, preferred_element_type=jnp.float32)
            * score_scale
        )
        grad_key = (
            jnp.einsum(
                "ihst,ishd->ithd", grad_scores, query_blk, preferred_element_type=jnp.float32
            )
            * score_scale
        )
        grad_value = jnp.einsum(
            "ihst,ishd->ithd",
            probs.astype(jnp.bfloat16),
            grad_blk,
            preferred_element_type=jnp.float32,
        )
        return (
            grad_query.astype(jnp.bfloat16),
            grad_key.astype(jnp.bfloat16),
            grad_value.astype(jnp.bfloat16),
        )

    pieces = lax.map(
        one_group,
        (
            query.reshape(block_shape),
            keys.reshape(block_shape),
            values.reshape(block_shape),
            grad_att.reshape(block_shape),
            log_total,
        ),
    )
    return jnp.stack([piece.reshape(row_count, head_count * HEAD_DIM) for piece in pieces])


def on_device(
    tokens,
    grad_out,
    gates,
    routes,
    ln1_gain,
    ln1_bias,
    ln2_gain,
    ln2_bias,
    w_qkv,
    w_attn_out,
    w_expert_in,
    w_expert_out,
):
    stream = tokens.astype(jnp.float32)
    feature_count = stream.shape[1]
    normed = normalize(stream, ln1_gain, ln1_bias).astype(jnp.bfloat16)
    qkv_part, out_part = (
        lax.all_gather(w_qkv, "wide", axis=1, tiled=True),
        lax.all_gather(w_attn_out, "wide", axis=1, tiled=True),
    )
    qkv_full, out_full = (qkv_part, out_part)
    att_rows = narrow_rows(normed)
    projected = jnp.einsum(
        "rd,jdc->jrc", att_rows, qkv_full, preferred_element_type=jnp.float32
    ).astype(jnp.bfloat16)
    head_count = projected.shape[2] // HEAD_DIM
    attended, log_total = attention_forward(projected[0], projected[1], projected[2], head_count)
    branch = jnp.dot(attended, out_full, preferred_element_type=jnp.float32)
    att_sum = narrow_sums(branch)
    resid = stream + att_sum
    normed_two = normalize(resid, ln2_gain, ln2_bias).astype(jnp.bfloat16)
    slot_ids, sources = route_slots(routes)
    owner_rows = sources // TOP
    padded = jnp.concatenate([normed_two, jnp.zeros((1, feature_count), jnp.bfloat16)], axis=0)
    dispatched = padded[owner_rows].reshape(CAP, EXPERTS, feature_count)
    gathered_slots = narrow_rows(dispatched)
    in_full, down_full = (
        lax.all_gather(w_expert_in, "wide", axis=1, tiled=True),
        lax.all_gather(w_expert_out, "wide", axis=2, tiled=True),
    )
    down_form = "cef,efd->ced"
    back_form = "ced,efd->cef"
    grad_down_form = "cef,ced->efd"
    preact = jnp.einsum("ced,edf->cef", gathered_slots, in_full, preferred_element_type=jnp.float32)
    activated = jax.nn.gelu(preact).astype(jnp.bfloat16)
    partial_out = jnp.einsum(down_form, activated, down_full, preferred_element_type=jnp.float32)
    expert_flat = narrow_sums(partial_out).reshape(CAP * EXPERTS, feature_count)
    mixed = (resid + jnp.sum(gates[:, :, None] * expert_flat[slot_ids], axis=1)).astype(
        jnp.bfloat16
    )
    cotangent = grad_out.astype(jnp.float32)
    gate_pad = jnp.concatenate([gates.reshape(-1), jnp.zeros((1,), jnp.float32)], axis=0)
    cot_pad = jnp.concatenate([cotangent, jnp.zeros((1, feature_count), jnp.float32)], axis=0)
    grad_disp = (
        (gate_pad[sources][:, None] * cot_pad[owner_rows])
        .astype(jnp.bfloat16)
        .reshape(CAP, EXPERTS, feature_count)
    )
    grad_slots = narrow_rows(grad_disp)
    grad_activated = jnp.einsum(
        back_form, grad_slots, down_full, preferred_element_type=jnp.float32
    )
    gelu_back = jax.vjp(jax.nn.gelu, preact)[1]
    grad_preact = gelu_back(grad_activated)[0].astype(jnp.bfloat16)
    grad_down = jnp.einsum(
        grad_down_form, activated, grad_slots, preferred_element_type=jnp.float32
    )
    grad_in = jnp.einsum(
        "ced,cef->edf", gathered_slots, grad_preact, preferred_element_type=jnp.float32
    )
    grad_partial = jnp.einsum(
        "cef,edf->ced", grad_preact, in_full, preferred_element_type=jnp.float32
    )
    grad_slot_rows = narrow_sums(grad_partial).reshape(CAP * EXPERTS, feature_count)
    grad_normed_two = jnp.sum(grad_slot_rows[slot_ids], axis=1)
    norm_two_back = jax.vjp(normalize, resid, ln2_gain, ln2_bias)[1]
    grad_resid_norm, grad_gain_two, grad_bias_two = norm_two_back(grad_normed_two)
    grad_resid = cotangent + grad_resid_norm
    grad_branch = grad_resid.astype(jnp.bfloat16)
    grad_branch_rows = narrow_rows(grad_branch)
    grad_out_weight = jnp.dot(attended.T, grad_branch_rows, preferred_element_type=jnp.float32)
    grad_att = jnp.dot(grad_branch_rows, out_full.T, preferred_element_type=jnp.float32).astype(
        jnp.bfloat16
    )
    grad_proj = attention_backward(
        projected[0], projected[1], projected[2], grad_att, log_total, head_count
    )
    grad_qkv_weight = jnp.einsum(
        "rd,jrc->jdc", att_rows, grad_proj, preferred_element_type=jnp.float32
    )
    grad_normed_part = jnp.einsum(
        "jrc,jdc->rd", grad_proj, qkv_full, preferred_element_type=jnp.float32
    )
    grad_normed = narrow_sums(grad_normed_part)
    norm_one_back = jax.vjp(normalize, stream, ln1_gain, ln1_bias)[1]
    grad_stream_norm, grad_gain_one, grad_bias_one = norm_one_back(grad_normed)
    grad_input = grad_resid + grad_stream_norm
    grad_in_block, grad_down_block = (
        lax.psum_scatter(
            grad_in.astype(jnp.bfloat16), "wide", scatter_dimension=1, tiled=True
        ).astype(jnp.float32),
        lax.psum_scatter(
            grad_down.astype(jnp.bfloat16), "wide", scatter_dimension=2, tiled=True
        ).astype(jnp.float32),
    )
    grad_qkv_block, grad_out_block = (
        lax.psum_scatter(
            grad_qkv_weight.astype(jnp.bfloat16), "wide", scatter_dimension=1, tiled=True
        ).astype(jnp.float32),
        lax.psum_scatter(
            grad_out_weight.astype(jnp.bfloat16), "wide", scatter_dimension=1, tiled=True
        ).astype(jnp.float32),
    )
    block_grads = (
        lax.psum(grad_qkv_block.astype(jnp.bfloat16), "dp").astype(jnp.float32),
        lax.psum(grad_out_block.astype(jnp.bfloat16), "dp").astype(jnp.float32),
        lax.psum(grad_in_block.astype(jnp.bfloat16), "dp").astype(jnp.float32),
        lax.psum(grad_down_block.astype(jnp.bfloat16), "dp").astype(jnp.float32),
    )
    norm_totals = lax.psum(
        (grad_gain_one, grad_bias_one, grad_gain_two, grad_bias_two), ("dp", "wide", "narrow")
    )
    return (
        mixed,
        grad_input,
        norm_totals[0],
        norm_totals[1],
        norm_totals[2],
        norm_totals[3],
        block_grads[0],
        block_grads[1],
        block_grads[2],
        block_grads[3],
    )


def solution(mesh):
    planes, wide, narrow = (mesh.shape[name] for name in ("dp", "wide", "narrow"))
    plane = wide * narrow
    if planes == 4 and EXPERTS % (2 * plane) == 0 and plane & (plane - 1) == 0 and narrow % 2 == 0:
        sizes = (planes // 2, 2, wide, narrow)
        split = Mesh(mesh.devices.reshape(sizes), ("pair", "parity", "wide", "narrow"))
        return placed(
            functools.partial(owned_on_device, (planes // 2, wide, narrow)),
            split,
            ("pair", "parity", "wide", "narrow"),
        )
    return placed(on_device, mesh, ("dp", "wide", "narrow"))


def placed(function, mesh, row_axes):
    rows = P(row_axes, None)
    specs_in = (
        rows,
        rows,
        rows,
        rows,
        P(),
        P(),
        P(),
        P(),
        P(None, "wide", "narrow"),
        P("narrow", "wide"),
        P(None, "wide", "narrow"),
        P(None, "narrow", "wide"),
    )
    specs_out = (
        rows,
        rows,
        P(),
        P(),
        P(),
        P(),
        P(None, "wide", "narrow"),
        P("narrow", "wide"),
        P(None, "wide", "narrow"),
        P(None, "narrow", "wide"),
    )
    return jax.shard_map(
        function, mesh=mesh, in_specs=specs_in, out_specs=specs_out, check_vma=False
    )
```

```python
import functools
import math

import jax
import jax.numpy as jnp
from jax import lax
from jax.experimental import pallas as pl
from jax.experimental.pallas import tpu as pltpu
from jax.sharding import Mesh, PartitionSpec as P

HEAD_DIM = 64
EXPERTS = 32
TOP = 2
SEQ = 197
IMG_STEP = 4
CAP = 66

norm_eps = 1e-06

f32 = jnp.float32
bf16 = jnp.bfloat16


SLOTS = -(-CAP // 8) * 8
IMG_ROWS = -(-SEQ // 16) * 16
LANES = 128
TAIL = 16
VMEM_LIMIT = 56 * 1024 * 1024


def dot(a, b):
    return lax.dot_general(a, b, (((1,), (0,)), ((), ())), preferred_element_type=f32)


def dot_bt(a, b):
    return lax.dot_general(a, b, (((1,), (1,)), ((), ())), preferred_element_type=f32)


def dot_at(a, b):
    return lax.dot_general(a, b, (((0,), (0,)), ((), ())), preferred_element_type=f32)


def norm_parts(values):
    average = jnp.mean(values, axis=-1, keepdims=True)
    centered = values - average
    scale = lax.rsqrt(jnp.mean(centered * centered, axis=-1, keepdims=True) + norm_eps)
    return centered * scale, scale


def norm_back(hat, scale, gain, grad):
    t = grad * gain
    return scale * (
        t
        - jnp.mean(t, axis=-1, keepdims=True)
        - hat * jnp.mean(t * hat, axis=-1, keepdims=True)
    )


def full_spec(shape):
    zeros = (0,) * len(shape)
    return pl.BlockSpec(shape, lambda *_: zeros)


def image_spec(shape):
    rest = (0,) * (len(shape) - 1)
    return pl.BlockSpec((1,) + shape[1:], lambda i: (i,) + rest)


def back_rows(slot_ref, k, group, wide, offset):
    first = TOP + k if wide else k
    here = slot_ref[0, :, 2 * TOP + k : 2 * TOP + k + 1] == group
    return jnp.where(here, slot_ref[0, :, first : first + 1] + offset, -1)


def one_hot(mask):
    return mask.astype(f32).astype(bf16)


def route_kernel(plane, own_ref, routes_ref, routes_t_ref, back_ref, slot_t_ref):
    rows = routes_ref.shape[0]
    quarters = EXPERTS // plane
    groups = quarters // 2
    before = lax.broadcasted_iota(jnp.int32, (rows, rows), 0)
    after = lax.broadcasted_iota(jnp.int32, (rows, rows), 1)
    ids_t = lax.broadcasted_iota(jnp.int32, (EXPERTS, rows), 0)
    ids = lax.broadcasted_iota(jnp.int32, (rows, EXPERTS), 1)
    hot_t = [(ids_t == routes_t_ref[k : k + 1, :]).astype(f32) for k in range(TOP)]
    hot = [(ids == routes_ref[:, k : k + 1]).astype(f32) for k in range(TOP)]
    count_t = dot(sum(hot_t).astype(bf16), one_hot(before < after))
    count = dot(one_hot(after < before), sum(hot).astype(bf16))

    def place_of(ids):
        group, parity = ids // (2 * plane), ids // plane % 2
        return ids % plane, jnp.where(parity == own_ref[0], group, groups + group)

    for k in range(TOP):
        rank_t = jnp.sum(hot_t[k] * count_t, axis=0, keepdims=True).astype(jnp.int32)
        place, q = place_of(routes_t_ref[k : k + 1, :])
        slot_t_ref[k : k + 1, :] = (place * quarters + q) * SLOTS + rank_t
        rank = jnp.sum(hot[k] * count, axis=1, keepdims=True).astype(jnp.int32)
        chosen = routes_ref[:, k : k + 1]
        item = chosen % (2 * plane)
        back_ref[:, k : k + 1] = item * SLOTS + rank
        back_ref[:, TOP + k : TOP + k + 1] = item * 2 * SLOTS + rank
        back_ref[:, 2 * TOP + k : 2 * TOP + k + 1] = chosen // (2 * plane)


def route(own, routes, plane):
    rows = routes.shape[0]
    return pl.pallas_call(
        functools.partial(route_kernel, plane),
        in_specs=[pl.BlockSpec(memory_space=pltpu.SMEM)] + [pl.BlockSpec(memory_space=pltpu.VMEM)] * 2,
        out_shape=[
            jax.ShapeDtypeStruct((rows, 3 * TOP), jnp.int32),
            jax.ShapeDtypeStruct((TOP, rows), jnp.int32),
        ],
        compiler_params=pltpu.CompilerParams(vmem_limit_bytes=VMEM_LIMIT),
        cost_estimate=pl.CostEstimate(flops=60_000_000, bytes_accessed=100_000, transcendentals=0),
        name="route",
    )(own, routes, routes.T)


def grad_slots_kernel(plane, group, own_ref, sent_ref, gd_ref):
    rows = sent_ref.shape[1] - 2 * HEADER
    features = sent_ref.shape[2]
    header = jnp.concatenate(
        [sent_ref[0, i * HEADER : (i + 1) * HEADER, :].astype(f32) for i in range(2)], axis=1
    )[:, :rows]
    before = lax.broadcasted_iota(jnp.int32, (rows, rows), 0)
    after = lax.broadcasted_iota(jnp.int32, (rows, rows), 1)
    ids_t = lax.broadcasted_iota(jnp.int32, (EXPERTS, rows), 0)
    routes = [header[k : k + 1, :].astype(jnp.int32) for k in range(TOP)]
    gates = [
        (header[2 + k : 3 + k, :] + header[4 + k : 5 + k, :]) + header[6 + k : 7 + k, :]
        for k in range(TOP)
    ]
    hot = [(ids_t == routes[k]).astype(f32) for k in range(TOP)]
    count = dot(sum(hot).astype(bf16), one_hot(before < after))
    per = plane * SLOTS
    place = lax.broadcasted_iota(jnp.int32, (per, rows), 0)
    here = []
    for k in range(TOP):
        rank = jnp.sum(hot[k] * count, axis=0, keepdims=True).astype(jnp.int32)
        mine = routes[k] // plane == 2 * group + own_ref[0]
        here.append(place == jnp.where(mine, routes[k] % plane * SLOTS + rank, -1))
    gate = sum(jnp.where(here[k], gates[k], 0.0) for k in range(TOP))
    picked = dot(one_hot(here[0] | here[1]), sent_ref[0, 2 * HEADER :, :])
    weighed = jnp.sum(gate, axis=1, keepdims=True) * picked
    for p in range(plane):
        gd_ref[p, 0] = weighed[p * SLOTS : (p + 1) * SLOTS, :].astype(bf16)


HEADER = 8


def with_header(routes, gates, cot):
    rows, features = cot.shape
    high = lax.reduce_precision(gates, 8, 7)
    middle = lax.reduce_precision(gates - high, 8, 7)
    low = (gates - high) - middle
    lines = jnp.concatenate([v.T for v in (routes.astype(f32), high, middle, low)], axis=0)
    lines = jnp.pad(lines, ((0, 0), (0, 2 * features - rows))).astype(bf16)
    return jnp.concatenate([lines[:, :features], lines[:, features:], cot], axis=0)


def grad_slots(own, sent, plane, group):
    chunks, rows, features = sent.shape
    shape = (plane, chunks, SLOTS, features)
    return pl.pallas_call(
        functools.partial(grad_slots_kernel, plane, group),
        grid_spec=pltpu.PrefetchScalarGridSpec(
            num_scalar_prefetch=1,
            grid=(chunks,),
            in_specs=[pl.BlockSpec((1, rows, features), lambda i, own: (own[1] ^ i, 0, 0))],
            out_specs=pl.BlockSpec((plane, 1, SLOTS, features), lambda i, own: (0, i, 0, 0)),
        ),
        out_shape=jax.ShapeDtypeStruct(shape, bf16),
        compiler_params=pltpu.CompilerParams(vmem_limit_bytes=VMEM_LIMIT),
        cost_estimate=pl.CostEstimate(flops=8_000_000_000, bytes_accessed=10_000_000, transcendentals=0),
        name="grad_slots",
    )(own, sent)


def unpack_weights(wide, narrow, spot_ref, weights_refs, qkv_scratch, out_scratch):
    deep, across = qkv_scratch.shape[1] // wide, LANES
    for k in range(wide * narrow):
        block_ref = weights_refs[k % 2].at[k // 2]
        x = spot_ref[0] ^ (k // narrow)
        n = spot_ref[1] ^ (k % narrow)
        x_at = pl.multiple_of(x * deep, deep)
        n_at = pl.multiple_of(n * across, across)
        for j in range(3):
            qkv_scratch[j, pl.ds(x_at, deep), pl.ds(n_at, across)] = block_ref[
                j * deep : (j + 1) * deep, :
            ]
        for c in range(deep // LANES):
            first = 3 * deep + c * across
            out_scratch[
                pl.ds(n_at, across), pl.ds(pl.multiple_of(x_at + c * LANES, LANES), LANES)
            ] = block_ref[first : first + across, :]


def head_masks():
    lane = lax.broadcasted_iota(jnp.int32, (1, LANES), 1)
    per = LANES // HEAD_DIM
    return [(lane // HEAD_DIM) == h for h in range(per)]


def masked(value, mask):
    return jnp.where(mask, value, jnp.zeros_like(value))


def forward_kernel(
    wide,
    narrow,
    tile,
    spot_ref,
    tokens_ref,
    norms_ref,
    weights_a_ref,
    weights_b_ref,
    slot_t_ref,
    proj_ref,
    att_ref,
    resid_ref,
    x_ref,
    qkv_w,
    out_w,
    norm_scratch,
):
    step = pl.program_id(0)
    features = tokens_ref.shape[2]

    @pl.when(step == 0)
    def _():
        unpack_weights(wide, narrow, spot_ref, (weights_a_ref, weights_b_ref), qkv_w, out_w)
        norm_scratch[...] = jnp.zeros_like(norm_scratch)

    stream = tokens_ref[0].astype(f32)
    hat, _ = norm_parts(stream)
    normed = (hat * norms_ref[0:1, :] + norms_ref[1:2, :]).astype(bf16)
    proj = [dot(normed, qkv_w[j]).astype(bf16) for j in range(3)]
    for j in range(3):
        proj_ref[0, :, j * features : (j + 1) * features] = proj[j]
    masks = head_masks()
    scale = HEAD_DIM ** (-0.5)
    pieces = []
    for pair in range(features // LANES):
        cols = slice(pair * LANES, (pair + 1) * LANES)
        q, k, v = proj[0][:, cols], proj[1][:, cols], proj[2][:, cols]
        total = None
        for mask in masks:
            scores = dot_bt(masked(q, mask), k) * scale
            weights = jnp.exp(scores - jnp.max(scores, axis=-1, keepdims=True))
            probs = weights / jnp.sum(weights, axis=-1, keepdims=True)
            one = dot(probs.astype(bf16), masked(v, mask))
            total = one if total is None else total + one
        pieces.append(total.astype(bf16))
    attended = jnp.concatenate(pieces, axis=1)
    att_ref[0] = attended
    resid = stream + dot(attended, out_w[...])
    resid_ref[0] = resid
    hat_two, _ = norm_parts(resid)
    norm_scratch[step, : stream.shape[0], :] = (
        hat_two * norms_ref[2:3, :] + norms_ref[3:4, :]
    ).astype(bf16)

    @pl.when(step == pl.num_programs(0) - 1)
    def _():
        count = slot_t_ref.shape[1]
        rows = norm_scratch[...].reshape(count, features)
        for start in range(0, x_ref.shape[0], tile):
            place = lax.broadcasted_iota(jnp.int32, (tile, count), 0) + start
            here = (place == slot_t_ref[0:1, :]) | (place == slot_t_ref[1:2, :])
            x_ref[start : start + tile, :] = dot(one_hot(here), rows).astype(bf16)


def attention_and_slots(spot, tokens, norms, weights, slot_t, wide, narrow):
    images, rows, features = tokens.shape
    total = EXPERTS * SLOTS
    tile = 384 if total % 384 == 0 else SLOTS * wide * narrow
    per_image = [(images, rows, 3 * features), (images, rows, features), (images, rows, features)]
    return pl.pallas_call(
        functools.partial(forward_kernel, wide, narrow, tile),
        grid=(images,),
        in_specs=[
            pl.BlockSpec(memory_space=pltpu.SMEM),
            image_spec(tokens.shape),
            full_spec(norms.shape),
            full_spec(weights[0].shape),
            full_spec(weights[1].shape),
            full_spec(slot_t.shape),
        ],
        out_specs=[image_spec(s) for s in per_image] + [full_spec((total, features))],
        out_shape=[
            jax.ShapeDtypeStruct(per_image[0], bf16),
            jax.ShapeDtypeStruct(per_image[1], bf16),
            jax.ShapeDtypeStruct(per_image[2], f32),
            jax.ShapeDtypeStruct((total, features), bf16),
        ],
        scratch_shapes=[
            pltpu.VMEM((3, features, features), bf16),
            pltpu.VMEM((features, features), bf16),
            pltpu.VMEM((images, IMG_ROWS, features), bf16),
        ],
        compiler_params=pltpu.CompilerParams(vmem_limit_bytes=VMEM_LIMIT),
        cost_estimate=pl.CostEstimate(flops=6_000_000_000, bytes_accessed=9_000_000, transcendentals=2_000_000),
        name="attention_forward",
    )(spot, tokens, norms, *weights, slot_t)


def pack_kernel(first_ref, w_in_ref, w_out_ref, *out_refs):
    deep, hidden = w_in_ref.shape[1], w_in_ref.shape[2]
    base = deep * (hidden // LANES) if len(out_refs) == 1 else 0
    for c in range(hidden // LANES):
        out_refs[0][0, c * deep : (c + 1) * deep, :] = w_in_ref[0, :, c * LANES : (c + 1) * LANES]
    for c in range(deep // LANES):
        out_refs[-1][0, base + c * hidden : base + (c + 1) * hidden, :] = w_out_ref[
            0, :, c * LANES : (c + 1) * LANES
        ]


def pack(first, w_in, w_out, plane, arrays):
    deep, hidden = w_in.shape[1], w_in.shape[2]
    rows = 2 * deep * hidden // LANES // arrays
    at = lambda i, first: (first[0] + i, 0, 0)
    return pl.pallas_call(
        pack_kernel,
        grid_spec=pltpu.PrefetchScalarGridSpec(
            num_scalar_prefetch=1,
            grid=(plane,),
            in_specs=[pl.BlockSpec((1, deep, hidden), at), pl.BlockSpec((1, hidden, deep), at)],
            out_specs=[pl.BlockSpec((1, rows, LANES), lambda i, first: (i, 0, 0))] * arrays,
        ),
        out_shape=[jax.ShapeDtypeStruct((plane, rows, LANES), bf16)] * arrays,
        cost_estimate=pl.CostEstimate(flops=0, bytes_accessed=9_000_000, transcendentals=0),
        name="pack_weights",
    )(first, w_in, w_out)


GELU_A = math.sqrt(2.0 / math.pi)
GELU_B = 0.044715 * GELU_A


def gelu_pair(u):
    u2 = u * u
    p = GELU_B * u2 + GELU_A
    half = 0.5 * jnp.tanh(u * p) + 0.5
    slope = half + (u * (6.0 * p - 4.0 * GELU_A)) * (half - half * half)
    return u * half, slope


def identity(size):
    a = lax.broadcasted_iota(jnp.int32, (size, size), 0)
    b = lax.broadcasted_iota(jnp.int32, (size, size), 1)
    return (a == b).astype(f32).astype(bf16)


def expert_kernel(deep, hidden, parts, tile, where_ref, *refs):
    x_refs, (gd_ref, wi_ref, wo_ref, gi_ref, go_ref) = refs[:parts], refs[parts : parts + 5]
    gx_ref, y_ref = refs[parts + 5 : parts + 7]
    (x_s, gd_s, act, gp, wi_s, wo_s, y_acc, gx_acc, sem) = refs[parts + 7 :]
    step = pl.program_id(0)
    wide = wi_ref.shape[0]
    rows, features = x_s.shape
    own_rows = rows // 2
    chunk = own_rows // 2

    @pl.when(step == 0)
    def _():
        copies = [pltpu.make_async_copy(gd_ref, gd_s, sem.at[parts])]
        first = 0
        for i, x_ref in enumerate(x_refs):
            part = x_ref if len(x_ref.shape) == 2 else x_ref.at[where_ref[0]]
            count = part.shape[0]
            copies.append(pltpu.make_async_copy(part, x_s.at[pl.ds(first, count), :], sem.at[i]))
            first += count
        for copy in copies:
            copy.start()
        y_acc[...] = jnp.zeros_like(y_acc)
        gx_acc[...] = jnp.zeros_like(gx_acc)
        for copy in copies:
            copy.wait()


    for x in range(wide):
        for c in range(hidden // LANES):
            wi_s[x * deep : (x + 1) * deep, c * LANES : (c + 1) * LANES] = wi_ref[
                x, 0, c * deep : (c + 1) * deep, :
            ]
        for c in range(deep // LANES):
            first = x * deep + c * LANES
            wo_s[:, first : first + LANES] = wo_ref[x, 0, c * hidden : (c + 1) * hidden, :]

    for t in range(rows // tile):
        at = slice(t * tile, (t + 1) * tile)
        value, slope = gelu_pair(dot(x_s[at, :], wi_s[...]))
        value = value.astype(bf16)
        act[at, :] = value
        back = (dot_bt(gd_s[at, :], wo_s[...]) * slope).astype(bf16)
        gp[at, :] = back
        if t < own_rows // tile:
            y_acc[at, :] += dot(value, wo_s[...])
            gx_acc[at, :] += dot_bt(back, wi_s[...])
    gin = dot_at(x_s[...], gp[...]).astype(bf16)
    for x in range(wide):
        for c in range(hidden // LANES):
            gi_ref[x, 0, c * deep : (c + 1) * deep, :] = gin[
                x * deep : (x + 1) * deep, c * LANES : (c + 1) * LANES
            ]
    gout = dot_at(act[...], gd_s[...]).astype(bf16)
    for x in range(wide):
        for c in range(deep // LANES):
            first = x * deep + c * LANES
            go_ref[x, 0, c * hidden : (c + 1) * hidden, :] = gout[:, first : first + LANES]

    @pl.when(step == pl.num_programs(0) - 1)
    def _():
        for i in range(2):
            at = slice(i * chunk, (i + 1) * chunk)
            to = pl.ds(pl.multiple_of((where_ref[1] ^ i) * chunk, chunk), chunk)
            gx_ref[to, :] = gx_acc[at, :].astype(bf16)
            y_ref[to, :] = y_acc[at, :].astype(bf16)


def expert(where, xs, gd, weights, wide, narrow, deep, hidden):
    rows, features = gd.shape
    own_rows = rows // 2
    chunk = own_rows // 2
    packed = deep * hidden // LANES
    last = len(weights) - 1
    tile = 384 if own_rows % 384 == 0 else SLOTS * 2
    anywhere = pl.BlockSpec(memory_space=pl.ANY)
    whole = lambda shape: pl.BlockSpec(shape, lambda s: (0,) * len(shape))
    per_step = pl.BlockSpec((wide, 1, packed, LANES), lambda s: (0, s, 0, 0))
    blocks = (wide, narrow, packed, LANES)
    g_in, g_out, gx, y = pl.pallas_call(
        functools.partial(expert_kernel, deep, hidden, len(xs), tile),
        grid=(narrow,),
        in_specs=[pl.BlockSpec(memory_space=pltpu.SMEM)] + [anywhere] * (len(xs) + 1)
        + [per_step, pl.BlockSpec((wide, 1, packed, LANES), lambda s: (0, s, 1 - last, 0))],
        out_specs=[per_step] * 2 + [whole((own_rows, features))] * 2,
        scratch_shapes=[
            pltpu.VMEM((rows, features), bf16),
            pltpu.VMEM((rows, features), bf16),
            pltpu.VMEM((rows, hidden), bf16),
            pltpu.VMEM((rows, hidden), bf16),
            pltpu.VMEM((features, hidden), bf16),
            pltpu.VMEM((hidden, features), bf16),
            pltpu.VMEM((own_rows, features), f32),
            pltpu.VMEM((own_rows, features), f32),
            pltpu.SemaphoreType.DMA((len(xs) + 1,)),
        ],
        out_shape=[
            jax.ShapeDtypeStruct(blocks, bf16),
            jax.ShapeDtypeStruct(blocks, bf16),
        ]
        + [jax.ShapeDtypeStruct((own_rows, features), bf16)] * 2,
        compiler_params=pltpu.CompilerParams(vmem_limit_bytes=VMEM_LIMIT),
        cost_estimate=pl.CostEstimate(
            flops=2 * narrow * features * hidden * (4 * rows + 2 * own_rows),
            bytes_accessed=20_000_000,
            transcendentals=rows * hidden * narrow,
        ),
        name="expert",
    )(where, *xs, gd, *[w.reshape((wide, narrow) + w.shape[1:]) for w in (weights[0], weights[last])])
    return [g.reshape(wide * narrow, packed, LANES) for g in (g_in, g_out)], gx, y


def place_kernel(where_ref, g_ref, *refs):
    out_ref = refs[-1]
    rows = out_ref.shape[1]
    for i in range(out_ref.shape[0]):
        for c in range(out_ref.shape[2] // LANES):
            out_ref[i, :, c * LANES : (c + 1) * LANES] = g_ref[
                0, i, c * rows : (c + 1) * rows, :
            ].astype(f32)


def place(where, g, so_far, rows, columns):
    g = g.reshape((-1,) + g.shape[-3:])
    parts, plane, packed, _ = g.shape
    each = math.gcd(plane, 4)
    anywhere = pl.BlockSpec(memory_space=pl.ANY)
    part = (lambda where: where[0]) if parts > 1 else (lambda where: 0)
    return pl.pallas_call(
        place_kernel,
        grid_spec=pltpu.PrefetchScalarGridSpec(
            num_scalar_prefetch=1,
            grid=(plane // each,),
            in_specs=[pl.BlockSpec((1, each, packed, LANES), lambda i, where: (part(where), i, 0, 0))]
            + [anywhere] * len(so_far),
            out_specs=pl.BlockSpec(
                (each, rows, columns), lambda i, where: (where[1] // each + i, 0, 0)
            ),
        ),
        out_shape=jax.ShapeDtypeStruct((EXPERTS, rows, columns), f32),
        input_output_aliases={2 + i: i for i in range(len(so_far))},
        compiler_params=pltpu.CompilerParams(vmem_limit_bytes=VMEM_LIMIT),
        cost_estimate=pl.CostEstimate(flops=0, bytes_accessed=6_000_000, transcendentals=0),
        name="place_grads",
    )(where, g, *so_far)


def mixed_kernel(resid_ref, slot_ref, gates_ref, *rest):
    back_refs, mixed_ref = rest[:-1], rest[-1]
    total = resid_ref[0]
    rows = total.shape[0]
    for k in range(TOP):
        picked = None
        for g, back_ref in enumerate(back_refs):
            wide = g < len(back_refs) - 1
            place = lax.broadcasted_iota(jnp.int32, (rows, back_ref.shape[0]), 1)
            here = place == back_rows(slot_ref, k, g, wide, SLOTS if wide else 0)
            one = dot(one_hot(here), back_ref[...])
            picked = one if picked is None else picked + one
        total = total + gates_ref[0, :, k : k + 1] * picked
    mixed_ref[0] = total.astype(bf16)


def mix(resid, slots, gates, backs):
    return pl.pallas_call(
        mixed_kernel,
        grid=(resid.shape[0],),
        in_specs=[image_spec(resid.shape), image_spec(slots.shape), image_spec(gates.shape)]
        + [full_spec(y.shape) for y in backs],
        out_specs=image_spec(resid.shape),
        out_shape=jax.ShapeDtypeStruct(resid.shape, bf16),
        compiler_params=pltpu.CompilerParams(vmem_limit_bytes=VMEM_LIMIT),
        cost_estimate=pl.CostEstimate(flops=6_000_000_000, bytes_accessed=6_000_000, transcendentals=0),
        name="mix",
    )(resid, slots, gates, *backs)


def backward_kernel(wide, narrow, parts, *refs):
    (spot_ref, tokens_ref, cot_ref, norms_ref, weights_a_ref, weights_b_ref) = refs[:6]
    (slot_ref, proj_ref, att_ref, resid_ref) = refs[6:10]
    back_refs = refs[10 : 10 + parts]
    (grad_ref, grads_w_ref) = refs[10 + parts : 12 + parts]
    (qkv_w, out_w, normed_s, att_s, branch_s, proj_s, grads_n_ref) = refs[12 + parts :]
    step = pl.program_id(0)
    rows, features = tokens_ref.shape[1], tokens_ref.shape[2]

    @pl.when(step == 0)
    def _():
        unpack_weights(wide, narrow, spot_ref, (weights_a_ref, weights_b_ref), qkv_w, out_w)
        normed_s[...] = jnp.zeros_like(normed_s)
        att_s[...] = jnp.zeros_like(att_s)
        branch_s[...] = jnp.zeros_like(branch_s)
        proj_s[...] = jnp.zeros_like(proj_s)
        grads_n_ref[...] = jnp.zeros_like(grads_n_ref)

    grad_normed = None
    for g, back_ref in enumerate(back_refs):
        place = lax.broadcasted_iota(jnp.int32, (rows, back_ref.shape[0]), 1)
        own = [back_rows(slot_ref, k, g, g < parts - 1, 0) for k in range(TOP)]
        here = (place == own[0]) | (place == own[1])
        one = dot(one_hot(here), back_ref[...])
        grad_normed = one if grad_normed is None else grad_normed + one
    hat_two, scale_two = norm_parts(resid_ref[0])
    grads_n_ref[2:3, :] += jnp.sum(grad_normed * hat_two, axis=0, keepdims=True)
    grads_n_ref[3:4, :] += jnp.sum(grad_normed, axis=0, keepdims=True)
    grad_resid = cot_ref[0].astype(f32) + norm_back(
        hat_two, scale_two, norms_ref[2:3, :], grad_normed
    )
    branch = grad_resid.astype(bf16)
    branch_s[step, :rows, :] = branch
    att_s[step, :rows, :] = att_ref[0]
    grad_att = dot_bt(branch, out_w[...]).astype(bf16)

    masks = head_masks()
    scale = HEAD_DIM ** (-0.5)
    pairs = features // LANES
    pieces = [[None] * pairs for _ in range(3)]
    for pair in range(pairs):
        at = [j * features + pair * LANES for j in range(3)]
        q, k, v = [proj_ref[0, :, a : a + LANES] for a in at]
        ga = grad_att[:, pair * LANES : (pair + 1) * LANES]
        sums = [None] * 3
        for mask in masks:
            scores = dot_bt(masked(k, mask), q) * scale
            weights = jnp.exp(scores - jnp.max(scores, axis=0, keepdims=True))
            probs = weights / jnp.sum(weights, axis=0, keepdims=True)
            ga_h = masked(ga, mask)
            dprobs = dot_bt(v, ga_h)
            inner = jnp.sum(probs * dprobs, axis=0, keepdims=True)
            grad_scores = (probs * (dprobs - inner)).astype(bf16)
            parts_h = (
                dot_at(grad_scores, masked(k, mask)),
                dot(grad_scores, masked(q, mask)),
                dot(probs.astype(bf16), ga_h),
            )
            for j in range(3):
                sums[j] = parts_h[j] if sums[j] is None else sums[j] + parts_h[j]
        pieces[0][pair] = (sums[0] * scale).astype(bf16)
        pieces[1][pair] = (sums[1] * scale).astype(bf16)
        pieces[2][pair] = sums[2].astype(bf16)

    stream = tokens_ref[0].astype(f32)
    hat, scale_one = norm_parts(stream)
    normed_s[step, :rows, :] = (hat * norms_ref[0:1, :] + norms_ref[1:2, :]).astype(bf16)
    grad_first = None
    for j in range(3):
        grad_proj = jnp.concatenate(pieces[j], axis=1)
        proj_s[j, step, :rows, :] = grad_proj
        one = dot_bt(grad_proj, qkv_w[j])
        grad_first = one if grad_first is None else grad_first + one
    grads_n_ref[0:1, :] += jnp.sum(grad_first * hat, axis=0, keepdims=True)
    grads_n_ref[1:2, :] += jnp.sum(grad_first, axis=0, keepdims=True)
    grad_ref[0] = grad_resid + norm_back(hat, scale_one, norms_ref[0:1, :], grad_first)

    @pl.when(step == pl.num_programs(0) - 1)
    def _():
        count = normed_s.shape[0] * normed_s.shape[1]
        deep = features // wide
        flat = lambda value: value.reshape(count, features)
        normed_t = flat(normed_s[...])
        for j in range(3):
            grad = dot_at(normed_t, flat(proj_s[j])).astype(bf16)
            for x in range(wide):
                for n in range(narrow):
                    grads_w_ref[x * narrow + n, j * deep : (j + 1) * deep, :] = grad[
                        x * deep : (x + 1) * deep, n * LANES : (n + 1) * LANES
                    ]
        per = features // LANES
        tail = jnp.concatenate(
            [
                grads_n_ref[i : i + 1, c * LANES : (c + 1) * LANES]
                for i in range(4)
                for c in range(per)
            ],
            axis=0,
        )
        high = tail.astype(bf16)
        both = jnp.concatenate([high, (tail - high.astype(f32)).astype(bf16)], axis=0)
        for d in range(wide * narrow):
            grads_w_ref[d, grads_w_ref.shape[1] - 2 * TAIL :, :] = both
        grad = dot_at(flat(att_s[...]), flat(branch_s[...])).astype(bf16)
        for x in range(wide):
            for n in range(narrow):
                for c in range(deep // LANES):
                    first = 3 * deep + c * LANES
                    grads_w_ref[x * narrow + n, first : first + LANES, :] = grad[
                        n * LANES : (n + 1) * LANES,
                        x * deep + c * LANES : x * deep + (c + 1) * LANES,
                    ]


def attention_back(spot, tokens, cot, norms, weights, slots, proj, att, resid, backs, wide, narrow):
    images, rows, features = tokens.shape
    stash = (images, IMG_ROWS, features)
    small = (wide * narrow, weights[0].shape[1] + 2 * TAIL, LANES)
    return pl.pallas_call(
        functools.partial(backward_kernel, wide, narrow, len(backs)),
        grid=(images,),
        in_specs=[
            pl.BlockSpec(memory_space=pltpu.SMEM),
            image_spec(tokens.shape),
            image_spec(cot.shape),
            full_spec(norms.shape),
            full_spec(weights[0].shape),
            full_spec(weights[1].shape),
            image_spec(slots.shape),
            image_spec(proj.shape),
            image_spec(att.shape),
            image_spec(resid.shape),
        ]
        + [full_spec(back.shape) for back in backs],
        out_specs=[image_spec(tokens.shape), full_spec(small)],
        out_shape=[
            jax.ShapeDtypeStruct(tokens.shape, f32),
            jax.ShapeDtypeStruct(small, bf16),
        ],
        scratch_shapes=[
            pltpu.VMEM((3, features, features), bf16),
            pltpu.VMEM((features, features), bf16),
            pltpu.VMEM(stash, bf16),
            pltpu.VMEM(stash, bf16),
            pltpu.VMEM(stash, bf16),
            pltpu.VMEM((3,) + stash, bf16),
            pltpu.VMEM((4, features), f32),
        ],
        compiler_params=pltpu.CompilerParams(vmem_limit_bytes=VMEM_LIMIT),
        cost_estimate=pl.CostEstimate(flops=9_000_000_000, bytes_accessed=12_000_000, transcendentals=2_000_000),
        name="attention_backward",
    )(spot, tokens, cot, norms, *weights, slots, proj, att, resid, *backs)


def owned_on_device(
    sizes,
    tokens,
    grad_out,
    gates,
    routes,
    ln1_gain,
    ln1_bias,
    ln2_gain,
    ln2_bias,
    w_qkv,
    w_attn_out,
    w_expert_in,
    w_expert_out,
):
    pairs, wide, narrow = sizes
    planes, plane = 2 * pairs, wide * narrow
    groups = EXPERTS // (2 * plane)
    rows, features = tokens.shape
    images = rows // SEQ
    qkv_deep = w_qkv.shape[1]
    deep, hidden = w_expert_in.shape[1], w_expert_in.shape[2]
    pair_index, parity = lax.axis_index("pair"), lax.axis_index("parity")
    x_index, n_index = lax.axis_index("wide"), lax.axis_index("narrow")
    own = parity.astype(jnp.int32).reshape(1)
    own_and_plane = jnp.stack([parity, 2 * pair_index + parity]).astype(jnp.int32)
    far_and_own = jnp.stack([1 - pair_index, parity]).astype(jnp.int32)
    spot = jnp.stack([x_index, n_index, x_index * narrow + n_index]).astype(jnp.int32)

    def in_plane(values):
        return lax.all_to_all(values, ("wide", "narrow"), 0, 0, tiled=True)

    def in_pair(values):
        return lax.all_to_all(values, ("parity", "wide", "narrow"), 0, 0, tiled=True)

    def across(values, k):
        return lax.ppermute(values, ("wide", "narrow"), [(i, i ^ k) for i in range(plane)])

    def along(values, k):
        return lax.ppermute(values, ("pair", "parity"), [(i, i ^ k) for i in range(planes)])

    def with_near(values):
        return lax.all_gather(values, "parity", axis=0)

    def after(values, first):
        return lax.optimization_barrier((values, first))[0]

    small = jnp.concatenate(
        [w_qkv.reshape(3 * qkv_deep, LANES)]
        + [w_attn_out[:, c * LANES : (c + 1) * LANES] for c in range(qkv_deep // LANES)],
        axis=0,
    )
    same_core = jnp.stack([small] + [across(small, k) for k in range(2, plane, 2)])
    weights = (same_core, across(same_core, 1))

    sent_all = lax.all_gather(with_header(routes, gates, grad_out), ("pair", "parity"), axis=0)

    back_slots, slot_t = route(own, routes, plane)
    packed = [
        pack(
            (g * 2 * plane + parity * plane).astype(jnp.int32).reshape(1),
            w_expert_in,
            w_expert_out,
            plane,
            1 if g else 2,
        )
        for g in range(groups)
    ]

    norms = jnp.stack([ln1_gain, ln1_bias, ln2_gain, ln2_bias])
    per_image = lambda values: values.reshape((images, SEQ) + values.shape[1:])
    slot_wide = jnp.pad(
        slot_t.reshape(TOP, images, SEQ), ((0, 0), (0, 0), (0, IMG_ROWS - SEQ)), constant_values=-1
    ).reshape(TOP, images * IMG_ROWS)
    tokens3, cot3, slots3, gates3 = map(per_image, (tokens, grad_out, back_slots, gates))
    proj, att, resid, x = attention_and_slots(
        spot, tokens3, norms, weights, slot_wide, wide, narrow
    )

    def quarter(moved, q):
        return moved[:, q * SLOTS : (q + 1) * SLOTS].reshape(plane * SLOTS, features)

    def by_plane(values):
        return jnp.moveaxis(values.reshape(plane, planes, SLOTS, features), 1, 0).reshape(
            planes * plane * SLOTS, features
        )

    gd_sent = [grad_slots(own_and_plane, sent_all, plane, g) for g in range(groups)]
    first_in = in_plane(packed[0][0])
    moved = in_plane(after(x, first_in).reshape(plane, -1, features))
    mine, other = quarter(moved, 0), quarter(moved, groups)
    nearest, far_mine = along(other, 1), along(mine, 2)
    first_out = in_plane(after(packed[0][1], (moved, gd_sent[0])))
    xs = [[mine, nearest, far_mine, along(other, 3)]]
    gd_parts = [v.reshape(plane, planes * SLOTS, features) for v in gd_sent]
    gds = [by_plane(in_plane(after(gd_parts[0], (first_out, nearest, far_mine, packed[1:]))))]
    nears = [
        jnp.concatenate([quarter(moved, g), along(quarter(moved, groups + g), 1)], axis=0)
        for g in range(1, groups)
    ]
    xs += [
        [near, lax.all_gather(after(near, xs[0]), "pair", axis=0)] for near in nears
    ]

    def to_tokens(parts, before):
        sent = jnp.concatenate([v.reshape(2 * plane, SLOTS, features) for v in parts], axis=1)
        return in_pair(after(sent, before)).reshape(-1, features)

    shapes = ((deep, hidden), (hidden, deep))
    out_blocks = [(), ()]

    def put(i, g, own_part, before):
        which = parity if own_part else 1 - parity
        where = jnp.stack([which, g * 2 * plane + which * plane]).astype(jnp.int32)
        part = after((grads if own_part else swaps)[g][i], before)
        out_blocks[i] = (place(where, part, out_blocks[i], *shapes[i]),)

    def after_blocks(values):
        values, out_blocks[:] = lax.optimization_barrier((values, out_blocks))
        return values

    held = (first_in, first_out)
    before = (gds[0], first_out, xs[0], nears)
    grads, swaps, gx_back, y_back = [], [], [], []
    last = groups - 1
    for g in range(groups):
        grad, gx, y = expert(far_and_own, xs[g], gds[g], held, wide, narrow, deep, hidden)
        grads.append([])
        swaps.append([])
        if g < last:
            held = tuple(in_plane(after(v, before)) for v in packed[g + 1])
            grads[g].append(in_plane(after(grad[0], held)))
            swaps[g].append(with_near(grads[g][0]))
            gds.append(by_plane(in_plane(after(gd_parts[g + 1], (grads[g][0], xs[g + 1])))))
            put(0, g, True, ())
            grads[g].append(in_plane(after_blocks(after(grad[1], gds[g + 1]))))
            swaps[g].append(with_near(grads[g][1]))
            gds[g + 1] = after(gds[g + 1], grads[g][1])
            put(1, g, True, ())
            before = to_tokens(after_blocks([gx, y]), grads[g][1])
            y_back.append(before)
            gx_back.append(before)
        else:
            grads[g].append(in_plane(after(grad[0], before)))
            swaps[g].append(with_near(grads[g][0]))
            if g:
                put(0, g - 1, False, ())
            before = to_tokens([after_blocks(gx)], grads[g][-1])
            gx_back.append(before)
            grads[g].append(in_plane(after(grad[1], before)))
            before = grads[g][1]
            last_y = y

    grad_input, grads_w = attention_back(
        spot, tokens3, cot3, norms, weights, slots3, proj, att, resid, gx_back, wide, narrow
    )
    count = grads_w.shape[1] - 2 * TAIL
    swaps[last].append(with_near(grads[last][1]))
    grads_w = in_plane(after(grads_w, before))
    y_back.append(to_tokens([last_y], grads_w))
    for g in range(last):
        put(1, g, False, ())
    put(0, last, True, ())
    put(1, last, True, ())
    put(0, last, False, ())
    mixed = mix(after_blocks(resid), slots3, gates3, y_back).reshape(rows, features)
    put(1, last, False, mixed)
    (out_in,), (out_out,) = out_blocks

    def low_rows(values):
        tail = values[count : count + TAIL]
        high = lax.reduce_precision(tail, 8, 7)
        rest = lax.reduce_precision(tail - high, 8, 7)
        kept = lax.reduce_precision(values[:count], 8, 7)
        return jnp.concatenate([kept, high, rest], axis=0).astype(bf16)

    def both_parts(values):
        values = values.astype(f32)
        return jnp.concatenate(
            [values[:count], values[count : count + TAIL] + values[count + TAIL :]], axis=0
        )

    block = low_rows(both_parts(jnp.sum(grads_w.astype(f32), axis=0)))
    for k in (1, 2):
        block = both_parts(block) + both_parts(along(block, k))
        block = low_rows(block) if k == 1 else block
    block = after(block, mixed)
    grads_n = block[count:].reshape(4, features)
    grad_qkv = block[: 3 * qkv_deep].reshape(3, qkv_deep, LANES)
    grad_attn_out = jnp.concatenate(
        [
            block[3 * qkv_deep + c * LANES : 3 * qkv_deep + (c + 1) * LANES]
            for c in range(qkv_deep // LANES)
        ],
        axis=1,
    )
    return (
        mixed,
        grad_input.reshape(rows, features),
        grads_n[0],
        grads_n[1],
        grads_n[2],
        grads_n[3],
        grad_qkv,
        grad_attn_out,
        out_in,
        out_out,
    )


def normalize(values, norm_gain, norm_shift):
    average = jnp.mean(values, axis=-1, keepdims=True)
    centered = values - average
    scaled = centered * lax.rsqrt(jnp.mean(centered * centered, axis=-1, keepdims=True) + norm_eps)
    return scaled * norm_gain + norm_shift


def route_slots(routes):
    flat_ids = routes.reshape(-1)
    onehot = (flat_ids[:, None] == jnp.arange(EXPERTS, dtype=jnp.int32)[None, :]).astype(jnp.int32)
    order_rank = jnp.sum(
        (jnp.cumsum(onehot, axis=0, dtype=jnp.int32) - 1) * onehot, axis=1, dtype=jnp.int32
    )
    slot_ids = order_rank * EXPERTS + flat_ids
    entry_count = flat_ids.shape[0]
    sources = (
        jnp.full((CAP * EXPERTS,), entry_count, jnp.int32)
        .at[slot_ids]
        .set(jnp.arange(entry_count, dtype=jnp.int32))
    )
    return (slot_ids.reshape(routes.shape), sources)


def narrow_rows(values):
    return lax.all_gather(values, "narrow", axis=0, tiled=True)


def narrow_sums(values):
    return lax.psum_scatter(
        values.astype(jnp.bfloat16), "narrow", scatter_dimension=0, tiled=True
    ).astype(jnp.float32)


def attention_forward(query, keys, values, head_count):
    row_count = query.shape[0]
    group_count = row_count // (IMG_STEP * SEQ)
    block_shape = (group_count, IMG_STEP, SEQ, head_count, HEAD_DIM)
    score_scale = HEAD_DIM ** (-0.5)

    def one_group(block):
        query_blk, key_blk, value_blk = block
        scores = (
            jnp.einsum("ishd,ithd->ihst", query_blk, key_blk, preferred_element_type=jnp.float32)
            * score_scale
        )
        row_top = jnp.max(scores, axis=-1, keepdims=True)
        weights = jnp.exp(scores - row_top)
        row_total = jnp.sum(weights, axis=-1, keepdims=True)
        probs = weights / row_total
        output = jnp.einsum(
            "ihst,ithd->ishd",
            probs.astype(jnp.bfloat16),
            value_blk,
            preferred_element_type=jnp.float32,
        )
        return (output.astype(jnp.bfloat16), (row_top + jnp.log(row_total))[..., 0])

    output, log_total = lax.map(
        one_group,
        (query.reshape(block_shape), keys.reshape(block_shape), values.reshape(block_shape)),
    )
    return (output.reshape(row_count, head_count * HEAD_DIM), log_total)


def attention_backward(query, keys, values, grad_att, log_total, head_count):
    row_count = query.shape[0]
    group_count = row_count // (IMG_STEP * SEQ)
    block_shape = (group_count, IMG_STEP, SEQ, head_count, HEAD_DIM)
    score_scale = HEAD_DIM ** (-0.5)

    def one_group(block):
        query_blk, key_blk, value_blk, grad_blk, total_blk = block
        scores = (
            jnp.einsum("ishd,ithd->ihst", query_blk, key_blk, preferred_element_type=jnp.float32)
            * score_scale
        )
        probs = jnp.exp(scores - total_blk[..., None])
        dprobs = jnp.einsum(
            "ishd,ithd->ihst", grad_blk, value_blk, preferred_element_type=jnp.float32
        )
        inner = jnp.sum(probs * dprobs, axis=-1, keepdims=True)
        grad_scores = (probs * (dprobs - inner)).astype(jnp.bfloat16)
        grad_query = (
            jnp.einsum("ihst,ithd->ishd", grad_scores, key_blk, preferred_element_type=jnp.float32)
            * score_scale
        )
        grad_key = (
            jnp.einsum(
                "ihst,ishd->ithd", grad_scores, query_blk, preferred_element_type=jnp.float32
            )
            * score_scale
        )
        grad_value = jnp.einsum(
            "ihst,ishd->ithd",
            probs.astype(jnp.bfloat16),
            grad_blk,
            preferred_element_type=jnp.float32,
        )
        return (
            grad_query.astype(jnp.bfloat16),
            grad_key.astype(jnp.bfloat16),
            grad_value.astype(jnp.bfloat16),
        )

    pieces = lax.map(
        one_group,
        (
            query.reshape(block_shape),
            keys.reshape(block_shape),
            values.reshape(block_shape),
            grad_att.reshape(block_shape),
            log_total,
        ),
    )
    return jnp.stack([piece.reshape(row_count, head_count * HEAD_DIM) for piece in pieces])


def on_device(
    tokens,
    grad_out,
    gates,
    routes,
    ln1_gain,
    ln1_bias,
    ln2_gain,
    ln2_bias,
    w_qkv,
    w_attn_out,
    w_expert_in,
    w_expert_out,
):
    stream = tokens.astype(jnp.float32)
    feature_count = stream.shape[1]
    normed = normalize(stream, ln1_gain, ln1_bias).astype(jnp.bfloat16)
    qkv_part, out_part = (
        lax.all_gather(w_qkv, "wide", axis=1, tiled=True),
        lax.all_gather(w_attn_out, "wide", axis=1, tiled=True),
    )
    qkv_full, out_full = (qkv_part, out_part)
    att_rows = narrow_rows(normed)
    projected = jnp.einsum(
        "rd,jdc->jrc", att_rows, qkv_full, preferred_element_type=jnp.float32
    ).astype(jnp.bfloat16)
    head_count = projected.shape[2] // HEAD_DIM
    attended, log_total = attention_forward(projected[0], projected[1], projected[2], head_count)
    branch = jnp.dot(attended, out_full, preferred_element_type=jnp.float32)
    att_sum = narrow_sums(branch)
    resid = stream + att_sum
    normed_two = normalize(resid, ln2_gain, ln2_bias).astype(jnp.bfloat16)
    slot_ids, sources = route_slots(routes)
    owner_rows = sources // TOP
    padded = jnp.concatenate([normed_two, jnp.zeros((1, feature_count), jnp.bfloat16)], axis=0)
    dispatched = padded[owner_rows].reshape(CAP, EXPERTS, feature_count)
    gathered_slots = narrow_rows(dispatched)
    in_full, down_full = (
        lax.all_gather(w_expert_in, "wide", axis=1, tiled=True),
        lax.all_gather(w_expert_out, "wide", axis=2, tiled=True),
    )
    down_form = "cef,efd->ced"
    back_form = "ced,efd->cef"
    grad_down_form = "cef,ced->efd"
    preact = jnp.einsum("ced,edf->cef", gathered_slots, in_full, preferred_element_type=jnp.float32)
    activated = jax.nn.gelu(preact).astype(jnp.bfloat16)
    partial_out = jnp.einsum(down_form, activated, down_full, preferred_element_type=jnp.float32)
    expert_flat = narrow_sums(partial_out).reshape(CAP * EXPERTS, feature_count)
    mixed = (resid + jnp.sum(gates[:, :, None] * expert_flat[slot_ids], axis=1)).astype(
        jnp.bfloat16
    )
    cotangent = grad_out.astype(jnp.float32)
    gate_pad = jnp.concatenate([gates.reshape(-1), jnp.zeros((1,), jnp.float32)], axis=0)
    cot_pad = jnp.concatenate([cotangent, jnp.zeros((1, feature_count), jnp.float32)], axis=0)
    grad_disp = (
        (gate_pad[sources][:, None] * cot_pad[owner_rows])
        .astype(jnp.bfloat16)
        .reshape(CAP, EXPERTS, feature_count)
    )
    grad_slots = narrow_rows(grad_disp)
    grad_activated = jnp.einsum(
        back_form, grad_slots, down_full, preferred_element_type=jnp.float32
    )
    gelu_back = jax.vjp(jax.nn.gelu, preact)[1]
    grad_preact = gelu_back(grad_activated)[0].astype(jnp.bfloat16)
    grad_down = jnp.einsum(
        grad_down_form, activated, grad_slots, preferred_element_type=jnp.float32
    )
    grad_in = jnp.einsum(
        "ced,cef->edf", gathered_slots, grad_preact, preferred_element_type=jnp.float32
    )
    grad_partial = jnp.einsum(
        "cef,edf->ced", grad_preact, in_full, preferred_element_type=jnp.float32
    )
    grad_slot_rows = narrow_sums(grad_partial).reshape(CAP * EXPERTS, feature_count)
    grad_normed_two = jnp.sum(grad_slot_rows[slot_ids], axis=1)
    norm_two_back = jax.vjp(normalize, resid, ln2_gain, ln2_bias)[1]
    grad_resid_norm, grad_gain_two, grad_bias_two = norm_two_back(grad_normed_two)
    grad_resid = cotangent + grad_resid_norm
    grad_branch = grad_resid.astype(jnp.bfloat16)
    grad_branch_rows = narrow_rows(grad_branch)
    grad_out_weight = jnp.dot(attended.T, grad_branch_rows, preferred_element_type=jnp.float32)
    grad_att = jnp.dot(grad_branch_rows, out_full.T, preferred_element_type=jnp.float32).astype(
        jnp.bfloat16
    )
    grad_proj = attention_backward(
        projected[0], projected[1], projected[2], grad_att, log_total, head_count
    )
    grad_qkv_weight = jnp.einsum(
        "rd,jrc->jdc", att_rows, grad_proj, preferred_element_type=jnp.float32
    )
    grad_normed_part = jnp.einsum(
        "jrc,jdc->rd", grad_proj, qkv_full, preferred_element_type=jnp.float32
    )
    grad_normed = narrow_sums(grad_normed_part)
    norm_one_back = jax.vjp(normalize, stream, ln1_gain, ln1_bias)[1]
    grad_stream_norm, grad_gain_one, grad_bias_one = norm_one_back(grad_normed)
    grad_input = grad_resid + grad_stream_norm
    grad_in_block, grad_down_block = (
        lax.psum_scatter(
            grad_in.astype(jnp.bfloat16), "wide", scatter_dimension=1, tiled=True
        ).astype(jnp.float32),
        lax.psum_scatter(
            grad_down.astype(jnp.bfloat16), "wide", scatter_dimension=2, tiled=True
        ).astype(jnp.float32),
    )
    grad_qkv_block, grad_out_block = (
        lax.psum_scatter(
            grad_qkv_weight.astype(jnp.bfloat16), "wide", scatter_dimension=1, tiled=True
        ).astype(jnp.float32),
        lax.psum_scatter(
            grad_out_weight.astype(jnp.bfloat16), "wide", scatter_dimension=1, tiled=True
        ).astype(jnp.float32),
    )
    block_grads = (
        lax.psum(grad_qkv_block.astype(jnp.bfloat16), "dp").astype(jnp.float32),
        lax.psum(grad_out_block.astype(jnp.bfloat16), "dp").astype(jnp.float32),
        lax.psum(grad_in_block.astype(jnp.bfloat16), "dp").astype(jnp.float32),
        lax.psum(grad_down_block.astype(jnp.bfloat16), "dp").astype(jnp.float32),
    )
    norm_totals = lax.psum(
        (grad_gain_one, grad_bias_one, grad_gain_two, grad_bias_two), ("dp", "wide", "narrow")
    )
    return (
        mixed,
        grad_input,
        norm_totals[0],
        norm_totals[1],
        norm_totals[2],
        norm_totals[3],
        block_grads[0],
        block_grads[1],
        block_grads[2],
        block_grads[3],
    )


def solution(mesh):
    planes, wide, narrow = (mesh.shape[name] for name in ("dp", "wide", "narrow"))
    plane = wide * narrow
    if planes == 4 and EXPERTS % (2 * plane) == 0 and plane & (plane - 1) == 0 and narrow % 2 == 0:
        sizes = (planes // 2, 2, wide, narrow)
        split = Mesh(mesh.devices.reshape(sizes), ("pair", "parity", "wide", "narrow"))
        return placed(
            functools.partial(owned_on_device, (planes // 2, wide, narrow)),
            split,
            ("pair", "parity", "wide", "narrow"),
        )
    return placed(on_device, mesh, ("dp", "wide", "narrow"))


def placed(function, mesh, row_axes):
    rows = P(row_axes, None)
    specs_in = (
        rows,
        rows,
        rows,
        rows,
        P(),
        P(),
        P(),
        P(),
        P(None, "wide", "narrow"),
        P("narrow", "wide"),
        P(None, "wide", "narrow"),
        P(None, "narrow", "wide"),
    )
    specs_out = (
        rows,
        rows,
        P(),
        P(),
        P(),
        P(),
        P(None, "wide", "narrow"),
        P("narrow", "wide"),
        P(None, "wide", "narrow"),
        P(None, "narrow", "wide"),
    )
    return jax.shard_map(
        function, mesh=mesh, in_specs=specs_in, out_specs=specs_out, check_vma=False
    )
```
